32 devices in a mesh: parts: 2 (over x), seq: 16 (over z, y, core).
Axes of the slice: x: 2, y: 2, z: 4, core: 2. Of those that a mesh axis runs over, the one named last changes fastest.
Arguments:
- latent: float32 [3072, 64], P(('parts', 'seq')), parts along dimension 0, may hold values from -6 to 6
- main_hidden: bfloat16 [3072, 5120], P(('parts', 'seq')), parts along dimension 0, may hold values from -10 to 10
- main_query: bfloat16 [3072, 5120], P(('parts', 'seq')), parts along dimension 0, may hold values from -40 to 40
- text_key: bfloat16 [1024, 5120], P(('parts', 'seq')), parts along dimension 0, may hold values from -40 to 40
- text_value: bfloat16 [1024, 5120], P(('parts', 'seq')), parts along dimension 0, may hold values from -12 to 12
- text_len: int32 [2], P('parts'), parts along dimension 0, may hold values from 128 to 512
- guide_hidden: bfloat16 [3072, 1536], P(('parts', 'seq')), parts along dimension 0, may hold values from -10 to 10
- guide_query: bfloat16 [3072, 768], P(('parts', 'seq')), parts along dimension 0, may hold values from -40 to 40
- guide_key: bfloat16 [3072, 768], P(('parts', 'seq')), parts along dimension 0, may hold values from -40 to 40
- guide_value: bfloat16 [3072, 768], P(('parts', 'seq')), parts along dimension 0, may hold values from -48 to 48
- guide_out: bfloat16 [768, 1536], replicated, may hold values from -0.21875 to 0.21875
- main_head: bfloat16 [5120, 64], replicated, may hold values from -0.078125 to 0.078125
- guide_head: bfloat16 [1536, 64], replicated, may hold values from -0.15625 to 0.15625
- main_modulation: float32 [4, 5120], P('parts'), parts along dimension 0, may hold values from -1.5 to 1.5
- guide_modulation: float32 [4, 1536], P('parts'), parts along dimension 0, may hold values from -1.5 to 1.5
- guidance_scale: float32 [2], P('parts'), parts along dimension 0, may hold values from 1.5 to 3.5
- sigma_table: float32 [51], replicated, may hold values from 0 to 1, as said below
- step_index: int32 [2], P('parts'), parts along dimension 0, may hold values from 0 to 49
Outputs:
- velocity: float32 [3072, 64], P(('parts', 'seq')), parts along dimension 0
- next_latent: float32 [3072, 64], P(('parts', 'seq')), parts along dimension 0
The draws below stay inside these ranges and needn't reach their ends.
There are 2 independent parts, one for each index of `parts`. The reference program is written for one: setup_inputs(seed, part) draws one part's arguments, and reference() takes and returns one part's arrays. A program takes and returns all parts, laid end to end along the dimension named above; an argument that names none is the same for every part. Nothing has to cross between parts.
Inputs may be any that keep to these rules, and one draw needn't show every extreme that they name: `sigma_table`: falls from 1 at index 0 to a small positive value at index 50.
All inputs are finite; a program needn't handle non-finite values.
Results may differ from the reference program's by a relative error of at most 0.0055.
Values may be sent and summed in bfloat16 or wider, within the bound.
A program may use at most 192 MiB of HBM per device.

```python
import math
import jax
import jax.numpy as jnp
from jax import lax

HDIM = 128
HM = 40
D = 5120
GH = 6
GA = 768
G = 1536
C = 64
TEXT = 512
STEPS = 50
TOKENS = 1536


def query_and_keys(key, query_rows, key_rows, heads):
    keys = jnp.clip(jax.random.normal(jax.random.fold_in(key, 11), (key_rows, heads * HDIM), jnp.float32), -5.0, 5.0)
    queries = 1.5 * jnp.clip(jax.random.normal(jax.random.fold_in(key, 12), (query_rows, heads * HDIM), jnp.float32), -5.0, 5.0)
    return (queries, keys)


def draw_main_query(key, part):
    return query_and_keys(jax.random.fold_in(key, 101), TOKENS, TEXT, HM)[0].astype(jnp.bfloat16)


def draw_text_key(key, part):
    return query_and_keys(jax.random.fold_in(key, 101), TOKENS, TEXT, HM)[1].astype(jnp.bfloat16)


def draw_guide_query(key, part):
    return query_and_keys(jax.random.fold_in(key, 202), TOKENS, TOKENS, GH)[0].astype(jnp.bfloat16)


def draw_guide_key(key, part):
    return query_and_keys(jax.random.fold_in(key, 202), TOKENS, TOKENS, GH)[1].astype(jnp.bfloat16)


def stream_draw(key, width, plain_scale):
    base = jnp.clip(jax.random.normal(jax.random.fold_in(key, 1), (TOKENS, width), jnp.float32), -6.0, 6.0)
    return plain_scale * base


def draw_main_hidden(key, part):
    return stream_draw(jax.random.fold_in(key, 303), D, 0.5).astype(jnp.bfloat16)


def draw_guide_hidden(key, part):
    return stream_draw(jax.random.fold_in(key, 404), G, 0.3).astype(jnp.bfloat16)


def draw_sigma_table(key, part):
    increments = jnp.exp(jax.random.uniform(jax.random.fold_in(key, 505), (STEPS,), jnp.float32, math.log(0.2), math.log(6.0)))
    climbed = jnp.concatenate([jnp.zeros((1,), jnp.float32), jnp.cumsum(increments)])
    return 1.0 - 0.97 * climbed / climbed[-1]


def block_levels(stream_key, shape, pieces, least, high):
    level = 1.0
    for dim, parts in pieces:
        heights = jax.random.uniform(jax.random.fold_in(jax.random.fold_in(stream_key, 6), dim), (parts,), jnp.float32, least / len(pieces), high / len(pieces))
        level = level * jnp.repeat(jnp.exp(heights), shape[dim] // parts).reshape((-1,) + (1,) * (len(shape) - 1 - dim))
    return level


def centred(stream_key, dims, scale, most, cuts=(), kind=jnp.bfloat16):
    gain = block_levels(stream_key, dims, cuts, -0.22, 0.18) if cuts else 1.0
    values = jax.random.normal(stream_key, dims, jnp.float32) * scale * gain
    return jnp.minimum(jnp.maximum(values, -most), most).astype(kind)


def setup_inputs(seed: int = 0, part: int = 0) -> dict:
    arg_keys = jax.random.split(jax.random.key(seed), 19)
    part_splits = jax.random.split(jax.random.fold_in(arg_keys[18], part), 19)
    latent = centred(part_splits[0], (TOKENS, C), 1.0, 6.0, ((0, 16),), jnp.float32)
    main_hidden = draw_main_hidden(jax.random.fold_in(jax.random.fold_in(arg_keys[18], part), 71), part)
    main_query = draw_main_query(jax.random.fold_in(jax.random.fold_in(arg_keys[18], part), 71), part)
    text_key = draw_text_key(jax.random.fold_in(jax.random.fold_in(arg_keys[18], part), 71), part)
    text_value = centred(part_splits[4], (TEXT, D), 2.0, 12.0, ((0, 16),))
    text_len = jax.random.randint(part_splits[5], (1,), TEXT // 4, TEXT + 1).astype(jnp.int32)
    guide_hidden = draw_guide_hidden(jax.random.fold_in(jax.random.fold_in(arg_keys[18], part), 71), part)
    guide_query = draw_guide_query(jax.random.fold_in(jax.random.fold_in(arg_keys[18], part), 71), part)
    guide_key = draw_guide_key(jax.random.fold_in(jax.random.fold_in(arg_keys[18], part), 71), part)
    guide_value = centred(part_splits[9], (TOKENS, GA), 8.0, 48.0, ((0, 16),))
    guide_out = centred(arg_keys[10], (GA, G), GA ** -0.5, 0.21875)
    main_head = centred(arg_keys[11], (D, C), D ** -0.5, 0.078125)
    guide_head = centred(arg_keys[12], (G, C), G ** -0.5, 0.15625)
    main_modulation = centred(part_splits[13], (2, D), 0.3, 1.5, (), jnp.float32)
    guide_modulation = centred(part_splits[14], (2, G), 0.3, 1.5, (), jnp.float32)
    guidance_scale = jnp.clip(jax.random.uniform(part_splits[15], (1,), jnp.float32, 1.5, 3.5), 1.5, 3.5)
    sigma_table = draw_sigma_table(jax.random.fold_in(arg_keys[18], 71), part)
    step_index = jax.random.randint(part_splits[17], (1,), 0, STEPS).astype(jnp.int32)
    return dict(latent=latent, main_hidden=main_hidden, main_query=main_query, text_key=text_key, text_value=text_value, text_len=text_len, guide_hidden=guide_hidden, guide_query=guide_query, guide_key=guide_key, guide_value=guide_value, guide_out=guide_out, main_head=main_head, guide_head=guide_head, main_modulation=main_modulation, guide_modulation=guide_modulation, guidance_scale=guidance_scale, sigma_table=sigma_table, step_index=step_index)


def start_state(height, heads, head_size):
    return (jnp.full((heads, height), -1e+30, jnp.float32), jnp.zeros((heads, height), jnp.float32), jnp.zeros((heads, height, head_size), jnp.float32))

def fold_step(running, queries, keys, values, heads, valid):
    height = queries.shape[0]
    head_size = queries.shape[1] // heads
    query_heads = queries.reshape(height, heads, head_size).astype(jnp.float32)
    key_heads = keys.reshape(keys.shape[0], heads, head_size).astype(jnp.float32)
    value_heads = values.reshape(values.shape[0], heads, head_size).astype(jnp.float32)
    scores = jnp.einsum('qhd,khd->hqk', query_heads, key_heads) * head_size ** (-0.5)
    scores = jnp.where(valid[None, None, :], scores, -1e+30)
    peak_old, totals, accumulated = running
    peak_new = jnp.maximum(peak_old, lax.optimization_barrier(jnp.max(scores, axis=-1)))
    weights = jnp.where(valid[None, None, :], jnp.exp(scores - peak_new[..., None]), 0.0)
    factor = jnp.exp(peak_old - peak_new)
    totals = totals * factor + lax.optimization_barrier(jnp.sum(weights, axis=-1))
    rounded = weights.astype(jnp.bfloat16).astype(jnp.float32)
    accumulated = accumulated * factor[..., None] + jnp.einsum('hqk,khd->hqd', rounded, value_heads)
    return (peak_new, totals, accumulated)

def finish(running):
    peak, totals, accumulated = running
    result = accumulated / totals[..., None]
    return result.transpose(1, 0, 2).reshape(result.shape[1], -1).astype(jnp.bfloat16)

def attention(queries, keys, values, heads, valid):
    height = queries.shape[0]
    block = math.gcd(height, 512)
    head_size = queries.shape[1] // heads
    blocks = queries.reshape(height // block, block, queries.shape[1])

    def one_block(query_block):
        state = start_state(block, heads, head_size)
        return finish(fold_step(state, query_block, keys, values, heads, valid))
    return lax.map(one_block, blocks).reshape(height, -1)

def head_out(summed, modulation, head_weight):
    centered = summed - lax.optimization_barrier(jnp.mean(summed, axis=-1, keepdims=True))
    spread = lax.optimization_barrier(jnp.mean(centered * centered, axis=-1, keepdims=True))
    normed = centered * lax.rsqrt(spread + 1e-06)
    shaped = (normed * (1.0 + modulation[1]) + modulation[0]).astype(jnp.bfloat16)
    return jnp.dot(shaped, head_weight, preferred_element_type=jnp.float32)

def reference(latent, main_hidden, main_query, text_key, text_value, text_len, guide_hidden, guide_query, guide_key, guide_value, guide_out, main_head, guide_head, main_modulation, guide_modulation, guidance_scale, sigma_table, step_index):
    live = jnp.arange(text_key.shape[0], dtype=jnp.int32) < text_len[0]
    main_attended = attention(main_query, text_key, text_value, HM, live)
    every = jnp.ones((guide_key.shape[0],), dtype=bool)
    guide_attended = attention(guide_query, guide_key, guide_value, GH, every)
    main_sum = main_hidden.astype(jnp.float32) + main_attended.astype(jnp.float32)
    guide_sum = guide_hidden.astype(jnp.float32) + jnp.dot(guide_attended, guide_out, preferred_element_type=jnp.float32)
    main_velocity = head_out(main_sum, main_modulation, main_head)
    guide_velocity = head_out(guide_sum, guide_modulation, guide_head)
    velocity = guide_velocity + guidance_scale[0] * (main_velocity - guide_velocity)
    positions = jnp.arange(sigma_table.shape[0], dtype=jnp.int32)
    sigma_now = jnp.sum(jnp.where(positions == step_index[0], sigma_table, 0.0))
    sigma_next = jnp.sum(jnp.where(positions == step_index[0] + 1, sigma_table, 0.0))
    next_latent = latent + (sigma_next - sigma_now) * velocity
    return (velocity, next_latent)
```

```python
import functools
import math

import jax
import jax.numpy as jnp
from jax import lax
from jax.experimental import pallas as pl
from jax.experimental.pallas import tpu as pltpu
from jax.sharding import PartitionSpec as P

HDIM = 128


def start_state(height, heads, head_size):
    return (
        jnp.full((heads, height), -1e30, jnp.float32),
        jnp.zeros((heads, height), jnp.float32),
        jnp.zeros((heads, height, head_size), jnp.float32),
    )


def fold_step(running, queries, keys, values, heads, valid):
    height = queries.shape[0]
    head_size = queries.shape[1] // heads
    query_heads = queries.reshape(height, heads, head_size)
    key_heads = keys.reshape(keys.shape[0], heads, head_size)
    value_heads = values.reshape(values.shape[0], heads, head_size)
    scores = jnp.einsum(
        "qhd,khd->hqk", query_heads, key_heads, preferred_element_type=jnp.float32
    ) * head_size ** (-0.5)
    if valid is not None:
        scores = jnp.where(valid[None, None, :], scores, -1e30)
    peak_old, totals, accumulated = running
    peak_new = jnp.maximum(peak_old, jnp.max(scores, axis=-1))
    weights = jnp.exp(scores - peak_new[..., None])
    if valid is not None:
        weights = jnp.where(valid[None, None, :], weights, 0.0)
    totals = jnp.sum(weights, axis=-1)
    accumulated = jnp.einsum(
        "hqk,khd->hqd",
        weights.astype(jnp.bfloat16),
        value_heads,
        preferred_element_type=jnp.float32,
    )
    return (peak_new, totals, accumulated)


def finish(running):
    peak, totals, accumulated = running
    result = accumulated / totals[..., None]
    return result.transpose(1, 0, 2).reshape(result.shape[1], -1).astype(jnp.bfloat16)


def head_out(summed, modulation, head_weight):
    centered = summed - jnp.mean(summed, axis=-1, keepdims=True)
    spread = jnp.mean(centered * centered, axis=-1, keepdims=True)
    normed = centered * lax.rsqrt(spread + 1e-06)
    shaped = (normed * (1.0 + modulation[1]) + modulation[0]).astype(jnp.bfloat16)
    return jnp.dot(shaped, head_weight, preferred_element_type=jnp.float32)


def per_device(
    latent,
    main_hidden,
    main_query,
    text_key,
    text_value,
    text_len,
    guide_hidden,
    guide_query,
    guide_key,
    guide_value,
    guide_out,
    main_head,
    guide_head,
    main_modulation,
    guide_modulation,
    guidance_scale,
    sigma_table,
    step_index,
):
    height = main_query.shape[0]
    main_heads = main_head.shape[0] // HDIM
    guide_heads = guide_out.shape[0] // HDIM
    all_text_keys = lax.all_gather(text_key, "seq", axis=0, tiled=True)
    all_text_values = lax.all_gather(text_value, "seq", axis=0, tiled=True)
    positions = jnp.arange(all_text_keys.shape[0], dtype=jnp.int32)
    folded = fold_step(
        start_state(height, main_heads, HDIM),
        main_query,
        all_text_keys,
        all_text_values,
        main_heads,
        positions < text_len[0],
    )
    main_sum = main_hidden.astype(jnp.float32) + finish(folded).astype(jnp.float32)
    main_velocity = head_out(main_sum, main_modulation, main_head)
    all_keys = lax.all_gather(guide_key, "seq", axis=0, tiled=True)
    all_values = lax.all_gather(guide_value, "seq", axis=0, tiled=True)
    folded = fold_step(
        start_state(height, guide_heads, HDIM), guide_query, all_keys, all_values, guide_heads, None
    )
    projected = jnp.dot(finish(folded), guide_out, preferred_element_type=jnp.float32)
    guide_sum = guide_hidden.astype(jnp.float32) + projected
    guide_velocity = head_out(guide_sum, guide_modulation, guide_head)
    velocity = guide_velocity + guidance_scale[0] * (main_velocity - guide_velocity)
    positions = jnp.arange(sigma_table.shape[0], dtype=jnp.int32)
    sigma_now = jnp.sum(jnp.where(positions == step_index[0], sigma_table, 0.0))
    sigma_next = jnp.sum(jnp.where(positions == step_index[0] + 1, sigma_table, 0.0))
    next_latent = latent + (sigma_next - sigma_now) * velocity
    return (velocity, next_latent)


def layout(mesh):
    axis = mesh.axis_names.index("seq")
    devices = mesh.devices
    for other in range(devices.ndim - 1, -1, -1):
        if other != axis:
            devices = devices.take(0, axis=other)
    places = [getattr(device, "coords", None) for device in devices]
    if places[0] is None:
        return 1, 1
    slab = sum(place[2] == places[0][2] for place in places)
    cores = sum(tuple(place) == tuple(places[0]) for place in places)
    return slab, cores


def shaped_rows(summed, modulation):
    centered = summed - jnp.mean(summed, axis=-1, keepdims=True)
    spread = jnp.mean(centered * centered, axis=-1, keepdims=True)
    normed = centered * lax.rsqrt(spread + 1e-06)
    return (normed * (1.0 + modulation[1:2]) + modulation[0:1]).astype(jnp.bfloat16)


def kernel(
    slabs,
    slab,
    cores,
    text_len,
    guidance_scale,
    sigma_table,
    step_index,
    latent,
    main_hidden,
    main_query,
    text_key,
    text_value,
    guide_hidden,
    guide_query,
    guide_key,
    guide_value,
    guide_out,
    main_head,
    guide_head,
    main_modulation,
    guide_modulation,
    velocity,
    next_latent,
    tk,
    tv,
    tq,
    to,
    att,
    gk,
    gv,
    gq,
    gacc,
    gml,
    racc,
    rml,
    v_latent,
    v_hidden,
    v_ghidden,
    v_gout,
    v_mhead,
    v_ghead,
    v_mmod,
    v_gmod,
    v_shaped,
    v_gshaped,
    local_sem,
    load_sem,
    t_send,
    t_recv,
    q_send,
    q_recv,
    g_send,
    g_recv,
    own_send,
    near_recv,
    fwd_send,
    far_recv,
    gc_send,
    gc_recv,
    o_send,
    o_recv,
    p_send,
    p_recv,
):
    me = lax.axis_index("seq")
    z = me // slab
    s = me % slab
    c = s % cores
    rows = main_query.shape[0]
    text_cols = tk.shape[-1]
    guide_cols = gk.shape[-1]
    heads = text_cols // HDIM
    guide_heads = guide_cols // HDIM
    keys = slabs * slab * tk.shape[2]
    guide_keys = slabs * cores * rows
    scale = HDIM ** (-0.5) * math.log2(math.e)

    def cols(ref, index, width):
        return ref.at[:, pl.ds(pl.multiple_of(index * width, 128), width)]

    def remote(src, dst, send, recv, target):
        return pltpu.make_async_remote_copy(
            src_ref=src,
            dst_ref=dst,
            send_sem=send,
            recv_sem=recv,
            device_id={"seq": target},
            device_id_type=pl.DeviceIdType.MESH,
        )

    def peer(j):
        return (s - c + (j // cores) * cores) % slab + (c + j) % cores

    def back(j):
        return (slab // cores - j // cores) % (slab // cores) * cores + (cores - j) % cores

    mine = [
        (cols(text_key, s, text_cols), tk.at[z, s]),
        (cols(text_value, s, text_cols), tv.at[z, s]),
        (cols(main_query, s, text_cols), tq.at[s]),
        (cols(guide_query, c, guide_cols), gq.at[s]),
        (cols(guide_key, c, guide_cols), gk.at[z, c]),
        (cols(guide_value, c, guide_cols), gv.at[z, c]),
    ]
    mine = [pltpu.make_async_copy(a, b, local_sem.at[i]) for i, (a, b) in enumerate(mine)]
    loads = [
        (main_hidden, v_hidden),
        (main_head, v_mhead),
        (main_modulation, v_mmod),
        (guide_out, v_gout),
        (guide_hidden, v_ghidden),
        (guide_head, v_ghead),
        (guide_modulation, v_gmod),
        (latent, v_latent),
    ]
    loads = [pltpu.make_async_copy(a, b, load_sem.at[i]) for i, (a, b) in enumerate(loads)]
    for copy in mine:
        copy.start()

    barrier = pltpu.get_barrier_semaphore()

    def greet(target):
        pl.semaphore_signal(
            barrier, inc=1, device_id={"seq": target}, device_id_type=pl.DeviceIdType.MESH
        )

    for j in range(1, slab):
        greet(z * slab + peer(j))

    @pl.when(z > 0)
    def _():
        greet(me - slab)

    @pl.when(z < slabs - 1)
    def _():
        greet(me + slab)

    ends = jnp.where(z > 0, 1, 0) + jnp.where(z < slabs - 1, 1, 0)
    pl.semaphore_wait(barrier, slab - 1 + ends)

    target = (me - slab, me + slab)
    has_target = (z > 0, z < slabs - 1)
    sent = []

    def both_ways(make):
        for way in range(2):

            @pl.when(has_target[way])
            def _(way=way):
                for copy in make(way):
                    copy.start()

            sent.append((has_target[way], functools.partial(make, way)))

    both = ((text_key, tk), (text_value, tv))
    guide_both = ((guide_key, gk), (guide_value, gv))

    def slab_text(j, kv):
        source, place = both[kv]
        t = peer(j)
        return remote(
            cols(source, t, text_cols),
            place.at[z, s],
            t_send.at[j, kv],
            t_recv.at[back(j), kv],
            z * slab + t,
        )

    def chain_own(j, kv, way):
        source, place = both[kv]
        t = peer(j)
        src = cols(source, s, text_cols) if j == 0 else place.at[z, t]
        return remote(
            src, place.at[z, t], own_send.at[way, j, kv], near_recv.at[way, j, kv], target[way]
        )

    def slab_guide(j, kv):
        source, place = guide_both[kv]
        t = peer(j)
        return remote(
            cols(source, t % cores, guide_cols),
            place.at[z, c],
            g_send.at[j, kv],
            g_recv.at[back(j), kv],
            z * slab + t,
        )

    def slab_query(j):
        t = peer(j)
        return (
            remote(
                cols(main_query, t, text_cols),
                tq.at[s],
                q_send.at[j, 0],
                q_recv.at[back(j), 0],
                z * slab + t,
            ),
            remote(
                cols(guide_query, t % cores, guide_cols),
                gq.at[s],
                q_send.at[j, 1],
                q_recv.at[back(j), 1],
                z * slab + t,
            ),
        )

    for kv in range(2):
        for j in range(slab - 1, 0, -1):
            slab_text(j, kv).start()
        both_ways(lambda way, kv=kv: [chain_own(0, kv, way)])
    for kv in range(2):
        for j in range(1, cores):
            slab_guide(j, kv).start()
    for j in range(slab - 1, 0, -1):
        for copy in slab_query(j):
            copy.start()
    for copy in loads:
        copy.start()

    def arrived(place, sem):
        pltpu.make_async_copy(place, place, sem).wait()

    for kv in range(2):
        place = both[kv][1]
        for j in range(1, slab):
            arrived(place.at[z, peer(j)], t_recv.at[j, kv])
            both_ways(lambda way, kv=kv, j=j: [chain_own(j, kv, way)])
    for copy in mine:
        copy.wait()
    for kv in range(2):
        place = guide_both[kv][1]
        for j in range(1, cores):
            arrived(place.at[z, peer(j) % cores], g_recv.at[j, kv])

    def guide_chain(d, kv, way):
        place = guide_both[kv][1]
        from_z = z + d if way == 0 else z - d
        return remote(
            place.at[from_z],
            place.at[from_z],
            gc_send.at[way, d, kv],
            gc_recv.at[way, d, kv],
            target[way],
        )

    both_ways(lambda way: [guide_chain(0, 0, way), guide_chain(0, 1, way)])

    def text_chain(d, kv, way):
        place = both[kv][1]
        from_z = z + d if way == 0 else z - d
        return remote(
            place.at[from_z],
            place.at[from_z],
            fwd_send.at[way, d, kv],
            far_recv.at[way, d, kv],
            target[way],
        )

    for d in range(1, slabs):
        for kv in range(2):
            place = both[kv][1]
            for way in range(2):
                from_z = z + d if way == 0 else z - d
                comes = from_z < slabs if way == 0 else from_z >= 0

                @pl.when(comes)
                def _(way=way, kv=kv, d=d, place=place, from_z=from_z):
                    if d == 1:
                        for j in range(slab):
                            arrived(place.at[from_z, peer(j)], near_recv.at[way, j, kv])
                    else:
                        arrived(place.at[from_z], far_recv.at[way, d - 1, kv])

                if d < slabs - 1:
                    goes = jnp.logical_and(comes, has_target[way])

                    @pl.when(goes)
                    def _(way=way, kv=kv, d=d):
                        text_chain(d, kv, way).start()

                    sent.append((goes, lambda way=way, kv=kv, d=d: [text_chain(d, kv, way)]))

    def guide_arrived(d, way):
        from_z = z + d if way == 0 else z - d
        for kv in range(2):
            arrived(guide_both[kv][1].at[from_z], gc_recv.at[way, d - 1, kv])

    for d in range(1, slabs):
        for way in range(2):
            comes = z + d < slabs if way == 0 else z - d >= 0
            goes = jnp.logical_and(comes, has_target[way])

            @pl.when(goes)
            def _(way=way, d=d):
                guide_arrived(d, way)
                if d < slabs - 1:
                    for kv in range(2):
                        guide_chain(d, kv, way).start()

            if d < slabs - 1:
                sent.append(
                    (goes, lambda way=way, d=d: [guide_chain(d, kv, way) for kv in range(2)])
                )

    for j in range(1, slab):
        arrived(tq.at[peer(j)], q_recv.at[j, 0])
        arrived(gq.at[peer(j)], q_recv.at[j, 1])

    positions = lax.broadcasted_iota(jnp.int32, (1, keys), 1)
    bias = jnp.where(positions < text_len[0], 0.0, -1e30).astype(jnp.float32)

    def weigh(q, k, bias=None):
        scores = lax.dot_general(
            q, k, (((1,), (1,)), ((), ())), preferred_element_type=jnp.float32
        )
        if bias is not None:
            scores = scores + bias
        peak = jnp.max(scores, axis=-1, keepdims=True)
        weights = jnp.exp2((scores - peak) * scale)
        return peak, weights, jnp.sum(weights, axis=-1, keepdims=True)

    groups = 2 if heads % 2 == 0 else 1
    width = text_cols // groups

    def give(j, group):
        t = peer(j)
        at = pl.ds(pl.multiple_of(s * text_cols + group * width, 128), width)
        return remote(
            to.at[t, :, pl.ds(group * width, width)],
            att.at[:, at],
            o_send.at[j, group],
            o_recv.at[back(j), group],
            z * slab + t,
        )

    for group in range(groups):

        def one_head(h, _):
            at = pl.ds(pl.multiple_of(group * width + h * HDIM, 128), HDIM)
            k = tk[:, :, :, at].reshape(keys, HDIM)
            v = tv[:, :, :, at].reshape(keys, HDIM)
            for t in range(slab):
                _, weights, total = weigh(tq[t, :, at], k, bias)
                out = jnp.dot(weights.astype(jnp.bfloat16), v, preferred_element_type=jnp.float32)
                to[t, :, at] = (out / total).astype(jnp.bfloat16)
            return 0

        lax.fori_loop(0, heads // groups, one_head, 0)
        for j in range(slab - 1, 0, -1):
            give(j, group).start()
    own_att = pltpu.make_async_copy(to.at[s], cols(att, s, text_cols), local_sem.at[0])
    own_att.start()

    for d in range(1, slabs):
        for way in range(2):
            comes = z + d < slabs if way == 0 else z - d >= 0
            last = jnp.logical_and(comes, jnp.logical_not(has_target[way]))

            @pl.when(last)
            def _(way=way, d=d):
                guide_arrived(d, way)

    for h in range(guide_heads):
        at = pl.ds(h * HDIM, HDIM)

        def one_owner(t, _):
            k = gk[:, :, :, at].reshape(guide_keys, HDIM)
            v = gv[:, :, :, at].reshape(guide_keys, HDIM)
            peak, weights, total = weigh(gq[t, :, at], k)
            gacc[t, :, at] = jnp.dot(
                weights.astype(jnp.bfloat16), v, preferred_element_type=jnp.float32
            )
            gml[t, :, h : h + 1] = peak
            gml[t, :, guide_heads + h : guide_heads + h + 1] = total
            return 0

        lax.fori_loop(0, slab, one_owner, 0)

    def part(j):
        t = peer(j)
        return (
            remote(gacc.at[t], racc.at[s], p_send.at[j, 0], p_recv.at[back(j), 0], z * slab + t),
            remote(gml.at[t], rml.at[s], p_send.at[j, 1], p_recv.at[back(j), 1], z * slab + t),
        )

    for j in range(slab - 1, 0, -1):
        for copy in part(j):
            copy.start()
    own_part = [
        pltpu.make_async_copy(gacc.at[s], racc.at[s], local_sem.at[1]),
        pltpu.make_async_copy(gml.at[s], rml.at[s], local_sem.at[2]),
    ]
    for copy in own_part:
        copy.start()

    for copy in loads:
        copy.wait()
    own_att.wait()
    for j in range(1, slab):
        for group in range(groups):
            at = pl.ds(pl.multiple_of(peer(j) * text_cols + group * width, 128), width)
            arrived(att.at[:, at], o_recv.at[j, group])

    step = 16

    def main_rows(i, _):
        at = pl.ds(pl.multiple_of(i * step, step), step)
        summed = v_hidden[at, :].astype(jnp.float32) + att[at, :].astype(jnp.float32)
        v_shaped[at, :] = shaped_rows(summed, v_mmod[...])
        return 0

    lax.fori_loop(0, rows // step, main_rows, 0)
    main_velocity = jnp.dot(v_shaped[...], v_mhead[...], preferred_element_type=jnp.float32)

    for copy in own_part:
        copy.wait()
    for j in range(1, slab):
        arrived(racc.at[peer(j)], p_recv.at[j, 0])
        arrived(rml.at[peer(j)], p_recv.at[j, 1])

    pieces = []
    for core in range(cores):
        members = range(core, slab, cores)
        for h in range(guide_heads):
            peaks = [rml[t, :, h : h + 1] for t in members]
            totals = [rml[t, :, guide_heads + h : guide_heads + h + 1] for t in members]
            peak = functools.reduce(jnp.maximum, peaks)
            factors = [jnp.exp2((p - peak) * scale) for p in peaks]
            total = sum(f * l for f, l in zip(factors, totals))
            summed = sum(
                f * racc[t, :, h * HDIM : (h + 1) * HDIM] for f, t in zip(factors, members)
            )
            pieces.append((summed / total).astype(jnp.bfloat16))
    guide_attended = jnp.concatenate(pieces, axis=-1)
    guide_sum = v_ghidden[...].astype(jnp.float32) + jnp.dot(
        guide_attended, v_gout[...], preferred_element_type=jnp.float32
    )
    v_gshaped[...] = shaped_rows(guide_sum, v_gmod[...])
    guide_velocity = jnp.dot(v_gshaped[...], v_ghead[...], preferred_element_type=jnp.float32)
    result = guide_velocity + guidance_scale[0] * (main_velocity - guide_velocity)
    now = step_index[0]
    velocity[...] = result
    next_latent[...] = v_latent[...] + (sigma_table[now + 1] - sigma_table[now]) * result

    for j in range(1, slab):
        for kv in range(2):
            slab_text(j, kv).wait_send()
            if j < cores:
                slab_guide(j, kv).wait_send()
        for copy in slab_query(j):
            copy.wait_send()
        for group in range(groups):
            give(j, group).wait_send()
        for copy in part(j):
            copy.wait_send()
    for goes, make in sent:

        @pl.when(goes)
        def _(make=make):
            for copy in make():
                copy.wait_send()


def fused(slabs, slab, cores, *args):
    (
        latent,
        main_hidden,
        main_query,
        text_key,
        text_value,
        text_len,
        guide_hidden,
        guide_query,
        guide_key,
        guide_value,
        guide_out,
        main_head,
        guide_head,
        main_modulation,
        guide_modulation,
        guidance_scale,
        sigma_table,
        step_index,
    ) = args
    rows, width = main_query.shape
    text_rows = text_key.shape[0]
    guide_width = guide_query.shape[1]
    text_cols = width // slab
    guide_cols = guide_width // cores
    bf16, f32 = jnp.bfloat16, jnp.float32
    dma = pltpu.SemaphoreType.DMA
    like = lambda x: pltpu.VMEM(x.shape, x.dtype)
    scratch = [
        pltpu.VMEM((slabs, slab, text_rows, text_cols), bf16),
        pltpu.VMEM((slabs, slab, text_rows, text_cols), bf16),
        pltpu.VMEM((slab, rows, text_cols), bf16),
        pltpu.VMEM((slab, rows, text_cols), bf16),
        pltpu.VMEM((rows, width), bf16),
        pltpu.VMEM((slabs, cores, rows, guide_cols), bf16),
        pltpu.VMEM((slabs, cores, rows, guide_cols), bf16),
        pltpu.VMEM((slab, rows, guide_cols), bf16),
        pltpu.VMEM((slab, rows, guide_cols), f32),
        pltpu.VMEM((slab, rows, 128), f32),
        pltpu.VMEM((slab, rows, guide_cols), f32),
        pltpu.VMEM((slab, rows, 128), f32),
        like(latent),
        like(main_hidden),
        like(guide_hidden),
        like(guide_out),
        like(main_head),
        like(guide_head),
        like(main_modulation),
        like(guide_modulation),
        pltpu.VMEM(main_hidden.shape, bf16),
        pltpu.VMEM(guide_hidden.shape, bf16),
        dma((6,)),
        dma((8,)),
        dma((slab, 2)),
        dma((slab, 2)),
        dma((slab, 2)),
        dma((slab, 2)),
        dma((cores, 2)),
        dma((cores, 2)),
        dma((2, slab, 2)),
        dma((2, slab, 2)),
        dma((2, slabs, 2)),
        dma((2, slabs, 2)),
        dma((2, slabs, 2)),
        dma((2, slabs, 2)),
        dma((slab, 2)),
        dma((slab, 2)),
        dma((slab, 2)),
        dma((slab, 2)),
    ]
    keys, guide_keys = slabs * slab * text_rows, slabs * cores * rows
    out = jax.ShapeDtypeStruct(latent.shape, f32)
    return pl.pallas_call(
        functools.partial(kernel, slabs, slab, cores),
        out_shape=(out, out),
        in_specs=[pl.BlockSpec(memory_space=pltpu.SMEM)] * 4
        + [pl.BlockSpec(memory_space=pl.ANY)] * 14,
        out_specs=[pl.BlockSpec(memory_space=pltpu.VMEM)] * 2,
        scratch_shapes=scratch,
        compiler_params=pltpu.CompilerParams(
            collective_id=0, has_side_effects=True, vmem_limit_bytes=48 * 1024 * 1024
        ),
        cost_estimate=pl.CostEstimate(
            flops=4 * rows * (keys * width + guide_keys * guide_width * slab // cores),
            bytes_accessed=2 * (2 * text_rows + 2 * rows) * width,
            transcendentals=rows * keys * width // HDIM,
        ),
    )(
        text_len,
        guidance_scale,
        sigma_table,
        step_index,
        latent,
        main_hidden,
        main_query,
        text_key,
        text_value,
        guide_hidden,
        guide_query,
        guide_key,
        guide_value,
        guide_out,
        main_head,
        guide_head,
        main_modulation,
        guide_modulation,
    )


def choose(count, slab, cores, *args):
    rows, width = args[2].shape
    text_rows = args[3].shape[0]
    guide_width = args[7].shape[1]
    fits = (
        slab > 1
        and cores > 1
        and count % slab == 0
        and slab % cores == 0
        and count > slab
        and rows % 16 == 0
        and text_rows % 16 == 0
        and width % (slab * HDIM) == 0
        and guide_width % (cores * HDIM) == 0
    )
    if fits:
        return fused(count // slab, slab, cores, *args)
    return per_device(*args)


def solution(mesh):
    placed = (
        P(("parts", "seq"), None),
        P(("parts", "seq"), None),
        P(("parts", "seq"), None),
        P(("parts", "seq"), None),
        P(("parts", "seq"), None),
        P("parts"),
        P(("parts", "seq"), None),
        P(("parts", "seq"), None),
        P(("parts", "seq"), None),
        P(("parts", "seq"), None),
        P(),
        P(),
        P(),
        P("parts", None),
        P("parts", None),
        P("parts"),
        P(),
        P("parts"),
    )
    slab, cores = layout(mesh)
    return jax.shard_map(
        functools.partial(choose, mesh.shape["seq"], slab, cores),
        mesh=mesh,
        in_specs=placed,
        out_specs=(P(("parts", "seq"), None), P(("parts", "seq"), None)),
        check_vma=False,
    )
```

```python
import functools
import math

import jax
import jax.numpy as jnp
from jax import lax
from jax.experimental import pallas as pl
from jax.experimental.pallas import tpu as pltpu
from jax.sharding import PartitionSpec as P

HDIM = 128


def start_state(height, heads, head_size):
    return (
        jnp.full((heads, height), -1e30, jnp.float32),
        jnp.zeros((heads, height), jnp.float32),
        jnp.zeros((heads, height, head_size), jnp.float32),
    )


def fold_step(running, queries, keys, values, heads, valid):
    height = queries.shape[0]
    head_size = queries.shape[1] // heads
    query_heads = queries.reshape(height, heads, head_size)
    key_heads = keys.reshape(keys.shape[0], heads, head_size)
    value_heads = values.reshape(values.shape[0], heads, head_size)
    scores = jnp.einsum(
        "qhd,khd->hqk", query_heads, key_heads, preferred_element_type=jnp.float32
    ) * head_size ** (-0.5)
    if valid is not None:
        scores = jnp.where(valid[None, None, :], scores, -1e30)
    peak_old, totals, accumulated = running
    peak_new = jnp.maximum(peak_old, jnp.max(scores, axis=-1))
    weights = jnp.exp(scores - peak_new[..., None])
    if valid is not None:
        weights = jnp.where(valid[None, None, :], weights, 0.0)
    totals = jnp.sum(weights, axis=-1)
    accumulated = jnp.einsum(
        "hqk,khd->hqd",
        weights.astype(jnp.bfloat16),
        value_heads,
        preferred_element_type=jnp.float32,
    )
    return (peak_new, totals, accumulated)


def finish(running):
    peak, totals, accumulated = running
    result = accumulated / totals[..., None]
    return result.transpose(1, 0, 2).reshape(result.shape[1], -1).astype(jnp.bfloat16)


def head_out(summed, modulation, head_weight):
    centered = summed - jnp.mean(summed, axis=-1, keepdims=True)
    spread = jnp.mean(centered * centered, axis=-1, keepdims=True)
    normed = centered * lax.rsqrt(spread + 1e-06)
    shaped = (normed * (1.0 + modulation[1]) + modulation[0]).astype(jnp.bfloat16)
    return jnp.dot(shaped, head_weight, preferred_element_type=jnp.float32)


def per_device(
    latent,
    main_hidden,
    main_query,
    text_key,
    text_value,
    text_len,
    guide_hidden,
    guide_query,
    guide_key,
    guide_value,
    guide_out,
    main_head,
    guide_head,
    main_modulation,
    guide_modulation,
    guidance_scale,
    sigma_table,
    step_index,
):
    height = main_query.shape[0]
    main_heads = main_head.shape[0] // HDIM
    guide_heads = guide_out.shape[0] // HDIM
    all_text_keys = lax.all_gather(text_key, "seq", axis=0, tiled=True)
    all_text_values = lax.all_gather(text_value, "seq", axis=0, tiled=True)
    positions = jnp.arange(all_text_keys.shape[0], dtype=jnp.int32)
    folded = fold_step(
        start_state(height, main_heads, HDIM),
        main_query,
        all_text_keys,
        all_text_values,
        main_heads,
        positions < text_len[0],
    )
    main_sum = main_hidden.astype(jnp.float32) + finish(folded).astype(jnp.float32)
    main_velocity = head_out(main_sum, main_modulation, main_head)
    all_keys = lax.all_gather(guide_key, "seq", axis=0, tiled=True)
    all_values = lax.all_gather(guide_value, "seq", axis=0, tiled=True)
    folded = fold_step(
        start_state(height, guide_heads, HDIM), guide_query, all_keys, all_values, guide_heads, None
    )
    projected = jnp.dot(finish(folded), guide_out, preferred_element_type=jnp.float32)
    guide_sum = guide_hidden.astype(jnp.float32) + projected
    guide_velocity = head_out(guide_sum, guide_modulation, guide_head)
    velocity = guide_velocity + guidance_scale[0] * (main_velocity - guide_velocity)
    positions = jnp.arange(sigma_table.shape[0], dtype=jnp.int32)
    sigma_now = jnp.sum(jnp.where(positions == step_index[0], sigma_table, 0.0))
    sigma_next = jnp.sum(jnp.where(positions == step_index[0] + 1, sigma_table, 0.0))
    next_latent = latent + (sigma_next - sigma_now) * velocity
    return (velocity, next_latent)


def layout(mesh):
    axis = mesh.axis_names.index("seq")
    devices = mesh.devices
    for other in range(devices.ndim - 1, -1, -1):
        if other != axis:
            devices = devices.take(0, axis=other)
    places = [getattr(device, "coords", None) for device in devices]
    if places[0] is None:
        return 1, 1
    slab = sum(place[2] == places[0][2] for place in places)
    cores = sum(tuple(place) == tuple(places[0]) for place in places)
    return slab, cores


def shaped_rows(summed, modulation):
    centered = summed - jnp.mean(summed, axis=-1, keepdims=True)
    spread = jnp.mean(centered * centered, axis=-1, keepdims=True)
    normed = centered * lax.rsqrt(spread + 1e-06)
    return (normed * (1.0 + modulation[1:2]) + modulation[0:1]).astype(jnp.bfloat16)


def across(a, b):
    return lax.dot_general(a, b, (((1,), (1,)), ((), ())), preferred_element_type=jnp.float32)


def kernel(
    slabs,
    slab,
    cores,
    text_len,
    guidance_scale,
    sigma_table,
    step_index,
    main_hidden,
    main_query,
    text_key,
    text_value,
    guide_hidden,
    guide_query,
    guide_key,
    guide_value,
    guide_out,
    main_head,
    guide_head,
    main_modulation,
    guide_modulation,
    plain,
    guided,
    change,
    tk,
    tv,
    tq,
    to,
    att,
    gk,
    gv,
    gq,
    gacc,
    gml,
    racc,
    rml,
    v_hidden,
    v_ghidden,
    v_gout,
    v_mhead,
    v_ghead,
    v_mmod,
    v_gmod,
    v_shaped,
    v_gshaped,
    local_sem,
    load_sem,
    t_send,
    t_recv,
    q_send,
    q_recv,
    g_send,
    g_recv,
    own_send,
    near_recv,
    fwd_send,
    far_recv,
    gc_send,
    gc_recv,
    o_send,
    o_recv,
    p_send,
    p_recv,
):
    me = lax.axis_index("seq")
    z = me // slab
    s = me % slab
    c = s % cores
    rows = main_query.shape[0]
    text_cols = tk.shape[-1]
    guide_cols = gk.shape[-1]
    heads = text_cols // HDIM
    guide_heads = guide_cols // HDIM
    keys = slabs * slab * tk.shape[2]
    guide_keys = slabs * cores * rows
    scale = HDIM ** (-0.5) * math.log2(math.e)

    def cols(ref, index, width):
        return ref.at[:, pl.ds(pl.multiple_of(index * width, 128), width)]

    def remote(src, dst, send, recv, target):
        return pltpu.make_async_remote_copy(
            src_ref=src,
            dst_ref=dst,
            send_sem=send,
            recv_sem=recv,
            device_id={"seq": target},
            device_id_type=pl.DeviceIdType.MESH,
        )

    def peer(j):
        return (s - c + (j // cores) * cores) % slab + (c + j) % cores

    def back(j):
        return (slab // cores - j // cores) % (slab // cores) * cores + (cores - j) % cores

    mine = [
        (cols(text_key, s, text_cols), tk.at[z, s]),
        (cols(text_value, s, text_cols), tv.at[z, s]),
        (cols(main_query, s, text_cols), tq.at[s]),
        (cols(guide_query, c, guide_cols), gq.at[s]),
        (cols(guide_key, c, guide_cols), gk.at[z, c]),
        (cols(guide_value, c, guide_cols), gv.at[z, c]),
    ]
    mine = [pltpu.make_async_copy(a, b, local_sem.at[i]) for i, (a, b) in enumerate(mine)]
    loads = [
        (main_hidden, v_hidden),
        (main_head, v_mhead),
        (main_modulation, v_mmod),
        (guide_out, v_gout),
        (guide_hidden, v_ghidden),
        (guide_head, v_ghead),
        (guide_modulation, v_gmod),
    ]
    loads = [pltpu.make_async_copy(a, b, load_sem.at[i]) for i, (a, b) in enumerate(loads)]
    for copy in mine:
        copy.start()

    barrier = pltpu.get_barrier_semaphore()

    def greet(target):
        pl.semaphore_signal(
            barrier, inc=1, device_id={"seq": target}, device_id_type=pl.DeviceIdType.MESH
        )

    for j in range(1, slab):
        greet(z * slab + peer(j))

    @pl.when(z > 0)
    def _():
        greet(me - slab)

    @pl.when(z < slabs - 1)
    def _():
        greet(me + slab)

    ends = jnp.where(z > 0, 1, 0) + jnp.where(z < slabs - 1, 1, 0)
    pl.semaphore_wait(barrier, slab - 1 + ends)

    target = (me - slab, me + slab)
    has_target = (z > 0, z < slabs - 1)
    sent = []

    def both_ways(make):
        for way in range(2):

            @pl.when(has_target[way])
            def _(way=way):
                for copy in make(way):
                    copy.start()

            sent.append((has_target[way], functools.partial(make, way)))

    both = ((text_key, tk), (text_value, tv))
    guide_both = ((guide_key, gk), (guide_value, gv))

    def slab_text(j, kv):
        source, place = both[kv]
        t = peer(j)
        return remote(
            cols(source, t, text_cols),
            place.at[z, s],
            t_send.at[j, kv],
            t_recv.at[back(j), kv],
            z * slab + t,
        )

    def chain_own(j, kv, way):
        source, place = both[kv]
        t = peer(j)
        src = cols(source, s, text_cols) if j == 0 else place.at[z, t]
        return remote(
            src, place.at[z, t], own_send.at[way, j, kv], near_recv.at[way, j, kv], target[way]
        )

    def slab_guide(j, kv):
        source, place = guide_both[kv]
        t = peer(j)
        return remote(
            cols(source, t % cores, guide_cols),
            place.at[z, c],
            g_send.at[j, kv],
            g_recv.at[back(j), kv],
            z * slab + t,
        )

    def slab_query(j):
        t = peer(j)
        return (
            remote(
                cols(main_query, t, text_cols),
                tq.at[s],
                q_send.at[j, 0],
                q_recv.at[back(j), 0],
                z * slab + t,
            ),
            remote(
                cols(guide_query, t % cores, guide_cols),
                gq.at[s],
                q_send.at[j, 1],
                q_recv.at[back(j), 1],
                z * slab + t,
            ),
        )

    for kv in range(2):
        for j in range(slab - 1, 0, -1):
            slab_text(j, kv).start()
        both_ways(lambda way, kv=kv: [chain_own(0, kv, way)])
    for kv in range(2):
        for j in range(1, cores):
            slab_guide(j, kv).start()
    for j in range(slab - 1, 0, -1):
        for copy in slab_query(j):
            copy.start()
    for copy in loads:
        copy.start()

    def arrived(place, sem):
        pltpu.make_async_copy(place, place, sem).wait()

    for kv in range(2):
        place = both[kv][1]
        for j in range(1, slab):
            arrived(place.at[z, peer(j)], t_recv.at[j, kv])
            both_ways(lambda way, kv=kv, j=j: [chain_own(j, kv, way)])
    for copy in mine:
        copy.wait()
    for kv in range(2):
        place = guide_both[kv][1]
        for j in range(1, cores):
            arrived(place.at[z, peer(j) % cores], g_recv.at[j, kv])

    def guide_chain(d, kv, way):
        place = guide_both[kv][1]
        from_z = z + d if way == 0 else z - d
        return remote(
            place.at[from_z],
            place.at[from_z],
            gc_send.at[way, d, kv],
            gc_recv.at[way, d, kv],
            target[way],
        )

    both_ways(lambda way: [guide_chain(0, 0, way), guide_chain(0, 1, way)])

    def text_chain(d, kv, way):
        place = both[kv][1]
        from_z = z + d if way == 0 else z - d
        return remote(
            place.at[from_z],
            place.at[from_z],
            fwd_send.at[way, d, kv],
            far_recv.at[way, d, kv],
            target[way],
        )

    for d in range(1, slabs):
        for kv in range(2):
            place = both[kv][1]
            for way in range(2):
                from_z = z + d if way == 0 else z - d
                comes = from_z < slabs if way == 0 else from_z >= 0

                @pl.when(comes)
                def _(way=way, kv=kv, d=d, place=place, from_z=from_z):
                    if d == 1:
                        for j in range(slab):
                            arrived(place.at[from_z, peer(j)], near_recv.at[way, j, kv])
                    else:
                        arrived(place.at[from_z], far_recv.at[way, d - 1, kv])

                if d < slabs - 1:
                    goes = jnp.logical_and(comes, has_target[way])

                    @pl.when(goes)
                    def _(way=way, kv=kv, d=d):
                        text_chain(d, kv, way).start()

                    sent.append((goes, lambda way=way, kv=kv, d=d: [text_chain(d, kv, way)]))

    def guide_arrived(d, way):
        from_z = z + d if way == 0 else z - d
        for kv in range(2):
            arrived(guide_both[kv][1].at[from_z], gc_recv.at[way, d - 1, kv])

    for d in range(1, slabs):
        for way in range(2):
            comes = z + d < slabs if way == 0 else z - d >= 0
            goes = jnp.logical_and(comes, has_target[way])

            @pl.when(goes)
            def _(way=way, d=d):
                guide_arrived(d, way)
                if d < slabs - 1:
                    for kv in range(2):
                        guide_chain(d, kv, way).start()

            if d < slabs - 1:
                sent.append(
                    (goes, lambda way=way, d=d: [guide_chain(d, kv, way) for kv in range(2)])
                )

    for j in range(1, slab):
        arrived(tq.at[peer(j)], q_recv.at[j, 0])
        arrived(gq.at[peer(j)], q_recv.at[j, 1])

    positions = lax.broadcasted_iota(jnp.int32, (1, keys), 1)
    bias = jnp.where(positions < text_len[0], 0.0, -1e30).astype(jnp.float32)

    def weigh(q, k, bias=None):
        scores = across(q, k)
        if bias is not None:
            scores = scores + bias
        peak = jnp.max(scores, axis=-1, keepdims=True)
        weights = jnp.exp2((scores - peak) * scale)
        return peak, weights, jnp.sum(weights, axis=-1, keepdims=True)

    groups = 2 if heads % 2 == 0 else 1
    width = text_cols // groups

    def give(j, group):
        t = peer(j)
        at = pl.ds(pl.multiple_of(s * text_cols + group * width, 128), width)
        return remote(
            to.at[t, :, pl.ds(group * width, width)],
            att.at[:, at],
            o_send.at[j, group],
            o_recv.at[back(j), group],
            z * slab + t,
        )

    for group in range(groups):

        def one_head(h, _):
            at = pl.ds(pl.multiple_of(group * width + h * HDIM, 128), HDIM)
            k = tk[:, :, :, at].reshape(keys, HDIM)
            v = tv[:, :, :, at].reshape(keys, HDIM)
            for t in range(slab):
                _, weights, total = weigh(tq[t, :, at], k, bias)
                out = jnp.dot(weights.astype(jnp.bfloat16), v, preferred_element_type=jnp.float32)
                to[t, :, at] = (out / total).astype(jnp.bfloat16)
            return 0

        lax.fori_loop(0, heads // groups, one_head, 0)
        for j in range(slab - 1, 0, -1):
            give(j, group).start()
    own_att = pltpu.make_async_copy(to.at[s], cols(att, s, text_cols), local_sem.at[0])
    own_att.start()

    for d in range(1, slabs):
        for way in range(2):
            comes = z + d < slabs if way == 0 else z - d >= 0
            last = jnp.logical_and(comes, jnp.logical_not(has_target[way]))

            @pl.when(last)
            def _(way=way, d=d):
                guide_arrived(d, way)

    for h in range(guide_heads):
        at = pl.ds(h * HDIM, HDIM)

        def one_owner(t, _):
            k = gk[:, :, :, at].reshape(guide_keys, HDIM)
            v = gv[:, :, :, at].reshape(guide_keys, HDIM)
            peak, weights, total = weigh(gq[t, :, at], k)
            gacc[t, :, at] = jnp.dot(
                weights.astype(jnp.bfloat16), v, preferred_element_type=jnp.float32
            )
            gml[t, :, h : h + 1] = peak
            gml[t, :, guide_heads + h : guide_heads + h + 1] = total
            return 0

        lax.fori_loop(0, slab, one_owner, 0)

    def part(j):
        t = peer(j)
        return (
            remote(gacc.at[t], racc.at[s], p_send.at[j, 0], p_recv.at[back(j), 0], z * slab + t),
            remote(gml.at[t], rml.at[s], p_send.at[j, 1], p_recv.at[back(j), 1], z * slab + t),
        )

    for j in range(slab - 1, 0, -1):
        for copy in part(j):
            copy.start()
    own_part = [
        pltpu.make_async_copy(gacc.at[s], racc.at[s], local_sem.at[1]),
        pltpu.make_async_copy(gml.at[s], rml.at[s], local_sem.at[2]),
    ]
    for copy in own_part:
        copy.start()

    for copy in loads:
        copy.wait()
    own_att.wait()
    for j in range(1, slab):
        for group in range(groups):
            at = pl.ds(pl.multiple_of(peer(j) * text_cols + group * width, 128), width)
            arrived(att.at[:, at], o_recv.at[j, group])

    step = 16

    def main_rows(i, _):
        at = pl.ds(pl.multiple_of(i * step, step), step)
        summed = v_hidden[at, :].astype(jnp.float32) + att[at, :].astype(jnp.float32)
        v_shaped[at, :] = shaped_rows(summed, v_mmod[...])
        return 0

    lax.fori_loop(0, rows // step, main_rows, 0)
    main_velocity = across(v_mhead[...], v_shaped[...])

    for copy in own_part:
        copy.wait()
    for j in range(1, slab):
        arrived(racc.at[peer(j)], p_recv.at[j, 0])
        arrived(rml.at[peer(j)], p_recv.at[j, 1])

    pieces = []
    for core in range(cores):
        members = range(core, slab, cores)
        for h in range(guide_heads):
            peaks = [rml[t, :, h : h + 1] for t in members]
            totals = [rml[t, :, guide_heads + h : guide_heads + h + 1] for t in members]
            peak = functools.reduce(jnp.maximum, peaks)
            factors = [jnp.exp2((p - peak) * scale) for p in peaks]
            total = sum(f * l for f, l in zip(factors, totals))
            summed = sum(
                f * racc[t, :, h * HDIM : (h + 1) * HDIM] for f, t in zip(factors, members)
            )
            pieces.append((summed / total).astype(jnp.bfloat16))
    guide_attended = jnp.concatenate(pieces, axis=-1)
    guide_sum = v_ghidden[...].astype(jnp.float32) + jnp.dot(
        guide_attended, v_gout[...], preferred_element_type=jnp.float32
    )
    v_gshaped[...] = shaped_rows(guide_sum, v_gmod[...])
    guide_velocity = across(v_ghead[...], v_gshaped[...])
    now = step_index[0]
    plain[...] = guide_velocity
    guided[...] = guidance_scale[0] * (main_velocity - guide_velocity)
    change[...] = jnp.full(change.shape, sigma_table[now + 1] - sigma_table[now], jnp.float32)

    for j in range(1, slab):
        for kv in range(2):
            slab_text(j, kv).wait_send()
            if j < cores:
                slab_guide(j, kv).wait_send()
        for copy in slab_query(j):
            copy.wait_send()
        for group in range(groups):
            give(j, group).wait_send()
        for copy in part(j):
            copy.wait_send()
    for goes, make in sent:

        @pl.when(goes)
        def _(make=make):
            for copy in make():
                copy.wait_send()


def fused(slabs, slab, cores, *args):
    (
        latent,
        main_hidden,
        main_query,
        text_key,
        text_value,
        text_len,
        guide_hidden,
        guide_query,
        guide_key,
        guide_value,
        guide_out,
        main_head,
        guide_head,
        main_modulation,
        guide_modulation,
        guidance_scale,
        sigma_table,
        step_index,
    ) = args
    main_head, guide_head = main_head.T, guide_head.T
    rows, width = main_query.shape
    text_rows = text_key.shape[0]
    guide_width = guide_query.shape[1]
    text_cols = width // slab
    guide_cols = guide_width // cores
    bf16, f32 = jnp.bfloat16, jnp.float32
    dma = pltpu.SemaphoreType.DMA
    like = lambda x: pltpu.VMEM(x.shape, x.dtype)
    scratch = [
        pltpu.VMEM((slabs, slab, text_rows, text_cols), bf16),
        pltpu.VMEM((slabs, slab, text_rows, text_cols), bf16),
        pltpu.VMEM((slab, rows, text_cols), bf16),
        pltpu.VMEM((slab, rows, text_cols), bf16),
        pltpu.VMEM((rows, width), bf16),
        pltpu.VMEM((slabs, cores, rows, guide_cols), bf16),
        pltpu.VMEM((slabs, cores, rows, guide_cols), bf16),
        pltpu.VMEM((slab, rows, guide_cols), bf16),
        pltpu.VMEM((slab, rows, guide_cols), f32),
        pltpu.VMEM((slab, rows, 128), f32),
        pltpu.VMEM((slab, rows, guide_cols), f32),
        pltpu.VMEM((slab, rows, 128), f32),
        like(main_hidden),
        like(guide_hidden),
        like(guide_out),
        like(main_head),
        like(guide_head),
        like(main_modulation),
        like(guide_modulation),
        pltpu.VMEM(main_hidden.shape, bf16),
        pltpu.VMEM(guide_hidden.shape, bf16),
        dma((6,)),
        dma((7,)),
        dma((slab, 2)),
        dma((slab, 2)),
        dma((slab, 2)),
        dma((slab, 2)),
        dma((cores, 2)),
        dma((cores, 2)),
        dma((2, slab, 2)),
        dma((2, slab, 2)),
        dma((2, slabs, 2)),
        dma((2, slabs, 2)),
        dma((2, slabs, 2)),
        dma((2, slabs, 2)),
        dma((slab, 2)),
        dma((slab, 2)),
        dma((slab, 2)),
        dma((slab, 2)),
    ]
    keys, guide_keys = slabs * slab * text_rows, slabs * cores * rows
    out = jax.ShapeDtypeStruct(latent.shape[::-1], f32)
    plain, guided, change = pl.pallas_call(
        functools.partial(kernel, slabs, slab, cores),
        out_shape=(out, out, jax.ShapeDtypeStruct((1, rows), f32)),
        in_specs=[pl.BlockSpec(memory_space=pltpu.SMEM)] * 4
        + [pl.BlockSpec(memory_space=pltpu.HBM)] * 13,
        out_specs=[pl.BlockSpec(memory_space=pltpu.VMEM)] * 3,
        scratch_shapes=scratch,
        compiler_params=pltpu.CompilerParams(
            collective_id=0, has_side_effects=True, vmem_limit_bytes=56 * 1024 * 1024
        ),
        cost_estimate=pl.CostEstimate(
            flops=4 * rows * (keys * width + guide_keys * guide_width * slab // cores),
            bytes_accessed=2 * (2 * text_rows + 2 * rows) * width,
            transcendentals=rows * keys * width // HDIM,
        ),
    )(
        text_len,
        guidance_scale,
        sigma_table,
        step_index,
        main_hidden,
        main_query,
        text_key,
        text_value,
        guide_hidden,
        guide_query,
        guide_key,
        guide_value,
        guide_out,
        main_head,
        guide_head,
        main_modulation,
        guide_modulation,
    )
    velocity = plain + guided
    return velocity.T, (latent.T + change * velocity).T


def choose(count, slab, cores, *args):
    rows, width = args[2].shape
    text_rows = args[3].shape[0]
    guide_width = args[7].shape[1]
    fits = (
        slab > 1
        and cores > 1
        and count % slab == 0
        and slab % cores == 0
        and count > slab
        and rows % 16 == 0
        and text_rows % 16 == 0
        and width % (slab * HDIM) == 0
        and guide_width % (cores * HDIM) == 0
    )
    if fits:
        return fused(count // slab, slab, cores, *args)
    return per_device(*args)


def solution(mesh):
    placed = (
        P(("parts", "seq"), None),
        P(("parts", "seq"), None),
        P(("parts", "seq"), None),
        P(("parts", "seq"), None),
        P(("parts", "seq"), None),
        P("parts"),
        P(("parts", "seq"), None),
        P(("parts", "seq"), None),
        P(("parts", "seq"), None),
        P(("parts", "seq"), None),
        P(),
        P(),
        P(),
        P("parts", None),
        P("parts", None),
        P("parts"),
        P(),
        P("parts"),
    )
    slab, cores = layout(mesh)
    return jax.shard_map(
        functools.partial(choose, mesh.shape["seq"], slab, cores),
        mesh=mesh,
        in_specs=placed,
        out_specs=(P(("parts", "seq"), None), P(("parts", "seq"), None)),
        check_vma=False,
    )
```

```python
import functools
import math

import jax
import jax.numpy as jnp
from jax import lax
from jax.experimental import pallas as pl
from jax.experimental.pallas import tpu as pltpu
from jax.sharding import PartitionSpec as P

HDIM = 128


def start_state(height, heads, head_size):
    return (
        jnp.full((heads, height), -1e30, jnp.float32),
        jnp.zeros((heads, height), jnp.float32),
        jnp.zeros((heads, height, head_size), jnp.float32),
    )


def fold_step(running, queries, keys, values, heads, valid):
    height = queries.shape[0]
    head_size = queries.shape[1] // heads
    query_heads = queries.reshape(height, heads, head_size)
    key_heads = keys.reshape(keys.shape[0], heads, head_size)
    value_heads = values.reshape(values.shape[0], heads, head_size)
    scores = jnp.einsum(
        "qhd,khd->hqk", query_heads, key_heads, preferred_element_type=jnp.float32
    ) * head_size ** (-0.5)
    if valid is not None:
        scores = jnp.where(valid[None, None, :], scores, -1e30)
    peak_old, totals, accumulated = running
    peak_new = jnp.maximum(peak_old, jnp.max(scores, axis=-1))
    weights = jnp.exp(scores - peak_new[..., None])
    if valid is not None:
        weights = jnp.where(valid[None, None, :], weights, 0.0)
    totals = jnp.sum(weights, axis=-1)
    accumulated = jnp.einsum(
        "hqk,khd->hqd",
        weights.astype(jnp.bfloat16),
        value_heads,
        preferred_element_type=jnp.float32,
    )
    return (peak_new, totals, accumulated)


def finish(running):
    peak, totals, accumulated = running
    result = accumulated / totals[..., None]
    return result.transpose(1, 0, 2).reshape(result.shape[1], -1).astype(jnp.bfloat16)


def head_out(summed, modulation, head_weight):
    centered = summed - jnp.mean(summed, axis=-1, keepdims=True)
    spread = jnp.mean(centered * centered, axis=-1, keepdims=True)
    normed = centered * lax.rsqrt(spread + 1e-06)
    shaped = (normed * (1.0 + modulation[1]) + modulation[0]).astype(jnp.bfloat16)
    return jnp.dot(shaped, head_weight, preferred_element_type=jnp.float32)


def per_device(
    latent,
    main_hidden,
    main_query,
    text_key,
    text_value,
    text_len,
    guide_hidden,
    guide_query,
    guide_key,
    guide_value,
    guide_out,
    main_head,
    guide_head,
    main_modulation,
    guide_modulation,
    guidance_scale,
    sigma_table,
    step_index,
):
    height = main_query.shape[0]
    main_heads = main_head.shape[0] // HDIM
    guide_heads = guide_out.shape[0] // HDIM
    all_text_keys = lax.all_gather(text_key, "seq", axis=0, tiled=True)
    all_text_values = lax.all_gather(text_value, "seq", axis=0, tiled=True)
    positions = jnp.arange(all_text_keys.shape[0], dtype=jnp.int32)
    folded = fold_step(
        start_state(height, main_heads, HDIM),
        main_query,
        all_text_keys,
        all_text_values,
        main_heads,
        positions < text_len[0],
    )
    main_sum = main_hidden.astype(jnp.float32) + finish(folded).astype(jnp.float32)
    main_velocity = head_out(main_sum, main_modulation, main_head)
    all_keys = lax.all_gather(guide_key, "seq", axis=0, tiled=True)
    all_values = lax.all_gather(guide_value, "seq", axis=0, tiled=True)
    folded = fold_step(
        start_state(height, guide_heads, HDIM), guide_query, all_keys, all_values, guide_heads, None
    )
    projected = jnp.dot(finish(folded), guide_out, preferred_element_type=jnp.float32)
    guide_sum = guide_hidden.astype(jnp.float32) + projected
    guide_velocity = head_out(guide_sum, guide_modulation, guide_head)
    velocity = guide_velocity + guidance_scale[0] * (main_velocity - guide_velocity)
    positions = jnp.arange(sigma_table.shape[0], dtype=jnp.int32)
    sigma_now = jnp.sum(jnp.where(positions == step_index[0], sigma_table, 0.0))
    sigma_next = jnp.sum(jnp.where(positions == step_index[0] + 1, sigma_table, 0.0))
    next_latent = latent + (sigma_next - sigma_now) * velocity
    return (velocity, next_latent)


def layout(mesh):
    axis = mesh.axis_names.index("seq")
    devices = mesh.devices
    for other in range(devices.ndim - 1, -1, -1):
        if other != axis:
            devices = devices.take(0, axis=other)
    places = [getattr(device, "coords", None) for device in devices]
    if places[0] is None:
        return 1, 1
    slab = sum(place[2] == places[0][2] for place in places)
    cores = sum(tuple(place) == tuple(places[0]) for place in places)
    return slab, cores


def shaped_rows(summed, modulation):
    centered = summed - jnp.mean(summed, axis=-1, keepdims=True)
    spread = jnp.mean(centered * centered, axis=-1, keepdims=True)
    normed = centered * lax.rsqrt(spread + 1e-06)
    return (normed * (1.0 + modulation[1:2]) + modulation[0:1]).astype(jnp.bfloat16)


def across(a, b):
    return lax.dot_general(a, b, (((1,), (1,)), ((), ())), preferred_element_type=jnp.float32)


def kernel(
    slabs,
    slab,
    cores,
    text_len,
    guidance_scale,
    sigma_table,
    step_index,
    main_hidden,
    main_query,
    text_key,
    text_value,
    guide_hidden,
    guide_query,
    guide_key,
    guide_value,
    guide_out,
    main_head,
    guide_head,
    main_modulation,
    guide_modulation,
    plain,
    guided,
    change,
    tk,
    tv,
    tq,
    to,
    att,
    hq,
    ho,
    gk,
    gv,
    gq,
    gacc,
    gml,
    racc,
    rml,
    v_hidden,
    v_ghidden,
    v_gout,
    v_mhead,
    v_ghead,
    v_mmod,
    v_gmod,
    v_shaped,
    v_gshaped,
    local_sem,
    load_sem,
    t_send,
    t_recv,
    q_send,
    q_recv,
    g_send,
    g_recv,
    own_send,
    near_recv,
    fwd_send,
    far_recv,
    gc_send,
    gc_recv,
    o_send,
    o_recv,
    p_send,
    p_recv,
    hq_send,
    hq_recv,
    ho_send,
    ho_recv,
):
    me = lax.axis_index("seq")
    z = me // slab
    s = me % slab
    c = s % cores
    rows = main_query.shape[0]
    text_cols = tk.shape[-1]
    guide_cols = gk.shape[-1]
    heads = text_cols // HDIM
    guide_heads = guide_cols // HDIM
    keys = slabs * slab * tk.shape[2]
    guide_keys = slabs * cores * rows
    width = text_cols // 2
    end = jnp.logical_or(z == 0, z == slabs - 1)
    host = jnp.logical_or(z == 1, z == slabs - 2)
    inner = jnp.where(z == 0, 1, slabs - 2) * slab
    outer = jnp.where(z == 1, 0, slabs - 1) * slab
    scale = HDIM ** (-0.5) * math.log2(math.e)

    def cols(ref, index, width):
        return ref.at[:, pl.ds(pl.multiple_of(index * width, 128), width)]

    def remote(src, dst, send, recv, target):
        return pltpu.make_async_remote_copy(
            src_ref=src,
            dst_ref=dst,
            send_sem=send,
            recv_sem=recv,
            device_id={"seq": target},
            device_id_type=pl.DeviceIdType.MESH,
        )

    def peer(j):
        return (s - c + (j // cores) * cores) % slab + (c + j) % cores

    def back(j):
        return (slab // cores - j // cores) % (slab // cores) * cores + (cores - j) % cores

    mine = [
        (cols(text_key, s, text_cols), tk.at[z, s]),
        (cols(text_value, s, text_cols), tv.at[z, s]),
        (cols(main_query, s, text_cols), tq.at[s]),
        (cols(guide_query, c, guide_cols), gq.at[s]),
        (cols(guide_key, c, guide_cols), gk.at[z, c]),
        (cols(guide_value, c, guide_cols), gv.at[z, c]),
    ]
    mine = [pltpu.make_async_copy(a, b, local_sem.at[i]) for i, (a, b) in enumerate(mine)]
    loads = [
        (main_hidden, v_hidden),
        (main_head, v_mhead),
        (main_modulation, v_mmod),
        (guide_out, v_gout),
        (guide_hidden, v_ghidden),
        (guide_head, v_ghead),
        (guide_modulation, v_gmod),
    ]
    loads = [pltpu.make_async_copy(a, b, load_sem.at[i]) for i, (a, b) in enumerate(loads)]
    for copy in mine:
        copy.start()

    barrier = pltpu.get_barrier_semaphore()

    def greet(target):
        pl.semaphore_signal(
            barrier, inc=1, device_id={"seq": target}, device_id_type=pl.DeviceIdType.MESH
        )

    for j in range(1, slab):
        greet(z * slab + peer(j))

    @pl.when(end)
    def _():
        for t in range(slab):
            greet(inner + t)

    @pl.when(host)
    def _():
        for t in range(slab):
            greet(outer + t)

    @pl.when(z > 1)
    def _():
        @pl.when(z < slabs - 1)
        def _():
            greet(me - slab)

    @pl.when(z < slabs - 2)
    def _():
        @pl.when(z > 0)
        def _():
            greet(me + slab)

    greeted = jnp.where(end, slab, 0) + jnp.where(host, slab, 0)
    greeted += jnp.where(jnp.logical_and(z > 1, z < slabs - 1), 1, 0)
    greeted += jnp.where(jnp.logical_and(z < slabs - 2, z > 0), 1, 0)
    pl.semaphore_wait(barrier, slab - 1 + greeted)

    target = (me - slab, me + slab)
    has_target = (z > 0, z < slabs - 1)
    target_end = (z == 1, z == slabs - 2)
    target_takes = tuple(
        jnp.logical_and(has, jnp.logical_not(is_end)) for has, is_end in zip(has_target, target_end)
    )
    sent = []

    def send_if(goes, make):
        @pl.when(goes)
        def _():
            for copy in make():
                copy.start()

        sent.append((goes, make))

    def both_ways(make, group=1):
        for way in range(2):
            goes = has_target[way] if group == 1 else target_takes[way]
            send_if(goes, functools.partial(make, way))

    both = ((text_key, tk), (text_value, tv))
    guide_both = ((guide_key, gk), (guide_value, gv))

    def slab_text(j, kv):
        source, place = both[kv]
        t = peer(j)
        return remote(
            cols(source, t, text_cols),
            place.at[z, s],
            t_send.at[j, kv],
            t_recv.at[back(j), kv],
            z * slab + t,
        )

    def half(place, group):
        return place.at[:, pl.ds(group * width, width)]

    def halves(place, group):
        return place.at[:, :, pl.ds(group * width, width)]

    def chain_own(j, kv, group, way):
        source, place = both[kv]
        t = peer(j)
        if j == 0:
            src = cols(source, s * 2 + group, width)
        else:
            src = half(place.at[z, t], group)
        unit = kv * 2 + group
        return remote(
            src,
            half(place.at[z, t], group),
            own_send.at[way, j, unit],
            near_recv.at[way, j, unit],
            target[way],
        )

    def slab_guide(j, kv):
        source, place = guide_both[kv]
        t = peer(j)
        return remote(
            cols(source, t % cores, guide_cols),
            place.at[z, c],
            g_send.at[j, kv],
            g_recv.at[back(j), kv],
            z * slab + t,
        )

    def slab_query(j, group):
        t = peer(j)
        return remote(
            cols(main_query, t * 2 + group, width),
            half(tq.at[s], group),
            q_send.at[j, group],
            q_recv.at[back(j), group],
            z * slab + t,
        )

    def slab_guide_query(j):
        t = peer(j)
        return remote(
            cols(guide_query, t % cores, guide_cols),
            gq.at[s],
            q_send.at[j, 2],
            q_recv.at[back(j), 2],
            z * slab + t,
        )

    def lend(t):
        return remote(
            cols(main_query, t * 2, width), hq.at[s], hq_send.at[t], hq_recv.at[s], inner + t
        )

    def repay(t):
        at = pl.ds(pl.multiple_of(s * text_cols, 128), width)
        return remote(ho.at[t], att.at[:, at], ho_send.at[t], ho_recv.at[s], outer + t)

    for kv in range(2):
        for j in range(slab - 1, 0, -1):
            slab_text(j, kv).start()
        for group in range(2):
            both_ways(lambda way, kv=kv, group=group: [chain_own(0, kv, group, way)], group)
    for kv in range(2):
        for j in range(1, cores):
            slab_guide(j, kv).start()
    for copy in loads:
        copy.start()

    def arrived(place, sem):
        pltpu.make_async_copy(place, place, sem).wait()

    for kv in range(2):
        place = both[kv][1]
        for j in range(1, slab):
            arrived(place.at[z, peer(j)], t_recv.at[j, kv])
            for group in range(2):
                both_ways(
                    lambda way, kv=kv, j=j, group=group: [chain_own(j, kv, group, way)], group
                )
    send_if(end, lambda: [lend(t) for t in range(slab)])
    for j in range(slab - 1, 0, -1):
        slab_query(j, 1).start()
    others = [j for j in range(slab - 1, 0, -1)]
    send_if(jnp.logical_not(end), lambda: [slab_query(j, 0) for j in others])
    for j in others:
        slab_guide_query(j).start()
    for copy in mine:
        copy.wait()
    for kv in range(2):
        place = guide_both[kv][1]
        for j in range(1, cores):
            arrived(place.at[z, peer(j) % cores], g_recv.at[j, kv])

    def guide_chain(d, kv, way):
        place = guide_both[kv][1]
        from_z = z + d if way == 0 else z - d
        return remote(
            place.at[from_z],
            place.at[from_z],
            gc_send.at[way, d, kv],
            gc_recv.at[way, d, kv],
            target[way],
        )

    both_ways(lambda way: [guide_chain(0, 0, way), guide_chain(0, 1, way)])

    def text_chain(d, kv, group, way):
        from_z = z + d if way == 0 else z - d
        block = halves(both[kv][1].at[from_z], group)
        unit = kv * 2 + group
        return remote(
            block, block, fwd_send.at[way, d, unit], far_recv.at[way, d, unit], target[way]
        )

    def coming(d, way):
        return z + d < slabs if way == 0 else z - d >= 0

    for d in range(1, slabs):
        for kv in range(2):
            place = both[kv][1]
            for way in range(2):
                from_z = z + d if way == 0 else z - d
                for group in range(2):
                    comes = coming(d, way)
                    if group == 0:
                        comes = jnp.logical_and(comes, jnp.logical_not(end))

                    @pl.when(comes)
                    def _(way=way, kv=kv, d=d, group=group, place=place, from_z=from_z):
                        unit = kv * 2 + group
                        if d == 1:
                            for j in range(slab):
                                arrived(
                                    half(place.at[from_z, peer(j)], group),
                                    near_recv.at[way, j, unit],
                                )
                        else:
                            arrived(
                                halves(place.at[from_z], group), far_recv.at[way, d - 1, unit]
                            )

                    if d < slabs - 1:
                        takes = has_target[way] if group == 1 else target_takes[way]
                        send_if(
                            jnp.logical_and(comes, takes),
                            lambda way=way, kv=kv, d=d, group=group: [
                                text_chain(d, kv, group, way)
                            ],
                        )

    def guide_arrived(d, way):
        from_z = z + d if way == 0 else z - d
        for kv in range(2):
            arrived(guide_both[kv][1].at[from_z], gc_recv.at[way, d - 1, kv])

    def pass_guide(d):
        for way in range(2):
            goes = jnp.logical_and(coming(d, way), has_target[way])

            @pl.when(goes)
            def _(way=way):
                guide_arrived(d, way)

            if d < slabs - 1:
                send_if(goes, lambda way=way: [guide_chain(d, kv, way) for kv in range(2)])

    positions = lax.broadcasted_iota(jnp.int32, (1, keys), 1)
    bias = jnp.where(positions < text_len[0], 0.0, -1e30).astype(jnp.float32)

    def weigh(q, k, bias=None):
        scores = across(q, k)
        if bias is not None:
            scores = scores + bias
        peak = jnp.max(scores, axis=-1, keepdims=True)
        weights = jnp.exp2((scores - peak) * scale)
        return peak, weights, jnp.sum(weights, axis=-1, keepdims=True)

    def give(j, group):
        t = peer(j)
        at = pl.ds(pl.multiple_of(s * text_cols + group * width, 128), width)
        return remote(
            half(to.at[t], group),
            att.at[:, at],
            o_send.at[j, group],
            o_recv.at[back(j), group],
            z * slab + t,
        )

    def text_heads(group, queries, results, first):
        def one_head(h, _):
            at = pl.ds(pl.multiple_of(group * width + h * HDIM, 128), HDIM)
            to_at = pl.ds(pl.multiple_of(first + h * HDIM, 128), HDIM)
            k = tk[:, :, :, at].reshape(keys, HDIM)
            v = tv[:, :, :, at].reshape(keys, HDIM)
            q = queries[:, :, to_at].reshape(slab * rows, HDIM)
            _, weights, total = weigh(q, k, bias)
            out = jnp.dot(weights.astype(jnp.bfloat16), v, preferred_element_type=jnp.float32)
            out = (out / total).astype(jnp.bfloat16)
            results[:, :, to_at] = out.reshape(slab, rows, HDIM)
            return 0

        lax.fori_loop(0, heads // 2, one_head, 0)

    @pl.when(host)
    def _():
        for t in range(slab):
            arrived(hq.at[t], hq_recv.at[t])
        text_heads(0, hq, ho, 0)

    send_if(host, lambda: [repay(t) for t in range(slab)])
    for d in range(1, slabs - 2):
        pass_guide(d)

    @pl.when(jnp.logical_not(end))
    def _():
        for j in range(1, slab):
            arrived(half(tq.at[peer(j)], 0), q_recv.at[j, 0])
        text_heads(0, tq, to, 0)

    send_if(jnp.logical_not(end), lambda: [give(j, 0) for j in others])
    for d in range(slabs - 2, slabs - 1):
        pass_guide(d)
    for j in range(1, slab):
        arrived(half(tq.at[peer(j)], 1), q_recv.at[j, 1])
        arrived(gq.at[peer(j)], q_recv.at[j, 2])
    text_heads(1, tq, to, width)
    for j in others:
        give(j, 1).start()
    own_att = [
        pltpu.make_async_copy(half(to.at[s], group), cols(att, s * 2 + group, width), local_sem.at[3 * group])
        for group in range(2)
    ]
    own_att[1].start()

    @pl.when(jnp.logical_not(end))
    def _():
        own_att[0].start()

    for d in range(1, slabs):
        for way in range(2):
            comes = z + d < slabs if way == 0 else z - d >= 0
            last = jnp.logical_and(comes, jnp.logical_not(has_target[way]))

            @pl.when(last)
            def _(way=way, d=d):
                guide_arrived(d, way)

    for h in range(guide_heads):
        at = pl.ds(h * HDIM, HDIM)

        k = gk[:, :, :, at].reshape(guide_keys, HDIM)
        v = gv[:, :, :, at].reshape(guide_keys, HDIM)
        peak, weights, total = weigh(gq[:, :, at].reshape(slab * rows, HDIM), k)
        out = jnp.dot(weights.astype(jnp.bfloat16), v, preferred_element_type=jnp.float32)
        gacc[:, :, at] = out.reshape(slab, rows, HDIM)
        gml[:, :, h : h + 1] = peak.reshape(slab, rows, 1)
        gml[:, :, guide_heads + h : guide_heads + h + 1] = total.reshape(slab, rows, 1)

    def part(j):
        t = peer(j)
        return (
            remote(gacc.at[t], racc.at[s], p_send.at[j, 0], p_recv.at[back(j), 0], z * slab + t),
            remote(gml.at[t], rml.at[s], p_send.at[j, 1], p_recv.at[back(j), 1], z * slab + t),
        )

    for j in range(slab - 1, 0, -1):
        for copy in part(j):
            copy.start()
    own_part = [
        pltpu.make_async_copy(gacc.at[s], racc.at[s], local_sem.at[1]),
        pltpu.make_async_copy(gml.at[s], rml.at[s], local_sem.at[2]),
    ]
    for copy in own_part:
        copy.start()

    for copy in loads:
        copy.wait()
    own_att[1].wait()
    for j in range(1, slab):
        arrived(cols(att, peer(j) * 2 + 1, width), o_recv.at[j, 1])

    @pl.when(jnp.logical_not(end))
    def _():
        own_att[0].wait()
        for j in range(1, slab):
            arrived(cols(att, peer(j) * 2, width), o_recv.at[j, 0])

    @pl.when(end)
    def _():
        for t in range(slab):
            arrived(cols(att, t * 2, width), ho_recv.at[t])

    step = 16

    def main_rows(i, _):
        at = pl.ds(pl.multiple_of(i * step, step), step)
        summed = v_hidden[at, :].astype(jnp.float32) + att[at, :].astype(jnp.float32)
        v_shaped[at, :] = shaped_rows(summed, v_mmod[...])
        return 0

    lax.fori_loop(0, rows // step, main_rows, 0)
    main_velocity = across(v_mhead[...], v_shaped[...])

    for copy in own_part:
        copy.wait()
    for j in range(1, slab):
        arrived(racc.at[peer(j)], p_recv.at[j, 0])
        arrived(rml.at[peer(j)], p_recv.at[j, 1])

    pieces = []
    for core in range(cores):
        members = range(core, slab, cores)
        for h in range(guide_heads):
            peaks = [rml[t, :, h : h + 1] for t in members]
            totals = [rml[t, :, guide_heads + h : guide_heads + h + 1] for t in members]
            peak = functools.reduce(jnp.maximum, peaks)
            factors = [jnp.exp2((p - peak) * scale) for p in peaks]
            total = sum(f * l for f, l in zip(factors, totals))
            summed = sum(
                f * racc[t, :, h * HDIM : (h + 1) * HDIM] for f, t in zip(factors, members)
            )
            pieces.append((summed / total).astype(jnp.bfloat16))
    guide_attended = jnp.concatenate(pieces, axis=-1)
    guide_sum = v_ghidden[...].astype(jnp.float32) + jnp.dot(
        guide_attended, v_gout[...], preferred_element_type=jnp.float32
    )
    v_gshaped[...] = shaped_rows(guide_sum, v_gmod[...])
    guide_velocity = across(v_ghead[...], v_gshaped[...])
    now = step_index[0]
    plain[...] = guide_velocity
    guided[...] = guidance_scale[0] * (main_velocity - guide_velocity)
    change[...] = jnp.full(change.shape, sigma_table[now + 1] - sigma_table[now], jnp.float32)

    for j in range(1, slab):
        for kv in range(2):
            slab_text(j, kv).wait_send()
            if j < cores:
                slab_guide(j, kv).wait_send()
        slab_query(j, 1).wait_send()
        slab_guide_query(j).wait_send()
        give(j, 1).wait_send()
        for copy in part(j):
            copy.wait_send()
    for goes, make in sent:

        @pl.when(goes)
        def _(make=make):
            for copy in make():
                copy.wait_send()


def fused(slabs, slab, cores, *args):
    (
        latent,
        main_hidden,
        main_query,
        text_key,
        text_value,
        text_len,
        guide_hidden,
        guide_query,
        guide_key,
        guide_value,
        guide_out,
        main_head,
        guide_head,
        main_modulation,
        guide_modulation,
        guidance_scale,
        sigma_table,
        step_index,
    ) = args
    main_head, guide_head = main_head.T, guide_head.T
    rows, width = main_query.shape
    text_rows = text_key.shape[0]
    guide_width = guide_query.shape[1]
    text_cols = width // slab
    guide_cols = guide_width // cores
    bf16, f32 = jnp.bfloat16, jnp.float32
    dma = pltpu.SemaphoreType.DMA
    like = lambda x: pltpu.VMEM(x.shape, x.dtype)
    scratch = [
        pltpu.VMEM((slabs, slab, text_rows, text_cols), bf16),
        pltpu.VMEM((slabs, slab, text_rows, text_cols), bf16),
        pltpu.VMEM((slab, rows, text_cols), bf16),
        pltpu.VMEM((slab, rows, text_cols), bf16),
        pltpu.VMEM((rows, width), bf16),
        pltpu.VMEM((slab, rows, text_cols // 2), bf16),
        pltpu.VMEM((slab, rows, text_cols // 2), bf16),
        pltpu.VMEM((slabs, cores, rows, guide_cols), bf16),
        pltpu.VMEM((slabs, cores, rows, guide_cols), bf16),
        pltpu.VMEM((slab, rows, guide_cols), bf16),
        pltpu.VMEM((slab, rows, guide_cols), f32),
        pltpu.VMEM((slab, rows, 128), f32),
        pltpu.VMEM((slab, rows, guide_cols), f32),
        pltpu.VMEM((slab, rows, 128), f32),
        like(main_hidden),
        like(guide_hidden),
        like(guide_out),
        like(main_head),
        like(guide_head),
        like(main_modulation),
        like(guide_modulation),
        pltpu.VMEM(main_hidden.shape, bf16),
        pltpu.VMEM(guide_hidden.shape, bf16),
        dma((6,)),
        dma((7,)),
        dma((slab, 2)),
        dma((slab, 2)),
        dma((slab, 3)),
        dma((slab, 3)),
        dma((cores, 2)),
        dma((cores, 2)),
        dma((2, slab, 4)),
        dma((2, slab, 4)),
        dma((2, slabs, 4)),
        dma((2, slabs, 4)),
        dma((2, slabs, 2)),
        dma((2, slabs, 2)),
        dma((slab, 2)),
        dma((slab, 2)),
        dma((slab, 2)),
        dma((slab, 2)),
        dma((slab,)),
        dma((slab,)),
        dma((slab,)),
        dma((slab,)),
    ]
    keys, guide_keys = slabs * slab * text_rows, slabs * cores * rows
    out = jax.ShapeDtypeStruct(latent.shape[::-1], f32)
    plain, guided, change = pl.pallas_call(
        functools.partial(kernel, slabs, slab, cores),
        out_shape=(out, out, jax.ShapeDtypeStruct((1, rows), f32)),
        in_specs=[pl.BlockSpec(memory_space=pltpu.SMEM)] * 4
        + [pl.BlockSpec(memory_space=pltpu.HBM)] * 13,
        out_specs=[pl.BlockSpec(memory_space=pltpu.VMEM)] * 3,
        scratch_shapes=scratch,
        compiler_params=pltpu.CompilerParams(
            collective_id=0, has_side_effects=True, vmem_limit_bytes=56 * 1024 * 1024
        ),
        cost_estimate=pl.CostEstimate(
            flops=4 * rows * (keys * width + guide_keys * guide_width * slab // cores),
            bytes_accessed=2 * (2 * text_rows + 2 * rows) * width,
            transcendentals=rows * keys * width // HDIM,
        ),
    )(
        text_len,
        guidance_scale,
        sigma_table,
        step_index,
        main_hidden,
        main_query,
        text_key,
        text_value,
        guide_hidden,
        guide_query,
        guide_key,
        guide_value,
        guide_out,
        main_head,
        guide_head,
        main_modulation,
        guide_modulation,
    )
    velocity = plain + guided
    return velocity.T, (latent.T + change * velocity).T


def choose(count, slab, cores, *args):
    rows, width = args[2].shape
    text_rows = args[3].shape[0]
    guide_width = args[7].shape[1]
    fits = (
        slab > 1
        and cores > 1
        and count % slab == 0
        and slab % cores == 0
        and count >= 4 * slab
        and rows % 16 == 0
        and text_rows % 16 == 0
        and width % (2 * slab * HDIM) == 0
        and guide_width % (cores * HDIM) == 0
    )
    if fits:
        return fused(count // slab, slab, cores, *args)
    return per_device(*args)


def solution(mesh):
    placed = (
        P(("parts", "seq"), None),
        P(("parts", "seq"), None),
        P(("parts", "seq"), None),
        P(("parts", "seq"), None),
        P(("parts", "seq"), None),
        P("parts"),
        P(("parts", "seq"), None),
        P(("parts", "seq"), None),
        P(("parts", "seq"), None),
        P(("parts", "seq"), None),
        P(),
        P(),
        P(),
        P("parts", None),
        P("parts", None),
        P("parts"),
        P(),
        P("parts"),
    )
    slab, cores = layout(mesh)
    return jax.shard_map(
        functools.partial(choose, mesh.shape["seq"], slab, cores),
        mesh=mesh,
        in_specs=placed,
        out_specs=(P(("parts", "seq"), None), P(("parts", "seq"), None)),
        check_vma=False,
    )
```

```python
import functools
import math

import jax
import jax.numpy as jnp
from jax import lax
from jax.experimental import pallas as pl
from jax.experimental.pallas import tpu as pltpu
from jax.sharding import PartitionSpec as P

HDIM = 128


def start_state(height, heads, head_size):
    return (
        jnp.full((heads, height), -1e30, jnp.float32),
        jnp.zeros((heads, height), jnp.float32),
        jnp.zeros((heads, height, head_size), jnp.float32),
    )


def fold_step(running, queries, keys, values, heads, valid):
    height = queries.shape[0]
    head_size = queries.shape[1] // heads
    query_heads = queries.reshape(height, heads, head_size)
    key_heads = keys.reshape(keys.shape[0], heads, head_size)
    value_heads = values.reshape(values.shape[0], heads, head_size)
    scores = jnp.einsum(
        "qhd,khd->hqk", query_heads, key_heads, preferred_element_type=jnp.float32
    ) * head_size ** (-0.5)
    if valid is not None:
        scores = jnp.where(valid[None, None, :], scores, -1e30)
    peak_old, totals, accumulated = running
    peak_new = jnp.maximum(peak_old, jnp.max(scores, axis=-1))
    weights = jnp.exp(scores - peak_new[..., None])
    if valid is not None:
        weights = jnp.where(valid[None, None, :], weights, 0.0)
    totals = jnp.sum(weights, axis=-1)
    accumulated = jnp.einsum(
        "hqk,khd->hqd",
        weights.astype(jnp.bfloat16),
        value_heads,
        preferred_element_type=jnp.float32,
    )
    return (peak_new, totals, accumulated)


def finish(running):
    peak, totals, accumulated = running
    result = accumulated / totals[..., None]
    return result.transpose(1, 0, 2).reshape(result.shape[1], -1).astype(jnp.bfloat16)


def head_out(summed, modulation, head_weight):
    centered = summed - jnp.mean(summed, axis=-1, keepdims=True)
    spread = jnp.mean(centered * centered, axis=-1, keepdims=True)
    normed = centered * lax.rsqrt(spread + 1e-06)
    shaped = (normed * (1.0 + modulation[1]) + modulation[0]).astype(jnp.bfloat16)
    return jnp.dot(shaped, head_weight, preferred_element_type=jnp.float32)


def per_device(
    latent,
    main_hidden,
    main_query,
    text_key,
    text_value,
    text_len,
    guide_hidden,
    guide_query,
    guide_key,
    guide_value,
    guide_out,
    main_head,
    guide_head,
    main_modulation,
    guide_modulation,
    guidance_scale,
    sigma_table,
    step_index,
):
    height = main_query.shape[0]
    main_heads = main_head.shape[0] // HDIM
    guide_heads = guide_out.shape[0] // HDIM
    all_text_keys = lax.all_gather(text_key, "seq", axis=0, tiled=True)
    all_text_values = lax.all_gather(text_value, "seq", axis=0, tiled=True)
    positions = jnp.arange(all_text_keys.shape[0], dtype=jnp.int32)
    folded = fold_step(
        start_state(height, main_heads, HDIM),
        main_query,
        all_text_keys,
        all_text_values,
        main_heads,
        positions < text_len[0],
    )
    main_sum = main_hidden.astype(jnp.float32) + finish(folded).astype(jnp.float32)
    main_velocity = head_out(main_sum, main_modulation, main_head)
    all_keys = lax.all_gather(guide_key, "seq", axis=0, tiled=True)
    all_values = lax.all_gather(guide_value, "seq", axis=0, tiled=True)
    folded = fold_step(
        start_state(height, guide_heads, HDIM), guide_query, all_keys, all_values, guide_heads, None
    )
    projected = jnp.dot(finish(folded), guide_out, preferred_element_type=jnp.float32)
    guide_sum = guide_hidden.astype(jnp.float32) + projected
    guide_velocity = head_out(guide_sum, guide_modulation, guide_head)
    velocity = guide_velocity + guidance_scale[0] * (main_velocity - guide_velocity)
    positions = jnp.arange(sigma_table.shape[0], dtype=jnp.int32)
    sigma_now = jnp.sum(jnp.where(positions == step_index[0], sigma_table, 0.0))
    sigma_next = jnp.sum(jnp.where(positions == step_index[0] + 1, sigma_table, 0.0))
    next_latent = latent + (sigma_next - sigma_now) * velocity
    return (velocity, next_latent)


def layout(mesh):
    axis = mesh.axis_names.index("seq")
    devices = mesh.devices
    for other in range(devices.ndim - 1, -1, -1):
        if other != axis:
            devices = devices.take(0, axis=other)
    places = [getattr(device, "coords", None) for device in devices]
    if places[0] is None:
        return 1, 1
    slab = sum(place[2] == places[0][2] for place in places)
    cores = sum(tuple(place) == tuple(places[0]) for place in places)
    return slab, cores


def shaped_rows(summed, modulation):
    centered = summed - jnp.mean(summed, axis=-1, keepdims=True)
    spread = jnp.mean(centered * centered, axis=-1, keepdims=True)
    normed = centered * lax.rsqrt(spread + 1e-06)
    return (normed * (1.0 + modulation[1:2]) + modulation[0:1]).astype(jnp.bfloat16)


def across(a, b):
    return lax.dot_general(a, b, (((1,), (1,)), ((), ())), preferred_element_type=jnp.float32)


def kernel(
    slabs,
    slab,
    cores,
    text_len,
    guidance_scale,
    sigma_table,
    step_index,
    main_hidden,
    main_query,
    text_key,
    text_value,
    guide_hidden,
    guide_query,
    guide_key,
    guide_value,
    guide_out,
    main_head,
    guide_head,
    main_modulation,
    guide_modulation,
    plain,
    guided,
    change,
    tk,
    tv,
    tq,
    to,
    att,
    hq,
    ho,
    tp,
    tl,
    gk,
    gv,
    gq,
    gacc,
    gml,
    racc,
    rml,
    v_hidden,
    v_ghidden,
    v_gout,
    v_mhead,
    v_ghead,
    v_mmod,
    v_gmod,
    v_shaped,
    v_gshaped,
    local_sem,
    load_sem,
    t_send,
    t_recv,
    q_send,
    q_recv,
    g_send,
    g_recv,
    own_send,
    near_recv,
    fwd_send,
    far_recv,
    gc_send,
    gc_recv,
    o_send,
    o_recv,
    p_send,
    p_recv,
    hq_send,
    hq_recv,
    ho_send,
    ho_recv,
):
    me = lax.axis_index("seq")
    z = me // slab
    s = me % slab
    c = s % cores
    rows = main_query.shape[0]
    text_cols = tk.shape[-1]
    guide_cols = gk.shape[-1]
    heads = text_cols // HDIM
    guide_heads = guide_cols // HDIM
    keys = slabs * slab * tk.shape[2]
    guide_keys = slabs * cores * rows
    width = text_cols // 2
    end = jnp.logical_or(z == 0, z == slabs - 1)
    host = jnp.logical_or(z == 1, z == slabs - 2)
    inner = jnp.where(z == 0, 1, slabs - 2) * slab
    outer = jnp.where(z == 1, 0, slabs - 1) * slab
    scale = HDIM ** (-0.5) * math.log2(math.e)

    def cols(ref, index, width):
        return ref.at[:, pl.ds(pl.multiple_of(index * width, 128), width)]

    def remote(src, dst, send, recv, target):
        return pltpu.make_async_remote_copy(
            src_ref=src,
            dst_ref=dst,
            send_sem=send,
            recv_sem=recv,
            device_id={"seq": target},
            device_id_type=pl.DeviceIdType.MESH,
        )

    def peer(j):
        return (s - c + (j // cores) * cores) % slab + (c + j) % cores

    def back(j):
        return (slab // cores - j // cores) % (slab // cores) * cores + (cores - j) % cores

    mine = [
        (cols(text_key, s, text_cols), tk.at[z, s]),
        (cols(text_value, s, text_cols), tv.at[z, s]),
        (cols(main_query, s, text_cols), tq.at[s]),
        (cols(guide_query, c, guide_cols), gq.at[s]),
        (cols(guide_key, c, guide_cols), gk.at[z, c]),
        (cols(guide_value, c, guide_cols), gv.at[z, c]),
    ]
    mine = [pltpu.make_async_copy(a, b, local_sem.at[i]) for i, (a, b) in enumerate(mine)]
    loads = [
        (main_hidden, v_hidden),
        (main_head, v_mhead),
        (main_modulation, v_mmod),
        (guide_out, v_gout),
        (guide_hidden, v_ghidden),
        (guide_head, v_ghead),
        (guide_modulation, v_gmod),
    ]
    loads = [pltpu.make_async_copy(a, b, load_sem.at[i]) for i, (a, b) in enumerate(loads)]
    for copy in mine:
        copy.start()

    barrier = pltpu.get_barrier_semaphore()

    def greet(target):
        pl.semaphore_signal(
            barrier, inc=1, device_id={"seq": target}, device_id_type=pl.DeviceIdType.MESH
        )

    for j in range(1, slab):
        greet(z * slab + peer(j))

    @pl.when(end)
    def _():
        for t in range(slab):
            greet(inner + t)

    @pl.when(host)
    def _():
        for t in range(slab):
            greet(outer + t)

    @pl.when(z > 1)
    def _():
        @pl.when(z < slabs - 1)
        def _():
            greet(me - slab)

    @pl.when(z < slabs - 2)
    def _():
        @pl.when(z > 0)
        def _():
            greet(me + slab)

    greeted = jnp.where(end, slab, 0) + jnp.where(host, slab, 0)
    greeted += jnp.where(jnp.logical_and(z > 1, z < slabs - 1), 1, 0)
    greeted += jnp.where(jnp.logical_and(z < slabs - 2, z > 0), 1, 0)
    pl.semaphore_wait(barrier, slab - 1 + greeted)

    target = (me - slab, me + slab)
    has_target = (z > 0, z < slabs - 1)
    target_end = (z == 1, z == slabs - 2)
    target_takes = tuple(
        jnp.logical_and(has, jnp.logical_not(is_end)) for has, is_end in zip(has_target, target_end)
    )
    sent = []

    def send_if(goes, make):
        @pl.when(goes)
        def _():
            for copy in make():
                copy.start()

        sent.append((goes, make))

    def both_ways(make, group=1):
        for way in range(2):
            goes = has_target[way] if group == 1 else target_takes[way]
            send_if(goes, functools.partial(make, way))

    both = ((text_key, tk), (text_value, tv))
    guide_both = ((guide_key, gk), (guide_value, gv))

    def slab_text(j, kv):
        source, place = both[kv]
        t = peer(j)
        return remote(
            cols(source, t, text_cols),
            place.at[z, s],
            t_send.at[j, kv],
            t_recv.at[back(j), kv],
            z * slab + t,
        )

    def half(place, group):
        return place.at[:, pl.ds(group * width, width)]

    def halves(place, group):
        return place.at[:, :, pl.ds(group * width, width)]

    def chain_own(j, kv, group, way):
        source, place = both[kv]
        t = peer(j)
        if j == 0:
            src = cols(source, s * 2 + group, width)
        else:
            src = half(place.at[z, t], group)
        unit = kv * 2 + group
        return remote(
            src,
            half(place.at[z, t], group),
            own_send.at[way, j, unit],
            near_recv.at[way, j, unit],
            target[way],
        )

    def slab_guide(j, kv):
        source, place = guide_both[kv]
        t = peer(j)
        return remote(
            cols(source, t % cores, guide_cols),
            place.at[z, c],
            g_send.at[j, kv],
            g_recv.at[back(j), kv],
            z * slab + t,
        )

    def slab_query(j, group):
        t = peer(j)
        return remote(
            cols(main_query, t * 2 + group, width),
            half(tq.at[s], group),
            q_send.at[j, group],
            q_recv.at[back(j), group],
            z * slab + t,
        )

    def slab_guide_query(j):
        t = peer(j)
        return remote(
            cols(guide_query, t % cores, guide_cols),
            gq.at[s],
            q_send.at[j, 2],
            q_recv.at[back(j), 2],
            z * slab + t,
        )

    def lend(t):
        return remote(
            cols(main_query, t * 2, width), hq.at[s], hq_send.at[t], hq_recv.at[s], inner + t
        )

    def repay(t):
        at = pl.ds(pl.multiple_of(s * text_cols, 128), width)
        return remote(ho.at[t], att.at[:, at], ho_send.at[t], ho_recv.at[s], outer + t)

    others = [j for j in range(slab - 1, 0, -1)]

    def arrived(place, sem):
        pltpu.make_async_copy(place, place, sem).wait()

    def begin_chain(kv, j):
        for group in range(2):
            both_ways(lambda way, group=group: [chain_own(j, kv, group, way)], group)

    for j in others:
        slab_text(j, 0).start()
    begin_chain(0, 0)
    for kv in range(2):
        for j in range(1, cores):
            slab_guide(j, kv).start()
    for j in range(1, slab):
        arrived(tk.at[z, peer(j)], t_recv.at[j, 0])
        begin_chain(0, j)
    send_if(end, lambda: [lend(t) for t in range(slab)])
    for j in others:
        slab_query(j, 1).start()
    send_if(jnp.logical_not(end), lambda: [slab_query(j, 0) for j in others])
    for j in others:
        slab_guide_query(j).start()
    for j in others:
        slab_text(j, 1).start()
    for copy in loads:
        copy.start()
    for copy in mine:
        copy.wait()
    for kv in range(2):
        place = guide_both[kv][1]
        for j in range(1, cores):
            arrived(place.at[z, peer(j) % cores], g_recv.at[j, kv])

    def guide_chain(d, kv, way):
        place = guide_both[kv][1]
        from_z = z + d if way == 0 else z - d
        return remote(
            place.at[from_z],
            place.at[from_z],
            gc_send.at[way, d, kv],
            gc_recv.at[way, d, kv],
            target[way],
        )

    def begin_guide(d):
        for way in range(2):
            turn = z + d == slabs - 1 if way == 0 else z == d
            send_if(
                jnp.logical_and(turn, has_target[way]),
                lambda way=way: [guide_chain(0, 0, way), guide_chain(0, 1, way)],
            )

    def text_chain(d, kv, group, way):
        from_z = z + d if way == 0 else z - d
        block = halves(both[kv][1].at[from_z], group)
        unit = kv * 2 + group
        return remote(
            block, block, fwd_send.at[way, d, unit], far_recv.at[way, d, unit], target[way]
        )

    def coming(d, way):
        return z + d < slabs if way == 0 else z - d >= 0

    def pass_text(d, kv):
        place = both[kv][1]
        for way in range(2):
            from_z = z + d if way == 0 else z - d
            for group in range(2):
                comes = coming(d, way)
                if group == 0:
                    comes = jnp.logical_and(comes, jnp.logical_not(end))
                unit = kv * 2 + group

                @pl.when(comes)
                def _(way=way, group=group, unit=unit, from_z=from_z):
                    if d == 1:
                        for j in range(slab):
                            arrived(
                                half(place.at[from_z, peer(j)], group), near_recv.at[way, j, unit]
                            )
                    else:
                        arrived(halves(place.at[from_z], group), far_recv.at[way, d - 1, unit])

                if d < slabs - 1:
                    takes = has_target[way] if group == 1 else target_takes[way]
                    send_if(
                        jnp.logical_and(comes, takes),
                        lambda way=way, group=group: [text_chain(d, kv, group, way)],
                    )

    begin_guide(0)
    for d in range(1, slabs):
        pass_text(d, 0)
        if d < slabs - 1:
            begin_guide(d)

    def guide_arrived(d, way):
        from_z = z + d if way == 0 else z - d
        for kv in range(2):
            arrived(guide_both[kv][1].at[from_z], gc_recv.at[way, d - 1, kv])

    def pass_guide(d):
        for way in range(2):
            goes = jnp.logical_and(coming(d, way), has_target[way])

            @pl.when(goes)
            def _(way=way):
                guide_arrived(d, way)

            if d < slabs - 1:
                send_if(goes, lambda way=way: [guide_chain(d, kv, way) for kv in range(2)])

    positions = lax.broadcasted_iota(jnp.int32, (1, keys), 1)
    bias = jnp.where(positions < text_len[0], 0.0, -1e30).astype(jnp.float32)

    def weigh(q, k, bias=None):
        scores = across(q, k)
        if bias is not None:
            scores = scores + bias
        peak = jnp.max(scores, axis=-1, keepdims=True)
        weights = jnp.exp2((scores - peak) * scale)
        return peak, weights, jnp.sum(weights, axis=-1, keepdims=True)

    def give(j, group):
        t = peer(j)
        at = pl.ds(pl.multiple_of(s * text_cols + group * width, 128), width)
        return remote(
            half(to.at[t], group),
            att.at[:, at],
            o_send.at[j, group],
            o_recv.at[back(j), group],
            z * slab + t,
        )

    def text_weights(group, queries, first, slot):
        def one_head(h, _):
            at = pl.ds(pl.multiple_of(group * width + h * HDIM, 128), HDIM)
            q_at = pl.ds(pl.multiple_of(first + h * HDIM, 128), HDIM)
            k = tk[:, :, :, at].reshape(keys, HDIM)
            q = queries[:, :, q_at].reshape(slab * rows, HDIM)
            _, weights, total = weigh(q, k, bias)
            tp[slot + h] = weights.astype(jnp.bfloat16)
            tl[slot + h] = total
            return 0

        lax.fori_loop(0, heads // 2, one_head, 0)

    def text_values(group, results, first, slot):
        def one_head(h, _):
            at = pl.ds(pl.multiple_of(group * width + h * HDIM, 128), HDIM)
            to_at = pl.ds(pl.multiple_of(first + h * HDIM, 128), HDIM)
            v = tv[:, :, :, at].reshape(keys, HDIM)
            out = jnp.dot(tp[slot + h], v, preferred_element_type=jnp.float32)
            out = (out / tl[slot + h]).astype(jnp.bfloat16)
            results[:, :, to_at] = out.reshape(slab, rows, HDIM)
            return 0

        lax.fori_loop(0, heads // 2, one_head, 0)

    @pl.when(host)
    def _():
        for t in range(slab):
            arrived(hq.at[t], hq_recv.at[t])
        text_weights(0, hq, 0, heads)

    for d in range(1, slabs - 2):
        pass_guide(d)

    @pl.when(jnp.logical_not(end))
    def _():
        for j in range(1, slab):
            arrived(half(tq.at[peer(j)], 0), q_recv.at[j, 0])
        text_weights(0, tq, 0, 0)

    for d in range(slabs - 2, slabs - 1):
        pass_guide(d)
    begin_chain(1, 0)
    for j in range(1, slab):
        arrived(tv.at[z, peer(j)], t_recv.at[j, 1])
        begin_chain(1, j)
    for j in range(1, slab):
        arrived(half(tq.at[peer(j)], 1), q_recv.at[j, 1])
        arrived(gq.at[peer(j)], q_recv.at[j, 2])
    text_weights(1, tq, width, heads // 2)

    for d in range(1, slabs):
        for way in range(2):
            comes = z + d < slabs if way == 0 else z - d >= 0
            last = jnp.logical_and(comes, jnp.logical_not(has_target[way]))

            @pl.when(last)
            def _(way=way, d=d):
                guide_arrived(d, way)

    for h in range(guide_heads):
        at = pl.ds(h * HDIM, HDIM)

        k = gk[:, :, :, at].reshape(guide_keys, HDIM)
        v = gv[:, :, :, at].reshape(guide_keys, HDIM)
        peak, weights, total = weigh(gq[:, :, at].reshape(slab * rows, HDIM), k)
        out = jnp.dot(weights.astype(jnp.bfloat16), v, preferred_element_type=jnp.float32)
        gacc[:, :, at] = out.reshape(slab, rows, HDIM)
        gml[:, :, h : h + 1] = peak.reshape(slab, rows, 1)
        gml[:, :, guide_heads + h : guide_heads + h + 1] = total.reshape(slab, rows, 1)

    def part(j):
        t = peer(j)
        return (
            remote(gacc.at[t], racc.at[s], p_send.at[j, 0], p_recv.at[back(j), 0], z * slab + t),
            remote(gml.at[t], rml.at[s], p_send.at[j, 1], p_recv.at[back(j), 1], z * slab + t),
        )

    for j in range(slab - 1, 0, -1):
        for copy in part(j):
            copy.start()
    own_part = [
        pltpu.make_async_copy(gacc.at[s], racc.at[s], local_sem.at[1]),
        pltpu.make_async_copy(gml.at[s], rml.at[s], local_sem.at[2]),
    ]
    for copy in own_part:
        copy.start()

    for d in range(1, slabs):
        pass_text(d, 1)

    @pl.when(host)
    def _():
        text_values(0, ho, 0, heads)

    send_if(host, lambda: [repay(t) for t in range(slab)])

    @pl.when(jnp.logical_not(end))
    def _():
        text_values(0, to, 0, 0)

    send_if(jnp.logical_not(end), lambda: [give(j, 0) for j in others])
    text_values(1, to, width, heads // 2)
    for j in others:
        give(j, 1).start()
    own_att = [
        pltpu.make_async_copy(half(to.at[s], group), cols(att, s * 2 + group, width), local_sem.at[3 * group])
        for group in range(2)
    ]
    own_att[1].start()

    @pl.when(jnp.logical_not(end))
    def _():
        own_att[0].start()

    for copy in loads:
        copy.wait()
    for copy in own_part:
        copy.wait()
    for j in range(1, slab):
        arrived(racc.at[peer(j)], p_recv.at[j, 0])
        arrived(rml.at[peer(j)], p_recv.at[j, 1])

    pieces = []
    for core in range(cores):
        members = range(core, slab, cores)
        for h in range(guide_heads):
            peaks = [rml[t, :, h : h + 1] for t in members]
            totals = [rml[t, :, guide_heads + h : guide_heads + h + 1] for t in members]
            peak = functools.reduce(jnp.maximum, peaks)
            factors = [jnp.exp2((p - peak) * scale) for p in peaks]
            total = sum(f * l for f, l in zip(factors, totals))
            summed = sum(
                f * racc[t, :, h * HDIM : (h + 1) * HDIM] for f, t in zip(factors, members)
            )
            pieces.append((summed / total).astype(jnp.bfloat16))
    guide_attended = jnp.concatenate(pieces, axis=-1)
    guide_sum = v_ghidden[...].astype(jnp.float32) + jnp.dot(
        guide_attended, v_gout[...], preferred_element_type=jnp.float32
    )
    v_gshaped[...] = shaped_rows(guide_sum, v_gmod[...])
    guide_velocity = across(v_ghead[...], v_gshaped[...])
    own_att[1].wait()
    for j in range(1, slab):
        arrived(cols(att, peer(j) * 2 + 1, width), o_recv.at[j, 1])

    @pl.when(jnp.logical_not(end))
    def _():
        own_att[0].wait()
        for j in range(1, slab):
            arrived(cols(att, peer(j) * 2, width), o_recv.at[j, 0])

    @pl.when(end)
    def _():
        for t in range(slab):
            arrived(cols(att, t * 2, width), ho_recv.at[t])

    step = 16

    def main_rows(i, _):
        at = pl.ds(pl.multiple_of(i * step, step), step)
        summed = v_hidden[at, :].astype(jnp.float32) + att[at, :].astype(jnp.float32)
        v_shaped[at, :] = shaped_rows(summed, v_mmod[...])
        return 0

    lax.fori_loop(0, rows // step, main_rows, 0)
    main_velocity = across(v_mhead[...], v_shaped[...])

    now = step_index[0]
    plain[...] = guide_velocity
    guided[...] = guidance_scale[0] * (main_velocity - guide_velocity)
    change[...] = jnp.full(change.shape, sigma_table[now + 1] - sigma_table[now], jnp.float32)

    for j in range(1, slab):
        for kv in range(2):
            slab_text(j, kv).wait_send()
            if j < cores:
                slab_guide(j, kv).wait_send()
        slab_query(j, 1).wait_send()
        slab_guide_query(j).wait_send()
        give(j, 1).wait_send()
        for copy in part(j):
            copy.wait_send()
    for goes, make in sent:

        @pl.when(goes)
        def _(make=make):
            for copy in make():
                copy.wait_send()


def fused(slabs, slab, cores, *args):
    (
        latent,
        main_hidden,
        main_query,
        text_key,
        text_value,
        text_len,
        guide_hidden,
        guide_query,
        guide_key,
        guide_value,
        guide_out,
        main_head,
        guide_head,
        main_modulation,
        guide_modulation,
        guidance_scale,
        sigma_table,
        step_index,
    ) = args
    main_head, guide_head = main_head.T, guide_head.T
    rows, width = main_query.shape
    text_rows = text_key.shape[0]
    guide_width = guide_query.shape[1]
    text_cols = width // slab
    guide_cols = guide_width // cores
    bf16, f32 = jnp.bfloat16, jnp.float32
    dma = pltpu.SemaphoreType.DMA
    like = lambda x: pltpu.VMEM(x.shape, x.dtype)
    scratch = [
        pltpu.VMEM((slabs, slab, text_rows, text_cols), bf16),
        pltpu.VMEM((slabs, slab, text_rows, text_cols), bf16),
        pltpu.VMEM((slab, rows, text_cols), bf16),
        pltpu.VMEM((slab, rows, text_cols), bf16),
        pltpu.VMEM((rows, width), bf16),
        pltpu.VMEM((slab, rows, text_cols // 2), bf16),
        pltpu.VMEM((slab, rows, text_cols // 2), bf16),
        pltpu.VMEM((3 * text_cols // 2 // HDIM, slab * rows, slabs * slab * text_rows), bf16),
        pltpu.VMEM((3 * text_cols // 2 // HDIM, slab * rows, 1), f32),
        pltpu.VMEM((slabs, cores, rows, guide_cols), bf16),
        pltpu.VMEM((slabs, cores, rows, guide_cols), bf16),
        pltpu.VMEM((slab, rows, guide_cols), bf16),
        pltpu.VMEM((slab, rows, guide_cols), f32),
        pltpu.VMEM((slab, rows, 128), f32),
        pltpu.VMEM((slab, rows, guide_cols), f32),
        pltpu.VMEM((slab, rows, 128), f32),
        like(main_hidden),
        like(guide_hidden),
        like(guide_out),
        like(main_head),
        like(guide_head),
        like(main_modulation),
        like(guide_modulation),
        pltpu.VMEM(main_hidden.shape, bf16),
        pltpu.VMEM(guide_hidden.shape, bf16),
        dma((6,)),
        dma((7,)),
        dma((slab, 2)),
        dma((slab, 2)),
        dma((slab, 3)),
        dma((slab, 3)),
        dma((cores, 2)),
        dma((cores, 2)),
        dma((2, slab, 4)),
        dma((2, slab, 4)),
        dma((2, slabs, 4)),
        dma((2, slabs, 4)),
        dma((2, slabs, 2)),
        dma((2, slabs, 2)),
        dma((slab, 2)),
        dma((slab, 2)),
        dma((slab, 2)),
        dma((slab, 2)),
        dma((slab,)),
        dma((slab,)),
        dma((slab,)),
        dma((slab,)),
    ]
    keys, guide_keys = slabs * slab * text_rows, slabs * cores * rows
    out = jax.ShapeDtypeStruct(latent.shape[::-1], f32)
    plain, guided, change = pl.pallas_call(
        functools.partial(kernel, slabs, slab, cores),
        out_shape=(out, out, jax.ShapeDtypeStruct((1, rows), f32)),
        in_specs=[pl.BlockSpec(memory_space=pltpu.SMEM)] * 4
        + [pl.BlockSpec(memory_space=pltpu.HBM)] * 13,
        out_specs=[pl.BlockSpec(memory_space=pltpu.VMEM)] * 3,
        scratch_shapes=scratch,
        compiler_params=pltpu.CompilerParams(
            collective_id=0, has_side_effects=True, vmem_limit_bytes=56 * 1024 * 1024
        ),
        cost_estimate=pl.CostEstimate(
            flops=4 * rows * (keys * width + guide_keys * guide_width * slab // cores),
            bytes_accessed=2 * (2 * text_rows + 2 * rows) * width,
            transcendentals=rows * keys * width // HDIM,
        ),
    )(
        text_len,
        guidance_scale,
        sigma_table,
        step_index,
        main_hidden,
        main_query,
        text_key,
        text_value,
        guide_hidden,
        guide_query,
        guide_key,
        guide_value,
        guide_out,
        main_head,
        guide_head,
        main_modulation,
        guide_modulation,
    )
    velocity = plain + guided
    return velocity.T, (latent.T + change * velocity).T


def choose(count, slab, cores, *args):
    rows, width = args[2].shape
    text_rows = args[3].shape[0]
    guide_width = args[7].shape[1]
    fits = (
        slab > 1
        and cores > 1
        and count % slab == 0
        and slab % cores == 0
        and count >= 4 * slab
        and rows % 16 == 0
        and text_rows % 16 == 0
        and width % (2 * slab * HDIM) == 0
        and guide_width % (cores * HDIM) == 0
    )
    if fits:
        return fused(count // slab, slab, cores, *args)
    return per_device(*args)


def solution(mesh):
    placed = (
        P(("parts", "seq"), None),
        P(("parts", "seq"), None),
        P(("parts", "seq"), None),
        P(("parts", "seq"), None),
        P(("parts", "seq"), None),
        P("parts"),
        P(("parts", "seq"), None),
        P(("parts", "seq"), None),
        P(("parts", "seq"), None),
        P(("parts", "seq"), None),
        P(),
        P(),
        P(),
        P("parts", None),
        P("parts", None),
        P("parts"),
        P(),
        P("parts"),
    )
    slab, cores = layout(mesh)
    return jax.shard_map(
        functools.partial(choose, mesh.shape["seq"], slab, cores),
        mesh=mesh,
        in_specs=placed,
        out_specs=(P(("parts", "seq"), None), P(("parts", "seq"), None)),
        check_vma=False,
    )
```

```python
import functools
import math

import jax
import jax.numpy as jnp
from jax import lax
from jax.experimental import pallas as pl
from jax.experimental.pallas import tpu as pltpu
from jax.sharding import PartitionSpec as P

HDIM = 128


def start_state(height, heads, head_size):
    return (
        jnp.full((heads, height), -1e30, jnp.float32),
        jnp.zeros((heads, height), jnp.float32),
        jnp.zeros((heads, height, head_size), jnp.float32),
    )


def fold_step(running, queries, keys, values, heads, valid):
    height = queries.shape[0]
    head_size = queries.shape[1] // heads
    query_heads = queries.reshape(height, heads, head_size)
    key_heads = keys.reshape(keys.shape[0], heads, head_size)
    value_heads = values.reshape(values.shape[0], heads, head_size)
    scores = jnp.einsum(
        "qhd,khd->hqk", query_heads, key_heads, preferred_element_type=jnp.float32
    ) * head_size ** (-0.5)
    if valid is not None:
        scores = jnp.where(valid[None, None, :], scores, -1e30)
    peak_old, totals, accumulated = running
    peak_new = jnp.maximum(peak_old, jnp.max(scores, axis=-1))
    weights = jnp.exp(scores - peak_new[..., None])
    if valid is not None:
        weights = jnp.where(valid[None, None, :], weights, 0.0)
    totals = jnp.sum(weights, axis=-1)
    accumulated = jnp.einsum(
        "hqk,khd->hqd",
        weights.astype(jnp.bfloat16),
        value_heads,
        preferred_element_type=jnp.float32,
    )
    return (peak_new, totals, accumulated)


def finish(running):
    peak, totals, accumulated = running
    result = accumulated / totals[..., None]
    return result.transpose(1, 0, 2).reshape(result.shape[1], -1).astype(jnp.bfloat16)


def head_out(summed, modulation, head_weight):
    centered = summed - jnp.mean(summed, axis=-1, keepdims=True)
    spread = jnp.mean(centered * centered, axis=-1, keepdims=True)
    normed = centered * lax.rsqrt(spread + 1e-06)
    shaped = (normed * (1.0 + modulation[1]) + modulation[0]).astype(jnp.bfloat16)
    return jnp.dot(shaped, head_weight, preferred_element_type=jnp.float32)


def per_device(
    latent,
    main_hidden,
    main_query,
    text_key,
    text_value,
    text_len,
    guide_hidden,
    guide_query,
    guide_key,
    guide_value,
    guide_out,
    main_head,
    guide_head,
    main_modulation,
    guide_modulation,
    guidance_scale,
    sigma_table,
    step_index,
):
    height = main_query.shape[0]
    main_heads = main_head.shape[0] // HDIM
    guide_heads = guide_out.shape[0] // HDIM
    all_text_keys = lax.all_gather(text_key, "seq", axis=0, tiled=True)
    all_text_values = lax.all_gather(text_value, "seq", axis=0, tiled=True)
    positions = jnp.arange(all_text_keys.shape[0], dtype=jnp.int32)
    folded = fold_step(
        start_state(height, main_heads, HDIM),
        main_query,
        all_text_keys,
        all_text_values,
        main_heads,
        positions < text_len[0],
    )
    main_sum = main_hidden.astype(jnp.float32) + finish(folded).astype(jnp.float32)
    main_velocity = head_out(main_sum, main_modulation, main_head)
    all_keys = lax.all_gather(guide_key, "seq", axis=0, tiled=True)
    all_values = lax.all_gather(guide_value, "seq", axis=0, tiled=True)
    folded = fold_step(
        start_state(height, guide_heads, HDIM), guide_query, all_keys, all_values, guide_heads, None
    )
    projected = jnp.dot(finish(folded), guide_out, preferred_element_type=jnp.float32)
    guide_sum = guide_hidden.astype(jnp.float32) + projected
    guide_velocity = head_out(guide_sum, guide_modulation, guide_head)
    velocity = guide_velocity + guidance_scale[0] * (main_velocity - guide_velocity)
    positions = jnp.arange(sigma_table.shape[0], dtype=jnp.int32)
    sigma_now = jnp.sum(jnp.where(positions == step_index[0], sigma_table, 0.0))
    sigma_next = jnp.sum(jnp.where(positions == step_index[0] + 1, sigma_table, 0.0))
    next_latent = latent + (sigma_next - sigma_now) * velocity
    return (velocity, next_latent)


def layout(mesh):
    axis = mesh.axis_names.index("seq")
    devices = mesh.devices
    for other in range(devices.ndim - 1, -1, -1):
        if other != axis:
            devices = devices.take(0, axis=other)
    places = [getattr(device, "coords", None) for device in devices]
    if places[0] is None:
        return 1, 1
    slab = sum(place[2] == places[0][2] for place in places)
    cores = sum(tuple(place) == tuple(places[0]) for place in places)
    return slab, cores


def shaped_rows(summed, modulation):
    centered = summed - jnp.mean(summed, axis=-1, keepdims=True)
    spread = jnp.mean(centered * centered, axis=-1, keepdims=True)
    normed = centered * lax.rsqrt(spread + 1e-06)
    return (normed * (1.0 + modulation[1:2]) + modulation[0:1]).astype(jnp.bfloat16)


def across(a, b):
    return lax.dot_general(a, b, (((1,), (1,)), ((), ())), preferred_element_type=jnp.float32)


def kernel(
    slabs,
    slab,
    cores,
    text_len,
    guidance_scale,
    sigma_table,
    step_index,
    main_hidden,
    main_query,
    text_key,
    text_value,
    guide_hidden,
    guide_query,
    guide_key,
    guide_value,
    guide_out,
    main_head,
    guide_head,
    main_modulation,
    guide_modulation,
    plain,
    guided,
    change,
    tk,
    tv,
    tq,
    to,
    att,
    hq,
    ho,
    tp,
    tl,
    gk,
    gv,
    gq,
    gacc,
    gml,
    racc,
    rml,
    v_hidden,
    v_ghidden,
    v_gout,
    v_mhead,
    v_ghead,
    v_mmod,
    v_gmod,
    v_shaped,
    v_gshaped,
    local_sem,
    load_sem,
    t_send,
    t_recv,
    q_send,
    q_recv,
    g_send,
    g_recv,
    own_send,
    near_recv,
    fwd_send,
    far_recv,
    gc_send,
    gc_recv,
    o_send,
    o_recv,
    p_send,
    p_recv,
    hq_send,
    hq_recv,
    ho_send,
    ho_recv,
):
    me = lax.axis_index("seq")
    z = me // slab
    s = me % slab
    c = s % cores
    rows = main_query.shape[0]
    text_cols = tk.shape[-1]
    guide_cols = gk.shape[-1]
    heads = text_cols // HDIM
    guide_heads = guide_cols // HDIM
    keys = slabs * slab * tk.shape[2]
    guide_keys = slabs * cores * rows
    width = text_cols // 2
    end = jnp.logical_or(z == 0, z == slabs - 1)
    host = jnp.logical_or(z == 1, z == slabs - 2)
    inner = jnp.where(z == 0, 1, slabs - 2) * slab
    outer = jnp.where(z == 1, 0, slabs - 1) * slab
    scale = HDIM ** (-0.5) * math.log2(math.e)

    def cols(ref, index, width):
        return ref.at[:, pl.ds(pl.multiple_of(index * width, 128), width)]

    def remote(src, dst, send, recv, target):
        return pltpu.make_async_remote_copy(
            src_ref=src,
            dst_ref=dst,
            send_sem=send,
            recv_sem=recv,
            device_id={"seq": target},
            device_id_type=pl.DeviceIdType.MESH,
        )

    def peer(j):
        return (s - c + (j // cores) * cores) % slab + (c + j) % cores

    def back(j):
        return (slab // cores - j // cores) % (slab // cores) * cores + (cores - j) % cores

    mine = [
        (cols(text_key, s, text_cols), tk.at[z, s]),
        (cols(text_value, s, text_cols), tv.at[z, s]),
        (cols(main_query, s, text_cols), tq.at[s]),
        (cols(guide_query, c, guide_cols), gq.at[s]),
        (cols(guide_key, c, guide_cols), gk.at[z, c]),
        (cols(guide_value, c, guide_cols), gv.at[z, c]),
    ]
    mine = [pltpu.make_async_copy(a, b, local_sem.at[i]) for i, (a, b) in enumerate(mine)]
    loads = [
        (main_hidden, v_hidden),
        (main_head, v_mhead),
        (main_modulation, v_mmod),
        (guide_out, v_gout),
        (guide_hidden, v_ghidden),
        (guide_head, v_ghead),
        (guide_modulation, v_gmod),
    ]
    loads = [pltpu.make_async_copy(a, b, load_sem.at[i]) for i, (a, b) in enumerate(loads)]
    for copy in mine:
        copy.start()

    barrier = pltpu.get_barrier_semaphore()

    def greet(target):
        pl.semaphore_signal(
            barrier, inc=1, device_id={"seq": target}, device_id_type=pl.DeviceIdType.MESH
        )

    for j in range(1, slab):
        greet(z * slab + peer(j))

    @pl.when(end)
    def _():
        for t in range(slab):
            greet(inner + t)

    @pl.when(host)
    def _():
        for t in range(slab):
            greet(outer + t)

    @pl.when(z > 1)
    def _():
        @pl.when(z < slabs - 1)
        def _():
            greet(me - slab)

    @pl.when(z < slabs - 2)
    def _():
        @pl.when(z > 0)
        def _():
            greet(me + slab)

    greeted = jnp.where(end, slab, 0) + jnp.where(host, slab, 0)
    greeted += jnp.where(jnp.logical_and(z > 1, z < slabs - 1), 1, 0)
    greeted += jnp.where(jnp.logical_and(z < slabs - 2, z > 0), 1, 0)
    pl.semaphore_wait(barrier, slab - 1 + greeted)

    target = (me - slab, me + slab)
    has_target = (z > 0, z < slabs - 1)
    target_end = (z == 1, z == slabs - 2)
    target_takes = tuple(
        jnp.logical_and(has, jnp.logical_not(is_end)) for has, is_end in zip(has_target, target_end)
    )
    sent = []

    def send_if(goes, make):
        @pl.when(goes)
        def _():
            for copy in make():
                copy.start()

        sent.append((goes, make))

    def both_ways(make, group=1):
        for way in range(2):
            goes = has_target[way] if group == 1 else target_takes[way]
            send_if(goes, functools.partial(make, way))

    both = ((text_key, tk), (text_value, tv))
    guide_both = ((guide_key, gk), (guide_value, gv))

    def slab_text(j, kv):
        source, place = both[kv]
        t = peer(j)
        return remote(
            cols(source, t, text_cols),
            place.at[z, s],
            t_send.at[j, kv],
            t_recv.at[back(j), kv],
            z * slab + t,
        )

    def half(place, group):
        return place.at[:, pl.ds(group * width, width)]

    def halves(place, group):
        return place.at[:, :, pl.ds(group * width, width)]

    def chain_own(j, kv, group, way):
        source, place = both[kv]
        t = peer(j)
        if j == 0:
            src = cols(source, s * 2 + group, width)
        else:
            src = half(place.at[z, t], group)
        unit = kv * 2 + group
        return remote(
            src,
            half(place.at[z, t], group),
            own_send.at[way, j, unit],
            near_recv.at[way, j, unit],
            target[way],
        )

    def slab_guide(j, kv):
        source, place = guide_both[kv]
        t = peer(j)
        return remote(
            cols(source, t % cores, guide_cols),
            place.at[z, c],
            g_send.at[j, kv],
            g_recv.at[back(j), kv],
            z * slab + t,
        )

    def slab_query(j, group):
        t = peer(j)
        return remote(
            cols(main_query, t * 2 + group, width),
            half(tq.at[s], group),
            q_send.at[j, group],
            q_recv.at[back(j), group],
            z * slab + t,
        )

    def slab_guide_query(j):
        t = peer(j)
        return remote(
            cols(guide_query, t % cores, guide_cols),
            gq.at[s],
            q_send.at[j, 2],
            q_recv.at[back(j), 2],
            z * slab + t,
        )

    def lend(t):
        return remote(
            cols(main_query, t * 2, width), hq.at[s], hq_send.at[t], hq_recv.at[s], inner + t
        )

    def repay(t):
        at = pl.ds(pl.multiple_of(s * text_cols, 128), width)
        return remote(ho.at[t], att.at[:, at], ho_send.at[t], ho_recv.at[s], outer + t)

    others = [j for j in range(slab - 1, 0, -1)]

    def arrived(place, sem):
        pltpu.make_async_copy(place, place, sem).wait()

    def begin_chain(kv, j, groups=(0, 1)):
        for group in groups:
            both_ways(lambda way, group=group: [chain_own(j, kv, group, way)], group)

    for j in others:
        slab_text(j, 0).start()
    begin_chain(0, 0)
    for kv in range(2):
        for j in range(1, cores):
            slab_guide(j, kv).start()
    for j in range(1, slab):
        arrived(tk.at[z, peer(j)], t_recv.at[j, 0])
        begin_chain(0, j)
    send_if(end, lambda: [lend(t) for t in range(slab)])
    for j in others:
        slab_text(j, 1).start()
    for j in others:
        slab_query(j, 1).start()
    send_if(jnp.logical_not(end), lambda: [slab_query(j, 0) for j in others])
    for j in others:
        slab_guide_query(j).start()
    for copy in loads:
        copy.start()
    for copy in mine:
        copy.wait()
    for kv in range(2):
        place = guide_both[kv][1]
        for j in range(1, cores):
            arrived(place.at[z, peer(j) % cores], g_recv.at[j, kv])

    def guide_chain(d, kv, way):
        place = guide_both[kv][1]
        from_z = z + d if way == 0 else z - d
        return remote(
            place.at[from_z],
            place.at[from_z],
            gc_send.at[way, d, kv],
            gc_recv.at[way, d, kv],
            target[way],
        )

    def begin_guide(d):
        for way in range(2):
            turn = z + d == slabs - 1 if way == 0 else z == d
            send_if(
                jnp.logical_and(turn, has_target[way]),
                lambda way=way: [guide_chain(0, 0, way), guide_chain(0, 1, way)],
            )

    def text_chain(d, kv, group, way):
        from_z = z + d if way == 0 else z - d
        block = halves(both[kv][1].at[from_z], group)
        unit = kv * 2 + group
        return remote(
            block, block, fwd_send.at[way, d, unit], far_recv.at[way, d, unit], target[way]
        )

    def coming(d, way):
        return z + d < slabs if way == 0 else z - d >= 0

    def pass_text(d, kv, groups=(0, 1)):
        place = both[kv][1]
        for way in range(2):
            from_z = z + d if way == 0 else z - d
            for group in groups:
                comes = coming(d, way)
                if group == 0:
                    comes = jnp.logical_and(comes, jnp.logical_not(end))
                unit = kv * 2 + group

                @pl.when(comes)
                def _(way=way, group=group, unit=unit, from_z=from_z):
                    if d == 1:
                        for j in range(slab):
                            arrived(
                                half(place.at[from_z, peer(j)], group), near_recv.at[way, j, unit]
                            )
                    else:
                        arrived(halves(place.at[from_z], group), far_recv.at[way, d - 1, unit])

                if d < slabs - 1:
                    takes = has_target[way] if group == 1 else target_takes[way]
                    send_if(
                        jnp.logical_and(comes, takes),
                        lambda way=way, group=group: [text_chain(d, kv, group, way)],
                    )

    begin_guide(0)
    for d in range(1, slabs):
        pass_text(d, 0)
        if d < slabs - 1:
            begin_guide(d)

    def guide_arrived(d, way):
        from_z = z + d if way == 0 else z - d
        for kv in range(2):
            arrived(guide_both[kv][1].at[from_z], gc_recv.at[way, d - 1, kv])

    def pass_guide(d):
        for way in range(2):
            goes = jnp.logical_and(coming(d, way), has_target[way])

            @pl.when(goes)
            def _(way=way):
                guide_arrived(d, way)

            if d < slabs - 1:
                send_if(goes, lambda way=way: [guide_chain(d, kv, way) for kv in range(2)])

    positions = lax.broadcasted_iota(jnp.int32, (1, keys), 1)
    bias = jnp.where(positions < text_len[0], 0.0, -1e30).astype(jnp.float32)

    def weigh(q, k, bias=None):
        scores = across(q, k)
        if bias is not None:
            scores = scores + bias
        peak = jnp.max(scores, axis=-1, keepdims=True)
        weights = jnp.exp2((scores - peak) * scale)
        return peak, weights, jnp.sum(weights, axis=-1, keepdims=True)

    def give(j, group):
        t = peer(j)
        at = pl.ds(pl.multiple_of(s * text_cols + group * width, 128), width)
        return remote(
            half(to.at[t], group),
            att.at[:, at],
            o_send.at[j, group],
            o_recv.at[back(j), group],
            z * slab + t,
        )

    def text_weights(group, queries, first, slot):
        def one_head(h, _):
            at = pl.ds(pl.multiple_of(group * width + h * HDIM, 128), HDIM)
            q_at = pl.ds(pl.multiple_of(first + h * HDIM, 128), HDIM)
            k = tk[:, :, :, at].reshape(keys, HDIM)
            q = queries[:, :, q_at].reshape(slab * rows, HDIM)
            _, weights, total = weigh(q, k, bias)
            tp[slot + h] = weights.astype(jnp.bfloat16)
            tl[slot + h] = total
            return 0

        lax.fori_loop(0, heads // 2, one_head, 0)

    def text_values(group, results, first, slot):
        def one_head(h, _):
            at = pl.ds(pl.multiple_of(group * width + h * HDIM, 128), HDIM)
            to_at = pl.ds(pl.multiple_of(first + h * HDIM, 128), HDIM)
            v = tv[:, :, :, at].reshape(keys, HDIM)
            out = jnp.dot(tp[slot + h], v, preferred_element_type=jnp.float32)
            out = (out / tl[slot + h]).astype(jnp.bfloat16)
            results[:, :, to_at] = out.reshape(slab, rows, HDIM)
            return 0

        lax.fori_loop(0, heads // 2, one_head, 0)

    begin_chain(1, 0, (0,))
    for j in range(1, slab):
        arrived(tv.at[z, peer(j)], t_recv.at[j, 1])
        begin_chain(1, j, (0,))

    @pl.when(host)
    def _():
        for t in range(slab):
            arrived(hq.at[t], hq_recv.at[t])
        text_weights(0, hq, 0, heads)

    for d in range(1, slabs - 2):
        pass_guide(d)

    @pl.when(jnp.logical_not(end))
    def _():
        for j in range(1, slab):
            arrived(half(tq.at[peer(j)], 0), q_recv.at[j, 0])
        text_weights(0, tq, 0, 0)

    for d in range(1, slabs - 2):
        pass_text(d, 1, (0,))
    for d in range(slabs - 2, slabs - 1):
        pass_guide(d)
    for j in range(slab):
        begin_chain(1, j, (1,))
    for j in range(1, slab):
        arrived(half(tq.at[peer(j)], 1), q_recv.at[j, 1])
        arrived(gq.at[peer(j)], q_recv.at[j, 2])
    text_weights(1, tq, width, heads // 2)
    for d in range(slabs - 2, slabs):
        pass_text(d, 1, (0,))

    @pl.when(host)
    def _():
        text_values(0, ho, 0, heads)

    send_if(host, lambda: [repay(t) for t in range(slab)])

    @pl.when(jnp.logical_not(end))
    def _():
        text_values(0, to, 0, 0)

    send_if(jnp.logical_not(end), lambda: [give(j, 0) for j in others])
    for d in range(1, slabs - 2):
        pass_text(d, 1, (1,))

    for d in range(1, slabs):
        for way in range(2):
            comes = z + d < slabs if way == 0 else z - d >= 0
            last = jnp.logical_and(comes, jnp.logical_not(has_target[way]))

            @pl.when(last)
            def _(way=way, d=d):
                guide_arrived(d, way)

    for h in range(guide_heads):
        at = pl.ds(h * HDIM, HDIM)

        k = gk[:, :, :, at].reshape(guide_keys, HDIM)
        v = gv[:, :, :, at].reshape(guide_keys, HDIM)
        peak, weights, total = weigh(gq[:, :, at].reshape(slab * rows, HDIM), k)
        out = jnp.dot(weights.astype(jnp.bfloat16), v, preferred_element_type=jnp.float32)
        gacc[:, :, at] = (out / total).astype(jnp.bfloat16).reshape(slab, rows, HDIM)
        gml[:, :, h : h + 1] = peak.reshape(slab, rows, 1)
        gml[:, :, guide_heads + h : guide_heads + h + 1] = total.reshape(slab, rows, 1)

    def part(j):
        t = peer(j)
        return (
            remote(gacc.at[t], racc.at[s], p_send.at[j, 0], p_recv.at[back(j), 0], z * slab + t),
            remote(gml.at[t], rml.at[s], p_send.at[j, 1], p_recv.at[back(j), 1], z * slab + t),
        )

    for j in range(slab - 1, 0, -1):
        for copy in part(j):
            copy.start()
    own_part = [
        pltpu.make_async_copy(gacc.at[s], racc.at[s], local_sem.at[1]),
        pltpu.make_async_copy(gml.at[s], rml.at[s], local_sem.at[2]),
    ]
    for copy in own_part:
        copy.start()

    for d in range(slabs - 2, slabs):
        pass_text(d, 1, (1,))
    text_values(1, to, width, heads // 2)
    for j in others:
        give(j, 1).start()
    own_att = [
        pltpu.make_async_copy(half(to.at[s], group), cols(att, s * 2 + group, width), local_sem.at[3 * group])
        for group in range(2)
    ]
    own_att[1].start()

    @pl.when(jnp.logical_not(end))
    def _():
        own_att[0].start()

    for copy in loads:
        copy.wait()
    for copy in own_part:
        copy.wait()
    for j in range(1, slab):
        arrived(racc.at[peer(j)], p_recv.at[j, 0])
        arrived(rml.at[peer(j)], p_recv.at[j, 1])

    pieces = []
    for core in range(cores):
        members = range(core, slab, cores)
        for h in range(guide_heads):
            peaks = [rml[t, :, h : h + 1] for t in members]
            totals = [rml[t, :, guide_heads + h : guide_heads + h + 1] for t in members]
            peak = functools.reduce(jnp.maximum, peaks)
            factors = [l * jnp.exp2((p - peak) * scale) for p, l in zip(peaks, totals)]
            total = sum(factors)
            summed = sum(
                f * racc[t, :, h * HDIM : (h + 1) * HDIM].astype(jnp.float32) for f, t in zip(factors, members)
            )
            pieces.append((summed / total).astype(jnp.bfloat16))
    guide_attended = jnp.concatenate(pieces, axis=-1)
    guide_sum = v_ghidden[...].astype(jnp.float32) + jnp.dot(
        guide_attended, v_gout[...], preferred_element_type=jnp.float32
    )
    v_gshaped[...] = shaped_rows(guide_sum, v_gmod[...])
    guide_velocity = across(v_ghead[...], v_gshaped[...])
    own_att[1].wait()
    for j in range(1, slab):
        arrived(cols(att, peer(j) * 2 + 1, width), o_recv.at[j, 1])

    @pl.when(jnp.logical_not(end))
    def _():
        own_att[0].wait()
        for j in range(1, slab):
            arrived(cols(att, peer(j) * 2, width), o_recv.at[j, 0])

    @pl.when(end)
    def _():
        for t in range(slab):
            arrived(cols(att, t * 2, width), ho_recv.at[t])

    step = 16

    def main_rows(i, _):
        at = pl.ds(pl.multiple_of(i * step, step), step)
        summed = v_hidden[at, :].astype(jnp.float32) + att[at, :].astype(jnp.float32)
        v_shaped[at, :] = shaped_rows(summed, v_mmod[...])
        return 0

    lax.fori_loop(0, rows // step, main_rows, 0)
    main_velocity = across(v_mhead[...], v_shaped[...])

    now = step_index[0]
    plain[...] = guide_velocity
    guided[...] = guidance_scale[0] * (main_velocity - guide_velocity)
    change[...] = jnp.full(change.shape, sigma_table[now + 1] - sigma_table[now], jnp.float32)

    for j in range(1, slab):
        for kv in range(2):
            slab_text(j, kv).wait_send()
            if j < cores:
                slab_guide(j, kv).wait_send()
        slab_query(j, 1).wait_send()
        slab_guide_query(j).wait_send()
        give(j, 1).wait_send()
        for copy in part(j):
            copy.wait_send()
    for goes, make in sent:

        @pl.when(goes)
        def _(make=make):
            for copy in make():
                copy.wait_send()


def fused(slabs, slab, cores, *args):
    (
        latent,
        main_hidden,
        main_query,
        text_key,
        text_value,
        text_len,
        guide_hidden,
        guide_query,
        guide_key,
        guide_value,
        guide_out,
        main_head,
        guide_head,
        main_modulation,
        guide_modulation,
        guidance_scale,
        sigma_table,
        step_index,
    ) = args
    main_head, guide_head = main_head.T, guide_head.T
    rows, width = main_query.shape
    text_rows = text_key.shape[0]
    guide_width = guide_query.shape[1]
    text_cols = width // slab
    guide_cols = guide_width // cores
    bf16, f32 = jnp.bfloat16, jnp.float32
    dma = pltpu.SemaphoreType.DMA
    like = lambda x: pltpu.VMEM(x.shape, x.dtype)
    scratch = [
        pltpu.VMEM((slabs, slab, text_rows, text_cols), bf16),
        pltpu.VMEM((slabs, slab, text_rows, text_cols), bf16),
        pltpu.VMEM((slab, rows, text_cols), bf16),
        pltpu.VMEM((slab, rows, text_cols), bf16),
        pltpu.VMEM((rows, width), bf16),
        pltpu.VMEM((slab, rows, text_cols // 2), bf16),
        pltpu.VMEM((slab, rows, text_cols // 2), bf16),
        pltpu.VMEM((3 * text_cols // 2 // HDIM, slab * rows, slabs * slab * text_rows), bf16),
        pltpu.VMEM((3 * text_cols // 2 // HDIM, slab * rows, 1), f32),
        pltpu.VMEM((slabs, cores, rows, guide_cols), bf16),
        pltpu.VMEM((slabs, cores, rows, guide_cols), bf16),
        pltpu.VMEM((slab, rows, guide_cols), bf16),
        pltpu.VMEM((slab, rows, guide_cols), bf16),
        pltpu.VMEM((slab, rows, 128), f32),
        pltpu.VMEM((slab, rows, guide_cols), bf16),
        pltpu.VMEM((slab, rows, 128), f32),
        like(main_hidden),
        like(guide_hidden),
        like(guide_out),
        like(main_head),
        like(guide_head),
        like(main_modulation),
        like(guide_modulation),
        pltpu.VMEM(main_hidden.shape, bf16),
        pltpu.VMEM(guide_hidden.shape, bf16),
        dma((6,)),
        dma((7,)),
        dma((slab, 2)),
        dma((slab, 2)),
        dma((slab, 3)),
        dma((slab, 3)),
        dma((cores, 2)),
        dma((cores, 2)),
        dma((2, slab, 4)),
        dma((2, slab, 4)),
        dma((2, slabs, 4)),
        dma((2, slabs, 4)),
        dma((2, slabs, 2)),
        dma((2, slabs, 2)),
        dma((slab, 2)),
        dma((slab, 2)),
        dma((slab, 2)),
        dma((slab, 2)),
        dma((slab,)),
        dma((slab,)),
        dma((slab,)),
        dma((slab,)),
    ]
    keys, guide_keys = slabs * slab * text_rows, slabs * cores * rows
    out = jax.ShapeDtypeStruct(latent.shape[::-1], f32)
    plain, guided, change = pl.pallas_call(
        functools.partial(kernel, slabs, slab, cores),
        out_shape=(out, out, jax.ShapeDtypeStruct((1, rows), f32)),
        in_specs=[pl.BlockSpec(memory_space=pltpu.SMEM)] * 4
        + [pl.BlockSpec(memory_space=pltpu.HBM)] * 13,
        out_specs=[pl.BlockSpec(memory_space=pltpu.VMEM)] * 3,
        scratch_shapes=scratch,
        compiler_params=pltpu.CompilerParams(
            collective_id=0, has_side_effects=True, vmem_limit_bytes=56 * 1024 * 1024
        ),
        cost_estimate=pl.CostEstimate(
            flops=4 * rows * (keys * width + guide_keys * guide_width * slab // cores),
            bytes_accessed=2 * (2 * text_rows + 2 * rows) * width,
            transcendentals=rows * keys * width // HDIM,
        ),
    )(
        text_len,
        guidance_scale,
        sigma_table,
        step_index,
        main_hidden,
        main_query,
        text_key,
        text_value,
        guide_hidden,
        guide_query,
        guide_key,
        guide_value,
        guide_out,
        main_head,
        guide_head,
        main_modulation,
        guide_modulation,
    )
    velocity = plain + guided
    return velocity.T, (latent.T + change * velocity).T


def choose(count, slab, cores, *args):
    rows, width = args[2].shape
    text_rows = args[3].shape[0]
    guide_width = args[7].shape[1]
    fits = (
        slab > 1
        and cores > 1
        and count % slab == 0
        and slab % cores == 0
        and count >= 4 * slab
        and rows % 16 == 0
        and text_rows % 16 == 0
        and width % (2 * slab * HDIM) == 0
        and guide_width % (cores * HDIM) == 0
    )
    if fits:
        return fused(count // slab, slab, cores, *args)
    return per_device(*args)


def solution(mesh):
    placed = (
        P(("parts", "seq"), None),
        P(("parts", "seq"), None),
        P(("parts", "seq"), None),
        P(("parts", "seq"), None),
        P(("parts", "seq"), None),
        P("parts"),
        P(("parts", "seq"), None),
        P(("parts", "seq"), None),
        P(("parts", "seq"), None),
        P(("parts", "seq"), None),
        P(),
        P(),
        P(),
        P("parts", None),
        P("parts", None),
        P("parts"),
        P(),
        P("parts"),
    )
    slab, cores = layout(mesh)
    return jax.shard_map(
        functools.partial(choose, mesh.shape["seq"], slab, cores),
        mesh=mesh,
        in_specs=placed,
        out_specs=(P(("parts", "seq"), None), P(("parts", "seq"), None)),
        check_vma=False,
    )
```

```python
import functools
import math

import jax
import jax.numpy as jnp
from jax import lax
from jax.experimental import pallas as pl
from jax.experimental.pallas import tpu as pltpu
from jax.sharding import PartitionSpec as P

HDIM = 128


def start_state(height, heads, head_size):
    return (
        jnp.full((heads, height), -1e30, jnp.float32),
        jnp.zeros((heads, height), jnp.float32),
        jnp.zeros((heads, height, head_size), jnp.float32),
    )


def fold_step(running, queries, keys, values, heads, valid):
    height = queries.shape[0]
    head_size = queries.shape[1] // heads
    query_heads = queries.reshape(height, heads, head_size)
    key_heads = keys.reshape(keys.shape[0], heads, head_size)
    value_heads = values.reshape(values.shape[0], heads, head_size)
    scores = jnp.einsum(
        "qhd,khd->hqk", query_heads, key_heads, preferred_element_type=jnp.float32
    ) * head_size ** (-0.5)
    if valid is not None:
        scores = jnp.where(valid[None, None, :], scores, -1e30)
    peak_old, totals, accumulated = running
    peak_new = jnp.maximum(peak_old, jnp.max(scores, axis=-1))
    weights = jnp.exp(scores - peak_new[..., None])
    if valid is not None:
        weights = jnp.where(valid[None, None, :], weights, 0.0)
    totals = jnp.sum(weights, axis=-1)
    accumulated = jnp.einsum(
        "hqk,khd->hqd",
        weights.astype(jnp.bfloat16),
        value_heads,
        preferred_element_type=jnp.float32,
    )
    return (peak_new, totals, accumulated)


def finish(running):
    peak, totals, accumulated = running
    result = accumulated / totals[..., None]
    return result.transpose(1, 0, 2).reshape(result.shape[1], -1).astype(jnp.bfloat16)


def head_out(summed, modulation, head_weight):
    centered = summed - jnp.mean(summed, axis=-1, keepdims=True)
    spread = jnp.mean(centered * centered, axis=-1, keepdims=True)
    normed = centered * lax.rsqrt(spread + 1e-06)
    shaped = (normed * (1.0 + modulation[1]) + modulation[0]).astype(jnp.bfloat16)
    return jnp.dot(shaped, head_weight, preferred_element_type=jnp.float32)


def per_device(
    latent,
    main_hidden,
    main_query,
    text_key,
    text_value,
    text_len,
    guide_hidden,
    guide_query,
    guide_key,
    guide_value,
    guide_out,
    main_head,
    guide_head,
    main_modulation,
    guide_modulation,
    guidance_scale,
    sigma_table,
    step_index,
):
    height = main_query.shape[0]
    main_heads = main_head.shape[0] // HDIM
    guide_heads = guide_out.shape[0] // HDIM
    all_text_keys = lax.all_gather(text_key, "seq", axis=0, tiled=True)
    all_text_values = lax.all_gather(text_value, "seq", axis=0, tiled=True)
    positions = jnp.arange(all_text_keys.shape[0], dtype=jnp.int32)
    folded = fold_step(
        start_state(height, main_heads, HDIM),
        main_query,
        all_text_keys,
        all_text_values,
        main_heads,
        positions < text_len[0],
    )
    main_sum = main_hidden.astype(jnp.float32) + finish(folded).astype(jnp.float32)
    main_velocity = head_out(main_sum, main_modulation, main_head)
    all_keys = lax.all_gather(guide_key, "seq", axis=0, tiled=True)
    all_values = lax.all_gather(guide_value, "seq", axis=0, tiled=True)
    folded = fold_step(
        start_state(height, guide_heads, HDIM), guide_query, all_keys, all_values, guide_heads, None
    )
    projected = jnp.dot(finish(folded), guide_out, preferred_element_type=jnp.float32)
    guide_sum = guide_hidden.astype(jnp.float32) + projected
    guide_velocity = head_out(guide_sum, guide_modulation, guide_head)
    velocity = guide_velocity + guidance_scale[0] * (main_velocity - guide_velocity)
    positions = jnp.arange(sigma_table.shape[0], dtype=jnp.int32)
    sigma_now = jnp.sum(jnp.where(positions == step_index[0], sigma_table, 0.0))
    sigma_next = jnp.sum(jnp.where(positions == step_index[0] + 1, sigma_table, 0.0))
    next_latent = latent + (sigma_next - sigma_now) * velocity
    return (velocity, next_latent)


def layout(mesh):
    axis = mesh.axis_names.index("seq")
    devices = mesh.devices
    for other in range(devices.ndim - 1, -1, -1):
        if other != axis:
            devices = devices.take(0, axis=other)
    places = [getattr(device, "coords", None) for device in devices]
    if places[0] is None:
        return 1, 1
    slab = sum(place[2] == places[0][2] for place in places)
    cores = sum(tuple(place) == tuple(places[0]) for place in places)
    return slab, cores


def shaped_rows(summed, modulation):
    centered = summed - jnp.mean(summed, axis=-1, keepdims=True)
    spread = jnp.mean(centered * centered, axis=-1, keepdims=True)
    normed = centered * lax.rsqrt(spread + 1e-06)
    return (normed * (1.0 + modulation[1:2]) + modulation[0:1]).astype(jnp.bfloat16)


def across(a, b):
    return lax.dot_general(a, b, (((1,), (1,)), ((), ())), preferred_element_type=jnp.float32)


def kernel(
    slabs,
    slab,
    cores,
    text_len,
    guidance_scale,
    sigma_table,
    step_index,
    main_hidden,
    main_query,
    text_key,
    text_value,
    guide_hidden,
    guide_query,
    guide_key,
    guide_value,
    guide_out,
    main_head,
    guide_head,
    main_modulation,
    guide_modulation,
    plain,
    guided,
    change,
    tk,
    tv,
    tq,
    to,
    att,
    hq,
    ho,
    tp,
    tl,
    gk,
    gv,
    gq,
    gacc,
    gml,
    racc,
    rml,
    v_hidden,
    v_ghidden,
    v_gout,
    v_mhead,
    v_ghead,
    v_mmod,
    v_gmod,
    v_shaped,
    v_gshaped,
    local_sem,
    load_sem,
    t_send,
    t_recv,
    q_send,
    q_recv,
    g_send,
    g_recv,
    own_send,
    near_recv,
    fwd_send,
    far_recv,
    gc_send,
    gc_recv,
    o_send,
    o_recv,
    p_send,
    p_recv,
    hq_send,
    hq_recv,
    ho_send,
    ho_recv,
):
    me = lax.axis_index("seq")
    z = me // slab
    s = me % slab
    c = s % cores
    rows = main_query.shape[0]
    text_cols = tk.shape[-1]
    guide_cols = gk.shape[-1]
    heads = text_cols // HDIM
    guide_heads = guide_cols // HDIM
    keys = slabs * slab * tk.shape[2]
    guide_keys = slabs * cores * rows
    width = text_cols // 2
    end = jnp.logical_or(z == 0, z == slabs - 1)
    host = jnp.logical_or(z == 1, z == slabs - 2)
    inner = jnp.where(z == 0, 1, slabs - 2) * slab
    outer = jnp.where(z == 1, 0, slabs - 1) * slab
    scale = HDIM ** (-0.5) * math.log2(math.e)

    def cols(ref, index, width):
        return ref.at[:, pl.ds(pl.multiple_of(index * width, 128), width)]

    def remote(src, dst, send, recv, target):
        return pltpu.make_async_remote_copy(
            src_ref=src,
            dst_ref=dst,
            send_sem=send,
            recv_sem=recv,
            device_id={"seq": target},
            device_id_type=pl.DeviceIdType.MESH,
        )

    def peer(j):
        return (s - c + (j // cores) * cores) % slab + (c + j) % cores

    def back(j):
        return (slab // cores - j // cores) % (slab // cores) * cores + (cores - j) % cores

    mine = [
        (cols(text_key, s, text_cols), tk.at[z, s]),
        (cols(text_value, s, text_cols), tv.at[z, s]),
        (cols(main_query, s, text_cols), tq.at[s]),
        (cols(guide_query, c, guide_cols), gq.at[s]),
        (cols(guide_key, c, guide_cols), gk.at[z, c]),
        (cols(guide_value, c, guide_cols), gv.at[z, c]),
    ]
    mine = [pltpu.make_async_copy(a, b, local_sem.at[i]) for i, (a, b) in enumerate(mine)]
    loads = [
        (main_hidden, v_hidden),
        (main_head, v_mhead),
        (main_modulation, v_mmod),
        (guide_out, v_gout),
        (guide_hidden, v_ghidden),
        (guide_head, v_ghead),
        (guide_modulation, v_gmod),
    ]
    loads = [pltpu.make_async_copy(a, b, load_sem.at[i]) for i, (a, b) in enumerate(loads)]
    for copy in mine:
        copy.start()

    barrier = pltpu.get_barrier_semaphore()

    def greet(target):
        pl.semaphore_signal(
            barrier, inc=1, device_id={"seq": target}, device_id_type=pl.DeviceIdType.MESH
        )

    for j in range(1, slab):
        greet(z * slab + peer(j))

    @pl.when(end)
    def _():
        for t in range(slab):
            greet(inner + t)

    @pl.when(host)
    def _():
        for t in range(slab):
            greet(outer + t)

    @pl.when(z > 1)
    def _():
        @pl.when(z < slabs - 1)
        def _():
            greet(me - slab)

    @pl.when(z < slabs - 2)
    def _():
        @pl.when(z > 0)
        def _():
            greet(me + slab)

    greeted = jnp.where(end, slab, 0) + jnp.where(host, slab, 0)
    greeted += jnp.where(jnp.logical_and(z > 1, z < slabs - 1), 1, 0)
    greeted += jnp.where(jnp.logical_and(z < slabs - 2, z > 0), 1, 0)
    pl.semaphore_wait(barrier, slab - 1 + greeted)

    target = (me - slab, me + slab)
    has_target = (z > 0, z < slabs - 1)
    target_end = (z == 1, z == slabs - 2)
    target_takes = tuple(
        jnp.logical_and(has, jnp.logical_not(is_end)) for has, is_end in zip(has_target, target_end)
    )
    sent = []

    def send_if(goes, make):
        @pl.when(goes)
        def _():
            for copy in make():
                copy.start()

        sent.append((goes, make))

    def both_ways(make, group=1):
        for way in range(2):
            goes = has_target[way] if group == 1 else target_takes[way]
            send_if(goes, functools.partial(make, way))

    both = ((text_key, tk), (text_value, tv))
    guide_both = ((guide_key, gk), (guide_value, gv))

    def slab_text(j, kv):
        source, place = both[kv]
        t = peer(j)
        return remote(
            cols(source, t, text_cols),
            place.at[z, s],
            t_send.at[j, kv],
            t_recv.at[back(j), kv],
            z * slab + t,
        )

    def half(place, group):
        return place.at[:, pl.ds(group * width, width)]

    def halves(place, group):
        return place.at[:, :, pl.ds(group * width, width)]

    def chain_own(j, kv, group, way):
        source, place = both[kv]
        t = peer(j)
        if j == 0:
            src = cols(source, s * 2 + group, width)
        else:
            src = half(place.at[z, t], group)
        unit = kv * 2 + group
        return remote(
            src,
            half(place.at[z, t], group),
            own_send.at[way, j, unit],
            near_recv.at[way, j, unit],
            target[way],
        )

    def slab_guide(j, kv):
        source, place = guide_both[kv]
        t = peer(j)
        return remote(
            cols(source, t % cores, guide_cols),
            place.at[z, c],
            g_send.at[j, kv],
            g_recv.at[back(j), kv],
            z * slab + t,
        )

    def slab_query(j, group):
        t = peer(j)
        return remote(
            cols(main_query, t * 2 + group, width),
            half(tq.at[s], group),
            q_send.at[j, group],
            q_recv.at[back(j), group],
            z * slab + t,
        )

    def slab_guide_query(j):
        t = peer(j)
        return remote(
            cols(guide_query, t % cores, guide_cols),
            gq.at[s],
            q_send.at[j, 2],
            q_recv.at[back(j), 2],
            z * slab + t,
        )

    def lend(t):
        return remote(
            cols(main_query, t * 2, width), hq.at[s], hq_send.at[t], hq_recv.at[s], inner + t
        )

    def repay(t):
        at = pl.ds(pl.multiple_of(s * text_cols, 128), width)
        return remote(ho.at[t], att.at[:, at], ho_send.at[t], ho_recv.at[s], outer + t)

    others = [j for j in range(slab - 1, 0, -1)]

    def arrived(place, sem):
        pltpu.make_async_copy(place, place, sem).wait()

    def begin_chain(kv, j, groups=(0, 1)):
        for group in groups:
            both_ways(lambda way, group=group: [chain_own(j, kv, group, way)], group)

    for j in others:
        slab_text(j, 0).start()
    begin_chain(0, 0)
    for kv in range(2):
        for j in range(1, cores):
            slab_guide(j, kv).start()
    for j in range(1, slab):
        arrived(tk.at[z, peer(j)], t_recv.at[j, 0])
        begin_chain(0, j)
    send_if(end, lambda: [lend(t) for t in range(slab)])
    for j in others:
        slab_text(j, 1).start()
    for j in others:
        slab_query(j, 1).start()
    send_if(jnp.logical_not(end), lambda: [slab_query(j, 0) for j in others])
    for j in others:
        slab_guide_query(j).start()
    for copy in loads:
        copy.start()
    for copy in mine:
        copy.wait()
    for kv in range(2):
        place = guide_both[kv][1]
        for j in range(1, cores):
            arrived(place.at[z, peer(j) % cores], g_recv.at[j, kv])

    def guide_chain(d, kv, way):
        place = guide_both[kv][1]
        from_z = z + d if way == 0 else z - d
        return remote(
            place.at[from_z],
            place.at[from_z],
            gc_send.at[way, d, kv],
            gc_recv.at[way, d, kv],
            target[way],
        )

    def begin_guide(d):
        for way in range(2):
            turn = z + d == slabs - 1 if way == 0 else z == d
            send_if(
                jnp.logical_and(turn, has_target[way]),
                lambda way=way: [guide_chain(0, 0, way), guide_chain(0, 1, way)],
            )

    def text_chain(d, kv, group, way):
        from_z = z + d if way == 0 else z - d
        block = halves(both[kv][1].at[from_z], group)
        unit = kv * 2 + group
        return remote(
            block, block, fwd_send.at[way, d, unit], far_recv.at[way, d, unit], target[way]
        )

    def coming(d, way):
        return z + d < slabs if way == 0 else z - d >= 0

    def pass_text(d, kv, groups=(0, 1)):
        place = both[kv][1]
        for way in range(2):
            from_z = z + d if way == 0 else z - d
            for group in groups:
                comes = coming(d, way)
                if group == 0:
                    comes = jnp.logical_and(comes, jnp.logical_not(end))
                unit = kv * 2 + group

                @pl.when(comes)
                def _(way=way, group=group, unit=unit, from_z=from_z):
                    if d == 1:
                        for j in range(slab):
                            arrived(
                                half(place.at[from_z, peer(j)], group), near_recv.at[way, j, unit]
                            )
                    else:
                        arrived(halves(place.at[from_z], group), far_recv.at[way, d - 1, unit])

                if d < slabs - 1:
                    takes = has_target[way] if group == 1 else target_takes[way]
                    send_if(
                        jnp.logical_and(comes, takes),
                        lambda way=way, group=group: [text_chain(d, kv, group, way)],
                    )

    begin_guide(0)
    for d in range(1, slabs):
        pass_text(d, 0)
        if d < slabs - 1:
            begin_guide(d)

    def guide_arrived(d, way):
        from_z = z + d if way == 0 else z - d
        for kv in range(2):
            arrived(guide_both[kv][1].at[from_z], gc_recv.at[way, d - 1, kv])

    def pass_guide(d):
        for way in range(2):
            goes = jnp.logical_and(coming(d, way), has_target[way])

            @pl.when(goes)
            def _(way=way):
                guide_arrived(d, way)

            if d < slabs - 1:
                send_if(goes, lambda way=way: [guide_chain(d, kv, way) for kv in range(2)])

    positions = lax.broadcasted_iota(jnp.int32, (1, keys), 1)
    bias = jnp.where(positions < text_len[0], 0.0, -1e30).astype(jnp.float32)

    def weigh(q, k, bias=None):
        scores = across(q, k)
        if bias is not None:
            scores = scores + bias
        peak = jnp.max(scores, axis=-1, keepdims=True)
        weights = jnp.exp2((scores - peak) * scale)
        return peak, weights, jnp.sum(weights, axis=-1, keepdims=True)

    def give(j, group):
        t = peer(j)
        at = pl.ds(pl.multiple_of(s * text_cols + group * width, 128), width)
        return remote(
            half(to.at[t], group),
            att.at[:, at],
            o_send.at[j, group],
            o_recv.at[back(j), group],
            z * slab + t,
        )

    def text_weights(group, queries, first, slot):
        def one_head(h, _):
            at = pl.ds(pl.multiple_of(group * width + h * HDIM, 128), HDIM)
            q_at = pl.ds(pl.multiple_of(first + h * HDIM, 128), HDIM)
            k = tk[:, :, :, at].reshape(keys, HDIM)
            q = queries[:, :, q_at].reshape(slab * rows, HDIM)
            _, weights, total = weigh(q, k, bias)
            tp[slot + h] = weights.astype(jnp.bfloat16)
            tl[slot + h] = total
            return 0

        lax.fori_loop(0, heads // 2, one_head, 0)

    def text_values(group, results, first, slot):
        def one_head(h, _):
            at = pl.ds(pl.multiple_of(group * width + h * HDIM, 128), HDIM)
            to_at = pl.ds(pl.multiple_of(first + h * HDIM, 128), HDIM)
            v = tv[:, :, :, at].reshape(keys, HDIM)
            out = jnp.dot(tp[slot + h], v, preferred_element_type=jnp.float32)
            out = (out / tl[slot + h]).astype(jnp.bfloat16)
            results[:, :, to_at] = out.reshape(slab, rows, HDIM)
            return 0

        lax.fori_loop(0, heads // 2, one_head, 0)

    begin_chain(1, 0, (0,))
    for j in range(1, slab):
        arrived(tv.at[z, peer(j)], t_recv.at[j, 1])
        begin_chain(1, j, (0,))

    @pl.when(host)
    def _():
        for t in range(slab):
            arrived(hq.at[t], hq_recv.at[t])
        text_weights(0, hq, 0, heads)

    for d in range(1, slabs - 2):
        pass_guide(d)
    for j in range(slab):
        begin_chain(1, j, (1,))

    @pl.when(jnp.logical_not(end))
    def _():
        for j in range(1, slab):
            arrived(half(tq.at[peer(j)], 0), q_recv.at[j, 0])
        text_weights(0, tq, 0, 0)

    for d in range(1, slabs - 2):
        pass_text(d, 1)
    for d in range(slabs - 2, slabs - 1):
        pass_guide(d)
    for j in range(1, slab):
        arrived(half(tq.at[peer(j)], 1), q_recv.at[j, 1])
        arrived(gq.at[peer(j)], q_recv.at[j, 2])
    text_weights(1, tq, width, heads // 2)
    for d in range(1, slabs):
        for way in range(2):
            comes = z + d < slabs if way == 0 else z - d >= 0
            last = jnp.logical_and(comes, jnp.logical_not(has_target[way]))

            @pl.when(last)
            def _(way=way, d=d):
                guide_arrived(d, way)

    for h in range(guide_heads):
        at = pl.ds(h * HDIM, HDIM)

        k = gk[:, :, :, at].reshape(guide_keys, HDIM)
        v = gv[:, :, :, at].reshape(guide_keys, HDIM)
        peak, weights, total = weigh(gq[:, :, at].reshape(slab * rows, HDIM), k)
        out = jnp.dot(weights.astype(jnp.bfloat16), v, preferred_element_type=jnp.float32)
        gacc[:, :, at] = (out / total).astype(jnp.bfloat16).reshape(slab, rows, HDIM)
        gml[:, :, h : h + 1] = peak.reshape(slab, rows, 1)
        gml[:, :, guide_heads + h : guide_heads + h + 1] = total.reshape(slab, rows, 1)

    def part(j):
        t = peer(j)
        return (
            remote(gacc.at[t], racc.at[s], p_send.at[j, 0], p_recv.at[back(j), 0], z * slab + t),
            remote(gml.at[t], rml.at[s], p_send.at[j, 1], p_recv.at[back(j), 1], z * slab + t),
        )

    for j in range(slab - 1, 0, -1):
        for copy in part(j):
            copy.start()
    own_part = [
        pltpu.make_async_copy(gacc.at[s], racc.at[s], local_sem.at[1]),
        pltpu.make_async_copy(gml.at[s], rml.at[s], local_sem.at[2]),
    ]
    for copy in own_part:
        copy.start()

    pass_text(slabs - 2, 1)

    @pl.when(host)
    def _():
        text_values(0, ho, 0, heads)

    send_if(host, lambda: [repay(t) for t in range(slab)])

    @pl.when(jnp.logical_not(end))
    def _():
        text_values(0, to, 0, 0)

    send_if(jnp.logical_not(end), lambda: [give(j, 0) for j in others])
    pass_text(slabs - 1, 1)
    text_values(1, to, width, heads // 2)
    for j in others:
        give(j, 1).start()
    own_att = [
        pltpu.make_async_copy(half(to.at[s], group), cols(att, s * 2 + group, width), local_sem.at[3 * group])
        for group in range(2)
    ]
    own_att[1].start()

    @pl.when(jnp.logical_not(end))
    def _():
        own_att[0].start()

    for copy in loads:
        copy.wait()
    for copy in own_part:
        copy.wait()
    for j in range(1, slab):
        arrived(racc.at[peer(j)], p_recv.at[j, 0])
        arrived(rml.at[peer(j)], p_recv.at[j, 1])

    pieces = []
    for core in range(cores):
        members = range(core, slab, cores)
        for h in range(guide_heads):
            peaks = [rml[t, :, h : h + 1] for t in members]
            totals = [rml[t, :, guide_heads + h : guide_heads + h + 1] for t in members]
            peak = functools.reduce(jnp.maximum, peaks)
            factors = [l * jnp.exp2((p - peak) * scale) for p, l in zip(peaks, totals)]
            total = sum(factors)
            summed = sum(
                f * racc[t, :, h * HDIM : (h + 1) * HDIM].astype(jnp.float32) for f, t in zip(factors, members)
            )
            pieces.append((summed / total).astype(jnp.bfloat16))
    guide_attended = jnp.concatenate(pieces, axis=-1)
    guide_sum = v_ghidden[...].astype(jnp.float32) + jnp.dot(
        guide_attended, v_gout[...], preferred_element_type=jnp.float32
    )
    v_gshaped[...] = shaped_rows(guide_sum, v_gmod[...])
    guide_velocity = across(v_ghead[...], v_gshaped[...])
    own_att[1].wait()
    for j in range(1, slab):
        arrived(cols(att, peer(j) * 2 + 1, width), o_recv.at[j, 1])

    @pl.when(jnp.logical_not(end))
    def _():
        own_att[0].wait()
        for j in range(1, slab):
            arrived(cols(att, peer(j) * 2, width), o_recv.at[j, 0])

    @pl.when(end)
    def _():
        for t in range(slab):
            arrived(cols(att, t * 2, width), ho_recv.at[t])

    step = 16

    def main_rows(i, _):
        at = pl.ds(pl.multiple_of(i * step, step), step)
        summed = v_hidden[at, :].astype(jnp.float32) + att[at, :].astype(jnp.float32)
        v_shaped[at, :] = shaped_rows(summed, v_mmod[...])
        return 0

    lax.fori_loop(0, rows // step, main_rows, 0)
    main_velocity = across(v_mhead[...], v_shaped[...])

    now = step_index[0]
    plain[...] = guide_velocity
    guided[...] = guidance_scale[0] * (main_velocity - guide_velocity)
    change[...] = jnp.full(change.shape, sigma_table[now + 1] - sigma_table[now], jnp.float32)

    for j in range(1, slab):
        for kv in range(2):
            slab_text(j, kv).wait_send()
            if j < cores:
                slab_guide(j, kv).wait_send()
        slab_query(j, 1).wait_send()
        slab_guide_query(j).wait_send()
        give(j, 1).wait_send()
        for copy in part(j):
            copy.wait_send()
    for goes, make in sent:

        @pl.when(goes)
        def _(make=make):
            for copy in make():
                copy.wait_send()


def fused(slabs, slab, cores, *args):
    (
        latent,
        main_hidden,
        main_query,
        text_key,
        text_value,
        text_len,
        guide_hidden,
        guide_query,
        guide_key,
        guide_value,
        guide_out,
        main_head,
        guide_head,
        main_modulation,
        guide_modulation,
        guidance_scale,
        sigma_table,
        step_index,
    ) = args
    main_head, guide_head = main_head.T, guide_head.T
    rows, width = main_query.shape
    text_rows = text_key.shape[0]
    guide_width = guide_query.shape[1]
    text_cols = width // slab
    guide_cols = guide_width // cores
    bf16, f32 = jnp.bfloat16, jnp.float32
    dma = pltpu.SemaphoreType.DMA
    like = lambda x: pltpu.VMEM(x.shape, x.dtype)
    scratch = [
        pltpu.VMEM((slabs, slab, text_rows, text_cols), bf16),
        pltpu.VMEM((slabs, slab, text_rows, text_cols), bf16),
        pltpu.VMEM((slab, rows, text_cols), bf16),
        pltpu.VMEM((slab, rows, text_cols), bf16),
        pltpu.VMEM((rows, width), bf16),
        pltpu.VMEM((slab, rows, text_cols // 2), bf16),
        pltpu.VMEM((slab, rows, text_cols // 2), bf16),
        pltpu.VMEM((3 * text_cols // 2 // HDIM, slab * rows, slabs * slab * text_rows), bf16),
        pltpu.VMEM((3 * text_cols // 2 // HDIM, slab * rows, 1), f32),
        pltpu.VMEM((slabs, cores, rows, guide_cols), bf16),
        pltpu.VMEM((slabs, cores, rows, guide_cols), bf16),
        pltpu.VMEM((slab, rows, guide_cols), bf16),
        pltpu.VMEM((slab, rows, guide_cols), bf16),
        pltpu.VMEM((slab, rows, 128), f32),
        pltpu.VMEM((slab, rows, guide_cols), bf16),
        pltpu.VMEM((slab, rows, 128), f32),
        like(main_hidden),
        like(guide_hidden),
        like(guide_out),
        like(main_head),
        like(guide_head),
        like(main_modulation),
        like(guide_modulation),
        pltpu.VMEM(main_hidden.shape, bf16),
        pltpu.VMEM(guide_hidden.shape, bf16),
        dma((6,)),
        dma((7,)),
        dma((slab, 2)),
        dma((slab, 2)),
        dma((slab, 3)),
        dma((slab, 3)),
        dma((cores, 2)),
        dma((cores, 2)),
        dma((2, slab, 4)),
        dma((2, slab, 4)),
        dma((2, slabs, 4)),
        dma((2, slabs, 4)),
        dma((2, slabs, 2)),
        dma((2, slabs, 2)),
        dma((slab, 2)),
        dma((slab, 2)),
        dma((slab, 2)),
        dma((slab, 2)),
        dma((slab,)),
        dma((slab,)),
        dma((slab,)),
        dma((slab,)),
    ]
    keys, guide_keys = slabs * slab * text_rows, slabs * cores * rows
    out = jax.ShapeDtypeStruct(latent.shape[::-1], f32)
    plain, guided, change = pl.pallas_call(
        functools.partial(kernel, slabs, slab, cores),
        out_shape=(out, out, jax.ShapeDtypeStruct((1, rows), f32)),
        in_specs=[pl.BlockSpec(memory_space=pltpu.SMEM)] * 4
        + [pl.BlockSpec(memory_space=pltpu.HBM)] * 13,
        out_specs=[pl.BlockSpec(memory_space=pltpu.VMEM)] * 3,
        scratch_shapes=scratch,
        compiler_params=pltpu.CompilerParams(
            collective_id=0, has_side_effects=True, vmem_limit_bytes=56 * 1024 * 1024
        ),
        cost_estimate=pl.CostEstimate(
            flops=4 * rows * (keys * width + guide_keys * guide_width * slab // cores),
            bytes_accessed=2 * (2 * text_rows + 2 * rows) * width,
            transcendentals=rows * keys * width // HDIM,
        ),
    )(
        text_len,
        guidance_scale,
        sigma_table,
        step_index,
        main_hidden,
        main_query,
        text_key,
        text_value,
        guide_hidden,
        guide_query,
        guide_key,
        guide_value,
        guide_out,
        main_head,
        guide_head,
        main_modulation,
        guide_modulation,
    )
    velocity = plain + guided
    return velocity.T, (latent.T + change * velocity).T


def choose(count, slab, cores, *args):
    rows, width = args[2].shape
    text_rows = args[3].shape[0]
    guide_width = args[7].shape[1]
    fits = (
        slab > 1
        and cores > 1
        and count % slab == 0
        and slab % cores == 0
        and count >= 4 * slab
        and rows % 16 == 0
        and text_rows % 16 == 0
        and width % (2 * slab * HDIM) == 0
        and guide_width % (cores * HDIM) == 0
    )
    if fits:
        return fused(count // slab, slab, cores, *args)
    return per_device(*args)


def solution(mesh):
    placed = (
        P(("parts", "seq"), None),
        P(("parts", "seq"), None),
        P(("parts", "seq"), None),
        P(("parts", "seq"), None),
        P(("parts", "seq"), None),
        P("parts"),
        P(("parts", "seq"), None),
        P(("parts", "seq"), None),
        P(("parts", "seq"), None),
        P(("parts", "seq"), None),
        P(),
        P(),
        P(),
        P("parts", None),
        P("parts", None),
        P("parts"),
        P(),
        P("parts"),
    )
    slab, cores = layout(mesh)
    return jax.shard_map(
        functools.partial(choose, mesh.shape["seq"], slab, cores),
        mesh=mesh,
        in_specs=placed,
        out_specs=(P(("parts", "seq"), None), P(("parts", "seq"), None)),
        check_vma=False,
    )
```

```python
import functools
import math

import jax
import jax.numpy as jnp
from jax import lax
from jax.experimental import pallas as pl
from jax.experimental.pallas import tpu as pltpu
from jax.sharding import PartitionSpec as P

HDIM = 128


def start_state(height, heads, head_size):
    return (
        jnp.full((heads, height), -1e30, jnp.float32),
        jnp.zeros((heads, height), jnp.float32),
        jnp.zeros((heads, height, head_size), jnp.float32),
    )


def fold_step(running, queries, keys, values, heads, valid):
    height = queries.shape[0]
    head_size = queries.shape[1] // heads
    query_heads = queries.reshape(height, heads, head_size)
    key_heads = keys.reshape(keys.shape[0], heads, head_size)
    value_heads = values.reshape(values.shape[0], heads, head_size)
    scores = jnp.einsum(
        "qhd,khd->hqk", query_heads, key_heads, preferred_element_type=jnp.float32
    ) * head_size ** (-0.5)
    if valid is not None:
        scores = jnp.where(valid[None, None, :], scores, -1e30)
    peak_old, totals, accumulated = running
    peak_new = jnp.maximum(peak_old, jnp.max(scores, axis=-1))
    weights = jnp.exp(scores - peak_new[..., None])
    if valid is not None:
        weights = jnp.where(valid[None, None, :], weights, 0.0)
    totals = jnp.sum(weights, axis=-1)
    accumulated = jnp.einsum(
        "hqk,khd->hqd",
        weights.astype(jnp.bfloat16),
        value_heads,
        preferred_element_type=jnp.float32,
    )
    return (peak_new, totals, accumulated)


def finish(running):
    peak, totals, accumulated = running
    result = accumulated / totals[..., None]
    return result.transpose(1, 0, 2).reshape(result.shape[1], -1).astype(jnp.bfloat16)


def head_out(summed, modulation, head_weight):
    centered = summed - jnp.mean(summed, axis=-1, keepdims=True)
    spread = jnp.mean(centered * centered, axis=-1, keepdims=True)
    normed = centered * lax.rsqrt(spread + 1e-06)
    shaped = (normed * (1.0 + modulation[1]) + modulation[0]).astype(jnp.bfloat16)
    return jnp.dot(shaped, head_weight, preferred_element_type=jnp.float32)


def per_device(
    latent,
    main_hidden,
    main_query,
    text_key,
    text_value,
    text_len,
    guide_hidden,
    guide_query,
    guide_key,
    guide_value,
    guide_out,
    main_head,
    guide_head,
    main_modulation,
    guide_modulation,
    guidance_scale,
    sigma_table,
    step_index,
):
    height = main_query.shape[0]
    main_heads = main_head.shape[0] // HDIM
    guide_heads = guide_out.shape[0] // HDIM
    all_text_keys = lax.all_gather(text_key, "seq", axis=0, tiled=True)
    all_text_values = lax.all_gather(text_value, "seq", axis=0, tiled=True)
    positions = jnp.arange(all_text_keys.shape[0], dtype=jnp.int32)
    folded = fold_step(
        start_state(height, main_heads, HDIM),
        main_query,
        all_text_keys,
        all_text_values,
        main_heads,
        positions < text_len[0],
    )
    main_sum = main_hidden.astype(jnp.float32) + finish(folded).astype(jnp.float32)
    main_velocity = head_out(main_sum, main_modulation, main_head)
    all_keys = lax.all_gather(guide_key, "seq", axis=0, tiled=True)
    all_values = lax.all_gather(guide_value, "seq", axis=0, tiled=True)
    folded = fold_step(
        start_state(height, guide_heads, HDIM), guide_query, all_keys, all_values, guide_heads, None
    )
    projected = jnp.dot(finish(folded), guide_out, preferred_element_type=jnp.float32)
    guide_sum = guide_hidden.astype(jnp.float32) + projected
    guide_velocity = head_out(guide_sum, guide_modulation, guide_head)
    velocity = guide_velocity + guidance_scale[0] * (main_velocity - guide_velocity)
    positions = jnp.arange(sigma_table.shape[0], dtype=jnp.int32)
    sigma_now = jnp.sum(jnp.where(positions == step_index[0], sigma_table, 0.0))
    sigma_next = jnp.sum(jnp.where(positions == step_index[0] + 1, sigma_table, 0.0))
    next_latent = latent + (sigma_next - sigma_now) * velocity
    return (velocity, next_latent)


def layout(mesh):
    axis = mesh.axis_names.index("seq")
    devices = mesh.devices
    for other in range(devices.ndim - 1, -1, -1):
        if other != axis:
            devices = devices.take(0, axis=other)
    places = [getattr(device, "coords", None) for device in devices]
    if places[0] is None:
        return 1, 1
    slab = sum(place[2] == places[0][2] for place in places)
    cores = sum(tuple(place) == tuple(places[0]) for place in places)
    return slab, cores


def shaped_rows(summed, modulation):
    centered = summed - jnp.mean(summed, axis=-1, keepdims=True)
    spread = jnp.mean(centered * centered, axis=-1, keepdims=True)
    normed = centered * lax.rsqrt(spread + 1e-06)
    return (normed * (1.0 + modulation[1:2]) + modulation[0:1]).astype(jnp.bfloat16)


def across(a, b):
    return lax.dot_general(a, b, (((1,), (1,)), ((), ())), preferred_element_type=jnp.float32)


def kernel(
    slabs,
    slab,
    cores,
    text_len,
    guidance_scale,
    sigma_table,
    step_index,
    main_hidden,
    main_query,
    text_key,
    text_value,
    guide_hidden,
    guide_query,
    guide_key,
    guide_value,
    guide_out,
    main_head,
    guide_head,
    main_modulation,
    guide_modulation,
    plain,
    guided,
    change,
    tk,
    tv,
    tq,
    to,
    att,
    hq,
    ho,
    tp,
    tl,
    gk,
    gv,
    gq,
    gacc,
    gml,
    racc,
    rml,
    v_hidden,
    v_ghidden,
    v_gout,
    v_mhead,
    v_ghead,
    v_mmod,
    v_gmod,
    v_shaped,
    v_gshaped,
    local_sem,
    load_sem,
    t_send,
    t_recv,
    q_send,
    q_recv,
    g_send,
    g_recv,
    own_send,
    near_recv,
    fwd_send,
    far_recv,
    gc_send,
    gc_recv,
    o_send,
    o_recv,
    p_send,
    p_recv,
    hq_send,
    hq_recv,
    ho_send,
    ho_recv,
):
    me = lax.axis_index("seq")
    z = me // slab
    s = me % slab
    c = s % cores
    rows = main_query.shape[0]
    text_cols = tk.shape[-1]
    guide_cols = gk.shape[-1]
    heads = text_cols // HDIM
    guide_heads = guide_cols // HDIM
    keys = slabs * slab * tk.shape[2]
    guide_keys = slabs * cores * rows
    width = text_cols // 2
    end = jnp.logical_or(z == 0, z == slabs - 1)
    host = jnp.logical_or(z == 1, z == slabs - 2)
    inner = jnp.where(z == 0, 1, slabs - 2) * slab
    outer = jnp.where(z == 1, 0, slabs - 1) * slab
    scale = HDIM ** (-0.5) * math.log2(math.e)

    def cols(ref, index, width):
        return ref.at[:, pl.ds(pl.multiple_of(index * width, 128), width)]

    def remote(src, dst, send, recv, target):
        return pltpu.make_async_remote_copy(
            src_ref=src,
            dst_ref=dst,
            send_sem=send,
            recv_sem=recv,
            device_id={"seq": target},
            device_id_type=pl.DeviceIdType.MESH,
        )

    def peer(j):
        return (s - c + (j // cores) * cores) % slab + (c + j) % cores

    def back(j):
        return (slab // cores - j // cores) % (slab // cores) * cores + (cores - j) % cores

    mine = [
        (cols(text_key, s, text_cols), tk.at[z, s]),
        (cols(text_value, s, text_cols), tv.at[z, s]),
        (cols(main_query, s, text_cols), tq.at[s]),
        (cols(guide_query, c, guide_cols), gq.at[s]),
        (cols(guide_key, c, guide_cols), gk.at[z, c]),
        (cols(guide_value, c, guide_cols), gv.at[z, c]),
    ]
    mine = [pltpu.make_async_copy(a, b, local_sem.at[i]) for i, (a, b) in enumerate(mine)]
    loads = [
        (main_hidden, v_hidden),
        (main_head, v_mhead),
        (main_modulation, v_mmod),
        (guide_out, v_gout),
        (guide_hidden, v_ghidden),
        (guide_head, v_ghead),
        (guide_modulation, v_gmod),
    ]
    loads = [pltpu.make_async_copy(a, b, load_sem.at[i]) for i, (a, b) in enumerate(loads)]
    for copy in mine:
        copy.start()

    barrier = pltpu.get_barrier_semaphore()

    def greet(target):
        pl.semaphore_signal(
            barrier, inc=1, device_id={"seq": target}, device_id_type=pl.DeviceIdType.MESH
        )

    for j in range(1, slab):
        greet(z * slab + peer(j))

    @pl.when(end)
    def _():
        for t in range(slab):
            greet(inner + t)

    @pl.when(host)
    def _():
        for t in range(slab):
            greet(outer + t)

    @pl.when(z > 1)
    def _():
        @pl.when(z < slabs - 1)
        def _():
            greet(me - slab)

    @pl.when(z < slabs - 2)
    def _():
        @pl.when(z > 0)
        def _():
            greet(me + slab)

    greeted = jnp.where(end, slab, 0) + jnp.where(host, slab, 0)
    greeted += jnp.where(jnp.logical_and(z > 1, z < slabs - 1), 1, 0)
    greeted += jnp.where(jnp.logical_and(z < slabs - 2, z > 0), 1, 0)
    pl.semaphore_wait(barrier, slab - 1 + greeted)

    target = (me - slab, me + slab)
    has_target = (z > 0, z < slabs - 1)
    target_end = (z == 1, z == slabs - 2)
    target_takes = tuple(
        jnp.logical_and(has, jnp.logical_not(is_end)) for has, is_end in zip(has_target, target_end)
    )
    sent = []

    def send_if(goes, make):
        @pl.when(goes)
        def _():
            for copy in make():
                copy.start()

        sent.append((goes, make))

    def both_ways(make, group=1):
        for way in range(2):
            goes = has_target[way] if group == 1 else target_takes[way]
            send_if(goes, functools.partial(make, way))

    both = ((text_key, tk), (text_value, tv))
    guide_both = ((guide_key, gk), (guide_value, gv))

    def slab_text(j, kv):
        source, place = both[kv]
        t = peer(j)
        return remote(
            cols(source, t, text_cols),
            place.at[z, s],
            t_send.at[j, kv],
            t_recv.at[back(j), kv],
            z * slab + t,
        )

    def half(place, group):
        return place.at[:, pl.ds(group * width, width)]

    def halves(place, group):
        return place.at[:, :, pl.ds(group * width, width)]

    def chain_own(j, kv, group, way):
        source, place = both[kv]
        t = peer(j)
        if j == 0:
            src = cols(source, s * 2 + group, width)
        else:
            src = half(place.at[z, t], group)
        unit = kv * 2 + group
        return remote(
            src,
            half(place.at[z, t], group),
            own_send.at[way, j, unit],
            near_recv.at[way, j, unit],
            target[way],
        )

    def slab_guide(j, kv):
        source, place = guide_both[kv]
        t = peer(j)
        return remote(
            cols(source, t % cores, guide_cols),
            place.at[z, c],
            g_send.at[j, kv],
            g_recv.at[back(j), kv],
            z * slab + t,
        )

    def slab_query(j, group):
        t = peer(j)
        return remote(
            cols(main_query, t * 2 + group, width),
            half(tq.at[s], group),
            q_send.at[j, group],
            q_recv.at[back(j), group],
            z * slab + t,
        )

    def slab_guide_query(j):
        t = peer(j)
        return remote(
            cols(guide_query, t % cores, guide_cols),
            gq.at[s],
            q_send.at[j, 2],
            q_recv.at[back(j), 2],
            z * slab + t,
        )

    def lend(t):
        return remote(
            cols(main_query, t * 2, width), hq.at[s], hq_send.at[t], hq_recv.at[s], inner + t
        )

    def repay(t):
        at = pl.ds(pl.multiple_of(s * text_cols, 128), width)
        return remote(ho.at[t], att.at[:, at], ho_send.at[t], ho_recv.at[s], outer + t)

    others = [j for j in range(slab - 1, 0, -1)]

    def arrived(place, sem):
        pltpu.make_async_copy(place, place, sem).wait()

    def begin_chain(kv, j):
        for group in range(2):
            both_ways(lambda way, group=group: [chain_own(j, kv, group, way)], group)

    for j in others:
        slab_text(j, 0).start()
    begin_chain(0, 0)
    for kv in range(2):
        for j in range(1, cores):
            slab_guide(j, kv).start()
    for j in range(1, slab):
        arrived(tk.at[z, peer(j)], t_recv.at[j, 0])
        begin_chain(0, j)
    send_if(end, lambda: [lend(t) for t in range(slab)])
    for j in others:
        slab_query(j, 1).start()
    send_if(jnp.logical_not(end), lambda: [slab_query(j, 0) for j in others])
    for j in others:
        slab_guide_query(j).start()
    for j in others:
        slab_text(j, 1).start()
    for copy in loads:
        copy.start()
    for copy in mine:
        copy.wait()
    for kv in range(2):
        place = guide_both[kv][1]
        for j in range(1, cores):
            arrived(place.at[z, peer(j) % cores], g_recv.at[j, kv])

    def guide_chain(d, kv, way):
        place = guide_both[kv][1]
        from_z = z + d if way == 0 else z - d
        return remote(
            place.at[from_z],
            place.at[from_z],
            gc_send.at[way, d, kv],
            gc_recv.at[way, d, kv],
            target[way],
        )

    def begin_guide(d):
        for way in range(2):
            turn = z + d == slabs - 1 if way == 0 else z == d
            send_if(
                jnp.logical_and(turn, has_target[way]),
                lambda way=way: [guide_chain(0, 0, way), guide_chain(0, 1, way)],
            )

    def text_chain(d, kv, group, way):
        from_z = z + d if way == 0 else z - d
        block = halves(both[kv][1].at[from_z], group)
        unit = kv * 2 + group
        return remote(
            block, block, fwd_send.at[way, d, unit], far_recv.at[way, d, unit], target[way]
        )

    def coming(d, way):
        return z + d < slabs if way == 0 else z - d >= 0

    def pass_text(d, kv):
        place = both[kv][1]
        for way in range(2):
            from_z = z + d if way == 0 else z - d
            for group in range(2):
                comes = coming(d, way)
                if group == 0:
                    comes = jnp.logical_and(comes, jnp.logical_not(end))
                unit = kv * 2 + group

                @pl.when(comes)
                def _(way=way, group=group, unit=unit, from_z=from_z):
                    if d == 1:
                        for j in range(slab):
                            arrived(
                                half(place.at[from_z, peer(j)], group), near_recv.at[way, j, unit]
                            )
                    else:
                        arrived(halves(place.at[from_z], group), far_recv.at[way, d - 1, unit])

                if d < slabs - 1:
                    takes = has_target[way] if group == 1 else target_takes[way]
                    send_if(
                        jnp.logical_and(comes, takes),
                        lambda way=way, group=group: [text_chain(d, kv, group, way)],
                    )

    begin_guide(0)
    for d in range(1, slabs):
        pass_text(d, 0)
        if d < slabs - 1:
            begin_guide(d)

    def guide_arrived(d, way):
        from_z = z + d if way == 0 else z - d
        for kv in range(2):
            arrived(guide_both[kv][1].at[from_z], gc_recv.at[way, d - 1, kv])

    def pass_guide(d):
        for way in range(2):
            goes = jnp.logical_and(coming(d, way), has_target[way])

            @pl.when(goes)
            def _(way=way):
                guide_arrived(d, way)

            if d < slabs - 1:
                send_if(goes, lambda way=way: [guide_chain(d, kv, way) for kv in range(2)])

    positions = lax.broadcasted_iota(jnp.int32, (1, keys), 1)
    bias = jnp.where(positions < text_len[0], 0.0, -1e30).astype(jnp.float32)

    def weigh(q, k, bias=None):
        scores = across(q, k)
        if bias is not None:
            scores = scores + bias
        peak = jnp.max(scores, axis=-1, keepdims=True)
        weights = jnp.exp2((scores - peak) * scale)
        return peak, weights, jnp.sum(weights, axis=-1, keepdims=True)

    def give(j, group):
        t = peer(j)
        at = pl.ds(pl.multiple_of(s * text_cols + group * width, 128), width)
        return remote(
            half(to.at[t], group),
            att.at[:, at],
            o_send.at[j, group],
            o_recv.at[back(j), group],
            z * slab + t,
        )

    def text_weights(group, queries, first, slot):
        def one_head(h, _):
            at = pl.ds(pl.multiple_of(group * width + h * HDIM, 128), HDIM)
            q_at = pl.ds(pl.multiple_of(first + h * HDIM, 128), HDIM)
            k = tk[:, :, :, at].reshape(keys, HDIM)
            q = queries[:, :, q_at].reshape(slab * rows, HDIM)
            _, weights, total = weigh(q, k, bias)
            tp[slot + h] = weights.astype(jnp.bfloat16)
            tl[slot + h] = total
            return 0

        lax.fori_loop(0, heads // 2, one_head, 0)

    def text_values(group, results, first, slot):
        def one_head(h, _):
            at = pl.ds(pl.multiple_of(group * width + h * HDIM, 128), HDIM)
            to_at = pl.ds(pl.multiple_of(first + h * HDIM, 128), HDIM)
            v = tv[:, :, :, at].reshape(keys, HDIM)
            out = jnp.dot(tp[slot + h], v, preferred_element_type=jnp.float32)
            out = (out / tl[slot + h]).astype(jnp.bfloat16)
            results[:, :, to_at] = out.reshape(slab, rows, HDIM)
            return 0

        lax.fori_loop(0, heads // 2, one_head, 0)

    @pl.when(host)
    def _():
        for t in range(slab):
            arrived(hq.at[t], hq_recv.at[t])
        text_weights(0, hq, 0, heads)

    for d in range(1, slabs - 2):
        pass_guide(d)

    @pl.when(jnp.logical_not(end))
    def _():
        for j in range(1, slab):
            arrived(half(tq.at[peer(j)], 0), q_recv.at[j, 0])
        text_weights(0, tq, 0, 0)

    begin_chain(1, 0)
    for j in range(1, slab):
        arrived(tv.at[z, peer(j)], t_recv.at[j, 1])
        begin_chain(1, j)
    for d in range(slabs - 2, slabs - 1):
        pass_guide(d)
    for j in range(1, slab):
        arrived(half(tq.at[peer(j)], 1), q_recv.at[j, 1])
        arrived(gq.at[peer(j)], q_recv.at[j, 2])
    text_weights(1, tq, width, heads // 2)

    for d in range(1, slabs):
        for way in range(2):
            comes = z + d < slabs if way == 0 else z - d >= 0
            last = jnp.logical_and(comes, jnp.logical_not(has_target[way]))

            @pl.when(last)
            def _(way=way, d=d):
                guide_arrived(d, way)

    for h in range(guide_heads):
        at = pl.ds(h * HDIM, HDIM)

        k = gk[:, :, :, at].reshape(guide_keys, HDIM)
        v = gv[:, :, :, at].reshape(guide_keys, HDIM)
        peak, weights, total = weigh(gq[:, :, at].reshape(slab * rows, HDIM), k)
        out = jnp.dot(weights.astype(jnp.bfloat16), v, preferred_element_type=jnp.float32)
        gacc[:, :, at] = (out / total).astype(jnp.bfloat16).reshape(slab, rows, HDIM)
        gml[:, :, h : h + 1] = peak.reshape(slab, rows, 1)
        gml[:, :, guide_heads + h : guide_heads + h + 1] = total.reshape(slab, rows, 1)

    def part(j):
        t = peer(j)
        return (
            remote(gacc.at[t], racc.at[s], p_send.at[j, 0], p_recv.at[back(j), 0], z * slab + t),
            remote(gml.at[t], rml.at[s], p_send.at[j, 1], p_recv.at[back(j), 1], z * slab + t),
        )

    for j in range(slab - 1, 0, -1):
        for copy in part(j):
            copy.start()
    own_part = [
        pltpu.make_async_copy(gacc.at[s], racc.at[s], local_sem.at[1]),
        pltpu.make_async_copy(gml.at[s], rml.at[s], local_sem.at[2]),
    ]
    for copy in own_part:
        copy.start()

    for d in range(1, slabs):
        pass_text(d, 1)

    @pl.when(host)
    def _():
        text_values(0, ho, 0, heads)

    send_if(host, lambda: [repay(t) for t in range(slab)])

    @pl.when(jnp.logical_not(end))
    def _():
        text_values(0, to, 0, 0)

    send_if(jnp.logical_not(end), lambda: [give(j, 0) for j in others])
    text_values(1, to, width, heads // 2)
    for j in others:
        give(j, 1).start()
    own_att = [
        pltpu.make_async_copy(half(to.at[s], group), cols(att, s * 2 + group, width), local_sem.at[3 * group])
        for group in range(2)
    ]
    own_att[1].start()

    @pl.when(jnp.logical_not(end))
    def _():
        own_att[0].start()

    for copy in loads:
        copy.wait()
    for copy in own_part:
        copy.wait()
    for j in range(1, slab):
        arrived(racc.at[peer(j)], p_recv.at[j, 0])
        arrived(rml.at[peer(j)], p_recv.at[j, 1])

    pieces = []
    for core in range(cores):
        members = range(core, slab, cores)
        for h in range(guide_heads):
            peaks = [rml[t, :, h : h + 1] for t in members]
            totals = [rml[t, :, guide_heads + h : guide_heads + h + 1] for t in members]
            peak = functools.reduce(jnp.maximum, peaks)
            factors = [l * jnp.exp2((p - peak) * scale) for p, l in zip(peaks, totals)]
            total = sum(factors)
            summed = sum(
                f * racc[t, :, h * HDIM : (h + 1) * HDIM].astype(jnp.float32) for f, t in zip(factors, members)
            )
            pieces.append((summed / total).astype(jnp.bfloat16))
    guide_attended = jnp.concatenate(pieces, axis=-1)
    guide_sum = v_ghidden[...].astype(jnp.float32) + jnp.dot(
        guide_attended, v_gout[...], preferred_element_type=jnp.float32
    )
    v_gshaped[...] = shaped_rows(guide_sum, v_gmod[...])
    guide_velocity = across(v_ghead[...], v_gshaped[...])
    own_att[1].wait()
    for j in range(1, slab):
        arrived(cols(att, peer(j) * 2 + 1, width), o_recv.at[j, 1])

    @pl.when(jnp.logical_not(end))
    def _():
        own_att[0].wait()
        for j in range(1, slab):
            arrived(cols(att, peer(j) * 2, width), o_recv.at[j, 0])

    @pl.when(end)
    def _():
        for t in range(slab):
            arrived(cols(att, t * 2, width), ho_recv.at[t])

    step = 16

    def main_rows(i, _):
        at = pl.ds(pl.multiple_of(i * step, step), step)
        summed = v_hidden[at, :].astype(jnp.float32) + att[at, :].astype(jnp.float32)
        v_shaped[at, :] = shaped_rows(summed, v_mmod[...])
        return 0

    lax.fori_loop(0, rows // step, main_rows, 0)
    main_velocity = across(v_mhead[...], v_shaped[...])

    now = step_index[0]
    plain[...] = guide_velocity
    guided[...] = guidance_scale[0] * (main_velocity - guide_velocity)
    change[...] = jnp.full(change.shape, sigma_table[now + 1] - sigma_table[now], jnp.float32)

    for j in range(1, slab):
        for kv in range(2):
            slab_text(j, kv).wait_send()
            if j < cores:
                slab_guide(j, kv).wait_send()
        slab_query(j, 1).wait_send()
        slab_guide_query(j).wait_send()
        give(j, 1).wait_send()
        for copy in part(j):
            copy.wait_send()
    for goes, make in sent:

        @pl.when(goes)
        def _(make=make):
            for copy in make():
                copy.wait_send()


def fused(slabs, slab, cores, *args):
    (
        latent,
        main_hidden,
        main_query,
        text_key,
        text_value,
        text_len,
        guide_hidden,
        guide_query,
        guide_key,
        guide_value,
        guide_out,
        main_head,
        guide_head,
        main_modulation,
        guide_modulation,
        guidance_scale,
        sigma_table,
        step_index,
    ) = args
    main_head, guide_head = main_head.T, guide_head.T
    rows, width = main_query.shape
    text_rows = text_key.shape[0]
    guide_width = guide_query.shape[1]
    text_cols = width // slab
    guide_cols = guide_width // cores
    bf16, f32 = jnp.bfloat16, jnp.float32
    dma = pltpu.SemaphoreType.DMA
    like = lambda x: pltpu.VMEM(x.shape, x.dtype)
    scratch = [
        pltpu.VMEM((slabs, slab, text_rows, text_cols), bf16),
        pltpu.VMEM((slabs, slab, text_rows, text_cols), bf16),
        pltpu.VMEM((slab, rows, text_cols), bf16),
        pltpu.VMEM((slab, rows, text_cols), bf16),
        pltpu.VMEM((rows, width), bf16),
        pltpu.VMEM((slab, rows, text_cols // 2), bf16),
        pltpu.VMEM((slab, rows, text_cols // 2), bf16),
        pltpu.VMEM((3 * text_cols // 2 // HDIM, slab * rows, slabs * slab * text_rows), bf16),
        pltpu.VMEM((3 * text_cols // 2 // HDIM, slab * rows, 1), f32),
        pltpu.VMEM((slabs, cores, rows, guide_cols), bf16),
        pltpu.VMEM((slabs, cores, rows, guide_cols), bf16),
        pltpu.VMEM((slab, rows, guide_cols), bf16),
        pltpu.VMEM((slab, rows, guide_cols), bf16),
        pltpu.VMEM((slab, rows, 128), f32),
        pltpu.VMEM((slab, rows, guide_cols), bf16),
        pltpu.VMEM((slab, rows, 128), f32),
        like(main_hidden),
        like(guide_hidden),
        like(guide_out),
        like(main_head),
        like(guide_head),
        like(main_modulation),
        like(guide_modulation),
        pltpu.VMEM(main_hidden.shape, bf16),
        pltpu.VMEM(guide_hidden.shape, bf16),
        dma((6,)),
        dma((7,)),
        dma((slab, 2)),
        dma((slab, 2)),
        dma((slab, 3)),
        dma((slab, 3)),
        dma((cores, 2)),
        dma((cores, 2)),
        dma((2, slab, 4)),
        dma((2, slab, 4)),
        dma((2, slabs, 4)),
        dma((2, slabs, 4)),
        dma((2, slabs, 2)),
        dma((2, slabs, 2)),
        dma((slab, 2)),
        dma((slab, 2)),
        dma((slab, 2)),
        dma((slab, 2)),
        dma((slab,)),
        dma((slab,)),
        dma((slab,)),
        dma((slab,)),
    ]
    keys, guide_keys = slabs * slab * text_rows, slabs * cores * rows
    out = jax.ShapeDtypeStruct(latent.shape[::-1], f32)
    plain, guided, change = pl.pallas_call(
        functools.partial(kernel, slabs, slab, cores),
        out_shape=(out, out, jax.ShapeDtypeStruct((1, rows), f32)),
        in_specs=[pl.BlockSpec(memory_space=pltpu.SMEM)] * 4
        + [pl.BlockSpec(memory_space=pltpu.HBM)] * 13,
        out_specs=[pl.BlockSpec(memory_space=pltpu.VMEM)] * 3,
        scratch_shapes=scratch,
        compiler_params=pltpu.CompilerParams(
            collective_id=0, has_side_effects=True, vmem_limit_bytes=56 * 1024 * 1024
        ),
        cost_estimate=pl.CostEstimate(
            flops=4 * rows * (keys * width + guide_keys * guide_width * slab // cores),
            bytes_accessed=2 * (2 * text_rows + 2 * rows) * width,
            transcendentals=rows * keys * width // HDIM,
        ),
    )(
        text_len,
        guidance_scale,
        sigma_table,
        step_index,
        main_hidden,
        main_query,
        text_key,
        text_value,
        guide_hidden,
        guide_query,
        guide_key,
        guide_value,
        guide_out,
        main_head,
        guide_head,
        main_modulation,
        guide_modulation,
    )
    velocity = plain + guided
    return velocity.T, (latent.T + change * velocity).T


def choose(count, slab, cores, *args):
    rows, width = args[2].shape
    text_rows = args[3].shape[0]
    guide_width = args[7].shape[1]
    fits = (
        slab > 1
        and cores > 1
        and count % slab == 0
        and slab % cores == 0
        and count >= 4 * slab
        and rows % 16 == 0
        and text_rows % 16 == 0
        and width % (2 * slab * HDIM) == 0
        and guide_width % (cores * HDIM) == 0
    )
    if fits:
        return fused(count // slab, slab, cores, *args)
    return per_device(*args)


def solution(mesh):
    placed = (
        P(("parts", "seq"), None),
        P(("parts", "seq"), None),
        P(("parts", "seq"), None),
        P(("parts", "seq"), None),
        P(("parts", "seq"), None),
        P("parts"),
        P(("parts", "seq"), None),
        P(("parts", "seq"), None),
        P(("parts", "seq"), None),
        P(("parts", "seq"), None),
        P(),
        P(),
        P(),
        P("parts", None),
        P("parts", None),
        P("parts"),
        P(),
        P("parts"),
    )
    slab, cores = layout(mesh)
    return jax.shard_map(
        functools.partial(choose, mesh.shape["seq"], slab, cores),
        mesh=mesh,
        in_specs=placed,
        out_specs=(P(("parts", "seq"), None), P(("parts", "seq"), None)),
        check_vma=False,
    )
```
